128 devices in a mesh: seq: 64 (over y, x, z), head: 2 (over core).
Axes of the slice: x: 4, y: 4, z: 4, core: 2. Of those that a mesh axis runs over, the one named last changes fastest.
Arguments:
- queries: bfloat16 [32768, 2048], P('seq', 'head'), may hold values from -8 to 8
- keys: bfloat16 [32768, 2048], P('seq', 'head'), may hold values from -8 to 8
- values: bfloat16 [32768, 2048], P('seq', 'head'), may hold values from -6 to 6
- out_grad: bfloat16 [32768, 2048], P('seq', 'head'), may hold values from -6 to 6
- cluster_ids: int32 [16, 32768, 1], P('head', 'seq'), may hold values from 0 to 255; in each aligned block of 512 rows (0 to 511, 512 to 1023, ..., all dimensions but the last counted through in order) at most 4 rows name the same one
- cluster_slot: int32 [256], replicated, may hold values from 0 to 255, each once
- centroids: float32 [16, 256, 128], P('head', 'seq'), may hold values from -6 to 6
Outputs:
- layer_out: bfloat16 [32768, 2048], P('seq', 'head')
- grad_queries: bfloat16 [32768, 2048], P('seq', 'head')
- grad_keys: bfloat16 [32768, 2048], P('seq', 'head')
- grad_values: bfloat16 [32768, 2048], P('seq', 'head')
- new_centroids: float32 [16, 256, 128], P('head', 'seq')
The draws below stay inside these ranges and needn't reach their ends.
Inputs may be any that keep to these rules, and one draw needn't show every extreme that they name: `cluster_ids`: for each head, among the tokens of one device no cluster is named more than 4 times, a bound that some block reaches. `cluster_slot`: each slot is taken by one cluster.
All inputs are finite; a program needn't handle non-finite values.
Results may differ from the reference program's by a relative error of at most 0.024.
The reference program's roundings to bfloat16 on the way (of `probs_low` and `grad_score`) count: a program that leaves them out, or rounds other values in their place, can miss the bound.
Values may be sent and summed in bfloat16 or wider, within the bound.
No kernel may reach another device: no remote copies, remote signals or barrier semaphores. Data moves between devices by JAX's collectives and lax.ppermute only.
A program may use at most 128 MiB of HBM per device.

```python
import math
import jax
import jax.numpy as jnp
import numpy as np
from jax import lax

H = 16
DH = 128
CLUSTERS = 256
TOK_DEV = 512
CAP = 4
TOKENS = 32768
SLOTS = 256


def draw_queries(key, part):
    own_key = jax.random.fold_in(key, 11)
    rows_drawn = jax.random.truncated_normal(own_key, -6.0, 6.0, (TOKENS, H * DH), jnp.float32)
    return rows_drawn.astype(jnp.bfloat16)


def draw_keys(key, part):
    own_key = jax.random.fold_in(key, 23)
    rows_drawn = jax.random.truncated_normal(own_key, -6.0, 6.0, (TOKENS, H * DH), jnp.float32)
    return rows_drawn.astype(jnp.bfloat16)


def shard_levels(key, dims, cuts, smallest, top_value):
    gain = 1.0
    for axis_at, parts in cuts:
        steps = jax.random.uniform(jax.random.fold_in(jax.random.fold_in(key, 6), axis_at), (parts,), jnp.float32, smallest / len(cuts), top_value / len(cuts))
        gain = gain * jnp.repeat(jnp.exp(steps), dims[axis_at] // parts).reshape((-1,) + (1,) * (len(dims) - 1 - axis_at))
    return gain


def assign_block(key, own, number, rows, number_of, top, most, slope):
    order = jax.random.permutation(key, number_of)
    packed, common = shares(number_of, rows * top, most, slope, True), shares(number_of, rows * top, most, slope, False)
    places = jnp.arange(number_of)

    def named(sizes, offset_by):
        used = int((sizes > 0).sum())
        fixed = max(1, used // 4)
        shifted = fixed + (places - fixed + offset_by * (used - fixed)) % max(1, number_of - fixed)
        return jnp.zeros((number_of,), jnp.int32).at[order[jnp.where(places < fixed, places, shifted)]].set(jnp.asarray(sizes, jnp.int32))

    sizes = jnp.where(number % 4 == 0, named(packed, number // 4), named(common, number - number // 4 - 1))
    mixed = jax.random.permutation(jax.random.fold_in(own, 3), number_of)
    donor, receiver = mixed[0:number_of // 2 * 2:2], mixed[1:number_of // 2 * 2:2]
    slack = jnp.minimum(sizes[donor] - 1, most - sizes[receiver]) // 2
    slack = jnp.where((donor == order[0]) | (receiver == order[0]) | (sizes[receiver] == 0), 0, jnp.maximum(slack, 0))
    shifted = jax.random.randint(jax.random.fold_in(own, 4), (number_of // 2,), 0, 1 << 20) % (slack + 1)
    sizes = sizes.at[donor].add(-shifted).at[receiver].add(shifted)
    items = jnp.searchsorted(jnp.cumsum(sizes), jnp.arange(rows * top), side="right").astype(jnp.int32)
    listing = items.reshape(top, rows).T
    listing = listing[jax.random.permutation(jax.random.fold_in(own, 1), rows)]
    offset_by = jax.random.randint(jax.random.fold_in(own, 2), (rows, 1), 0, top)
    return jnp.take_along_axis(listing, (jnp.arange(top)[None, :] + offset_by) % top, axis=1)


def shares(number_of, total, reach, skew, full):
    loads = [(1 << 20) // math.isqrt(grade ** skew) + 1 for grade in range(1, number_of + 1)]
    largest = reach if full else min(reach, max(-(-total // number_of), total * loads[0] // sum(loads)))
    least = 1 if total - largest >= number_of - 1 else 0
    given, surplus = [largest] + [least] * (number_of - 1), total - largest - least * (number_of - 1)
    while surplus > 0:
        free = [i for i in range(1, number_of) if given[i] < largest] or [i for i in range(1, number_of) if given[i] < reach]
        whole, remaining = sum([loads[i] for i in free]), surplus
        for i in free:
            extra = min(reach - given[i], max(1, remaining * loads[i] // whole), surplus)
            given[i] = given[i] + extra
            surplus = surplus - extra
    return np.array(given)


def scatter_about(rng, dims, width, limit, cuts=(), kind=jnp.bfloat16):
    values = jax.random.normal(rng, dims, jnp.float32) * width
    if len(cuts) > 0:
        values = shard_levels(rng, dims, cuts, -0.22, 0.18) * values
    return jnp.clip(values, min=-limit, max=limit).astype(kind)


def setup_inputs(seed: int = 0) -> dict:
    arg_keys = jax.random.split(jax.random.key(seed), 8)
    queries = draw_queries(jax.random.fold_in(arg_keys[7], 71), 0)
    keys = draw_keys(jax.random.fold_in(arg_keys[7], 71), 0)
    values = scatter_about(arg_keys[2], (TOKENS, H * DH), 1.0, 6.0, ((0, 64), (1, 2)))
    out_grad = scatter_about(arg_keys[3], (TOKENS, H * DH), 1.0, 6.0, ((0, 64), (1, 2)))
    cluster_ids_keys = jax.random.split(jax.random.fold_in(arg_keys[4], 1), H * TOKENS // TOK_DEV)
    cluster_ids_turns = jax.random.permutation(jax.random.fold_in(arg_keys[4], 3), H * TOKENS // TOK_DEV)
    cluster_ids = jax.vmap(lambda own, number: assign_block(jax.random.fold_in(arg_keys[4], 2), own, number, TOK_DEV, CLUSTERS, 1, CAP, 2))(cluster_ids_keys, cluster_ids_turns).reshape((H, TOKENS, 1))
    cluster_slot = jax.random.permutation(arg_keys[5], CLUSTERS).astype(jnp.int32)
    centroids = scatter_about(arg_keys[6], (H, CLUSTERS, DH), 1.0, 6.0, ((0, 2), (1, 64)), jnp.float32)
    return {"queries": queries, "keys": keys, "values": values, "out_grad": out_grad, "cluster_ids": cluster_ids, "cluster_slot": cluster_slot, "centroids": centroids}


DECAY_RATE = 0.9
MASKED = -1e+30

def rounded(array_in):
    return lax.optimization_barrier(array_in.astype(jnp.bfloat16)).astype(jnp.float32)

def attention_probs(query_rows, key_rows, valid_keys, score_scale):
    scores = jnp.einsum('hid,hjd->hij', query_rows, key_rows, precision=lax.Precision.HIGHEST) * score_scale
    slot_count = scores.shape[-1]
    row_at = lax.broadcasted_iota(jnp.int32, (slot_count, slot_count), 0)
    col_at = lax.broadcasted_iota(jnp.int32, (slot_count, slot_count), 1)
    allowed = (col_at <= row_at)[None, :, :] & valid_keys[:, None, :]
    scores = jnp.where(allowed, scores, MASKED)
    row_peak = lax.optimization_barrier(jnp.max(scores, axis=-1, keepdims=True))
    weights_raw = jnp.exp(scores - row_peak)
    return weights_raw / lax.optimization_barrier(jnp.sum(weights_raw, axis=-1, keepdims=True))

def cluster_group(query_h, key_h, value_h, grad_h, slot_table, valid_slots):
    score_scale = 1.0 / math.sqrt(DH)

    def fetch_rows(source):
        rows_now = source[slot_table].astype(jnp.float32)
        return jnp.where(valid_slots[:, :, None], rows_now, 0.0)
    query_rows = fetch_rows(query_h)
    key_rows = fetch_rows(key_h)
    value_rows = fetch_rows(value_h)
    grad_rows = fetch_rows(grad_h)
    probs_full = attention_probs(query_rows, key_rows, valid_slots, score_scale)
    probs_low = rounded(probs_full)
    out_rows = rounded(jnp.einsum('hij,hjd->hid', probs_low, value_rows, precision=lax.Precision.HIGHEST))
    grad_prob = jnp.einsum('hid,hjd->hij', grad_rows, value_rows, precision=lax.Precision.HIGHEST)
    row_delta = lax.optimization_barrier(jnp.sum(grad_rows * out_rows, axis=-1, keepdims=True))
    grad_score = rounded(probs_full * (grad_prob - row_delta) * score_scale)
    grad_query = jnp.einsum('hij,hjd->hid', grad_score, key_rows, precision=lax.Precision.HIGHEST)
    grad_key = jnp.einsum('hij,hid->hjd', grad_score, query_rows, precision=lax.Precision.HIGHEST)
    grad_value = jnp.einsum('hij,hid->hjd', probs_low, grad_rows, precision=lax.Precision.HIGHEST)
    return (out_rows, grad_query, grad_key, grad_value)

def head_pass(head_args):
    ids_h, query_h, key_h, value_h, grad_h = head_args
    cluster_iota = jnp.arange(CLUSTERS, dtype=jnp.int32)
    member = ids_h[:, None] == cluster_iota[None, :]
    counts = lax.optimization_barrier(jnp.sum(member.astype(jnp.int32), axis=0)).astype(jnp.int32)
    sorted_tokens = jnp.argsort(ids_h, stable=True).astype(jnp.int32)
    starts = (jnp.cumsum(counts) - counts).astype(jnp.int32)
    slot_iota = jnp.arange(SLOTS, dtype=jnp.int32)
    position = starts[:, None] + slot_iota[None, :]
    valid_all = slot_iota[None, :] < counts[:, None]
    slot_table = sorted_tokens[jnp.minimum(position, TOKENS - 1)]
    groups = CLUSTERS // 8

    def group_step(pair_in):
        return cluster_group(query_h, key_h, value_h, grad_h, pair_in[0], pair_in[1])
    results = lax.map(group_step, (slot_table.reshape(groups, 8, SLOTS), valid_all.reshape(groups, 8, SLOTS)))
    landing = jnp.where(valid_all, slot_table, TOKENS).reshape(-1)

    def place_rows(result):
        empty = jnp.zeros((TOKENS + 1, DH), jnp.float32)
        return empty.at[landing].set(result.reshape(-1, DH))[:TOKENS]
    key_sums = jax.ops.segment_sum(key_h.astype(jnp.float32), ids_h, num_segments=CLUSTERS)
    return (place_rows(results[0]), place_rows(results[1]), place_rows(results[2]), place_rows(results[3]), key_sums)

def reference(queries, keys, values, out_grad, cluster_ids, cluster_slot, centroids):

    def heads_first(array_in):
        return array_in.reshape(TOKENS, H, DH).transpose(1, 0, 2)

    def tokens_first(array_in):
        return array_in.transpose(1, 0, 2).reshape(TOKENS, H * DH).astype(jnp.bfloat16)
    results = lax.map(head_pass, (cluster_ids[:, :, 0], heads_first(queries), heads_first(keys), heads_first(values), heads_first(out_grad)))
    key_sums = results[4]
    by_slot = jnp.zeros_like(key_sums).at[:, cluster_slot].set(key_sums)
    blend_sum = DECAY_RATE * centroids + (1.0 - DECAY_RATE) * by_slot
    new_centroids = blend_sum / jnp.sqrt(lax.optimization_barrier(jnp.mean(blend_sum * blend_sum, axis=-1, keepdims=True)) + 1e-06)
    return (tokens_first(results[0]), tokens_first(results[1]), tokens_first(results[2]), tokens_first(results[3]), new_centroids)
```

```python
import math

import jax
import jax.numpy as jnp
from jax import lax
from jax.experimental import pallas as pl
from jax.experimental.pallas import tpu as pltpu
from jax.sharding import PartitionSpec as P

CAP = 4
DECAY_RATE = 0.9
MASKED = -1e30
ABSENT = 64.0
CHUNKS = 2
VMEM_BYTES = 48 * 1024 * 1024

F32 = jnp.float32
BF16 = jnp.bfloat16
CONTRACT_LAST = (((1,), (1,)), ((), ()))
CONTRACT_FIRST = (((0,), (0,)), ((), ()))


def iota(shape, dim):
    return lax.broadcasted_iota(jnp.int32, shape, dim)


def dot(left, right):
    return jnp.dot(left, right, preferred_element_type=F32)


def pack_kernel(ids_ref, slot_ref, q_ref, k_ref, v_ref, g_ref, send_ref, flat_ref, earlier_ref):
    tok_rows = ids_ref.shape[2]
    cluster_count = slot_ref.shape[1]
    slot_rows = cluster_count * CAP

    @pl.when(pl.program_id(0) == 0)
    def _():
        earlier_ref[...] = (iota((tok_rows, tok_rows), 0) < iota((tok_rows, tok_rows), 1)).astype(
            F32
        ).astype(BF16)

    ids_row = ids_ref[0]
    member = iota((cluster_count, tok_rows), 0) == ids_row
    member_f = jnp.where(member, 1.0, 0.0)
    member_low = member_f.astype(BF16)
    slots_low = jnp.broadcast_to(slot_ref[...].astype(F32), (8, cluster_count)).astype(BF16)
    slot_row = dot(slots_low, member_low)[0:1]
    rank_row = jnp.sum(dot(member_low, earlier_ref[...]) * member_f, axis=0, keepdims=True)
    flat_row = (slot_row * CAP + rank_row).astype(jnp.int32)
    flat_ref[0] = flat_row
    place = jnp.where(iota((slot_rows, tok_rows), 0) == flat_row, 1.0, 0.0).astype(BF16)
    ones = jnp.ones((tok_rows, 128), BF16)
    head_size = q_ref.shape[1]
    taken = dot(place, ones)
    out_shape = send_ref.shape[:2] + (head_size,)

    def put(at, rows):
        send_ref[:, :, at * head_size : (at + 1) * head_size] = rows.astype(BF16).reshape(out_shape)

    put(0, dot(place, q_ref[...]))
    put(1, dot(place, k_ref[...]) + (1.0 - taken) * ABSENT)
    put(2, dot(place, v_ref[...]))
    put(3, dot(place, g_ref[...]))


def owner_kernel(recv_ref, cent_ref, back_ref, new_ref, turn_ref, causal_ref, rows_ref, grads_ref):
    source_count, block_rows, width = recv_ref.shape
    head_size = width // 4
    owned = block_rows // CAP
    slot_count = source_count * CAP
    group_rows = 16 * block_rows
    groups = source_count // 16
    part = 16 * CAP
    score_scale = 1.0 / math.sqrt(head_size)

    @pl.when(pl.program_id(0) == 0)
    def _():
        row_at = iota((group_rows, group_rows), 0)
        col_at = iota((group_rows, group_rows), 1)
        cluster_of = row_at // part
        source_of = (row_at % part) // CAP
        from_row = source_of * block_rows + cluster_of * CAP + row_at % CAP
        turn_ref[...] = jnp.where(from_row == col_at, 1.0, 0.0).astype(BF16)
        causal_ref[...] = jnp.where(
            iota((slot_count, slot_count), 1) <= iota((slot_count, slot_count), 0), 0.0, MASKED
        )

    turn = turn_ref[...]
    for group in range(groups):
        arrived = recv_ref[group * 16 : (group + 1) * 16].reshape(group_rows, width)
        turned = dot(turn, arrived).astype(BF16)
        rows_ref[:, group * part : (group + 1) * part, :] = turned.reshape(owned, part, width)

    first_lane = jnp.where(iota((8, head_size), 1) == 0, 1.0, 0.0).astype(BF16)
    for cluster in range(owned):
        q = rows_ref[cluster, :, 0:head_size]
        k = rows_ref[cluster, :, head_size : 2 * head_size]
        v = rows_ref[cluster, :, 2 * head_size : 3 * head_size]
        g = rows_ref[cluster, :, 3 * head_size : 4 * head_size]
        marks = lax.dot_general(first_lane, k, CONTRACT_LAST, preferred_element_type=F32)
        present = marks < ABSENT / 2
        bias = jnp.where(present, 0.0, MASKED)[0:1]
        scores = lax.dot_general(q, k, CONTRACT_LAST, preferred_element_type=F32) * score_scale
        scores = scores + (causal_ref[...] + bias)
        weights = jnp.exp(scores - jnp.max(scores, axis=-1, keepdims=True))
        probs = weights / jnp.sum(weights, axis=-1, keepdims=True)
        probs_low = probs.astype(BF16)
        out = dot(probs_low, v).astype(BF16)
        grad_prob = lax.dot_general(g, v, CONTRACT_LAST, preferred_element_type=F32)
        delta = jnp.sum(g.astype(F32) * out.astype(F32), axis=-1, keepdims=True)
        grad_score = (probs * (grad_prob - delta) * score_scale).astype(BF16)
        grad_q = dot(grad_score, k)
        grad_k = lax.dot_general(grad_score, q, CONTRACT_FIRST, preferred_element_type=F32)
        grad_v = lax.dot_general(probs_low, g, CONTRACT_FIRST, preferred_element_type=F32)
        grads_ref[cluster, :, 0:head_size] = out
        grads_ref[cluster, :, head_size : 2 * head_size] = grad_q.astype(BF16)
        grads_ref[cluster, :, 2 * head_size : 3 * head_size] = grad_k.astype(BF16)
        grads_ref[cluster, :, 3 * head_size : 4 * head_size] = grad_v.astype(BF16)
        key_sums = dot(jnp.where(present, 1.0, 0.0).astype(BF16), k)[0:1]
        blend = DECAY_RATE * cent_ref[0, cluster : cluster + 1, :] + (1.0 - DECAY_RATE) * key_sums
        new_ref[0, cluster : cluster + 1, :] = blend / jnp.sqrt(
            jnp.mean(blend * blend, axis=-1, keepdims=True) + 1e-06
        )

    for group in range(groups):
        leaving = grads_ref[:, group * part : (group + 1) * part, :].reshape(group_rows, width)
        turned = lax.dot_general(turn, leaving, CONTRACT_FIRST, preferred_element_type=F32)
        back_ref[group * 16 : (group + 1) * 16] = turned.astype(BF16).reshape(
            16, block_rows, width
        )


def unpack_kernel(chunk, flat_ref, ret_ref, *refs):
    out_refs = refs[-4:]
    sources, block_rows, width = ret_ref.shape
    head_size = width // 4
    tok_rows, heads = flat_ref.shape
    slot_rows = sources * block_rows
    here = iota((tok_rows, heads), 1) == pl.program_id(0)
    flat_col = jnp.sum(jnp.where(here, flat_ref[...], 0), axis=1, keepdims=True)
    take = jnp.where(iota((tok_rows, slot_rows), 1) == flat_col, 1.0, 0.0).astype(BF16)
    rows = dot(take, ret_ref[...].reshape(slot_rows, width)).astype(BF16)
    for at, out_ref in enumerate(out_refs):
        out_ref[...] = rows[:, at * head_size : (at + 1) * head_size]


def params():
    return pltpu.CompilerParams(vmem_limit_bytes=VMEM_BYTES)


def body(queries, keys, values, out_grad, cluster_ids, cluster_slot, centroids):
    seq_count = lax.axis_size("seq")
    local_heads, tok_rows = cluster_ids.shape[:2]
    cluster_count = cluster_slot.shape[0]
    owned = cluster_count // seq_count
    head_size = centroids.shape[2]
    heads = local_heads // CHUNKS
    block_rows = owned * CAP
    width = 4 * head_size
    slot_count = seq_count * CAP
    sent = jax.ShapeDtypeStruct((seq_count, heads * block_rows, width), BF16)
    sent_bytes = seq_count * heads * block_rows * width * 2
    ids_rows = cluster_ids.reshape(local_heads, 1, tok_rows)
    slot_row = cluster_slot.reshape(1, cluster_count)
    block = pl.BlockSpec((seq_count, block_rows, width), lambda h: (0, h, 0))

    def exchange(rows):
        return lax.all_to_all(rows, "seq", split_axis=0, concat_axis=0, tiled=True)

    def pack(chunk):
        column = pl.BlockSpec((tok_rows, head_size), lambda h: (0, chunk * heads + h))
        return pl.pallas_call(
            pack_kernel,
            grid=(heads,),
            in_specs=[
                pl.BlockSpec((1, 1, tok_rows), lambda h: (chunk * heads + h, 0, 0)),
                pl.BlockSpec((1, cluster_count), lambda h: (0, 0)),
                column,
                column,
                column,
                column,
            ],
            out_specs=[block, pl.BlockSpec((1, 1, tok_rows), lambda h: (h, 0, 0))],
            out_shape=[sent, jax.ShapeDtypeStruct((heads, 1, tok_rows), jnp.int32)],
            scratch_shapes=[pltpu.VMEM((tok_rows, tok_rows), BF16)],
            compiler_params=params(),
            cost_estimate=pl.CostEstimate(
                flops=heads * 2 * 1024 * 512 * 640, bytes_accessed=2 * sent_bytes, transcendentals=0
            ),
            name="pack",
        )(ids_rows, slot_row, queries, keys, values, out_grad)

    def own(chunk, received):
        return pl.pallas_call(
            owner_kernel,
            grid=(heads,),
            in_specs=[
                block,
                pl.BlockSpec((1, owned, head_size), lambda h: (chunk * heads + h, 0, 0)),
            ],
            out_specs=[block, pl.BlockSpec((1, owned, head_size), lambda h: (h, 0, 0))],
            out_shape=[sent, jax.ShapeDtypeStruct((heads, owned, head_size), F32)],
            scratch_shapes=[
                pltpu.VMEM((16 * block_rows, 16 * block_rows), BF16),
                pltpu.VMEM((slot_count, slot_count), F32),
                pltpu.VMEM((owned, slot_count, width), BF16),
                pltpu.VMEM((owned, slot_count, width), BF16),
            ],
            compiler_params=params(),
            cost_estimate=pl.CostEstimate(
                flops=heads * owned * 7 * 2 * slot_count * slot_count * head_size,
                bytes_accessed=2 * sent_bytes,
                transcendentals=heads * owned * slot_count * slot_count,
            ),
            name="own",
        )(received, centroids)

    def unpack(chunk, flat_cols, returned, previous):
        column = pl.BlockSpec((tok_rows, head_size), lambda h: (0, chunk * heads + h))
        whole = jax.ShapeDtypeStruct((tok_rows, local_heads * head_size), BF16)

        def kernel(*refs):
            unpack_kernel(chunk, *refs)

        return pl.pallas_call(
            kernel,
            grid=(heads,),
            in_specs=[pl.BlockSpec((tok_rows, heads), lambda h: (0, 0)), block]
            + [pl.BlockSpec(memory_space=pl.ANY)] * len(previous),
            out_specs=[column] * 4,
            out_shape=[whole] * 4,
            input_output_aliases={2 + i: i for i in range(len(previous))},
            compiler_params=params(),
            cost_estimate=pl.CostEstimate(
                flops=heads * 2 * 1024 * 512 * 512, bytes_accessed=2 * sent_bytes, transcendentals=0
            ),
            name="unpack",
        )(flat_cols, returned, *previous)

    packed = [pack(chunk) for chunk in range(CHUNKS)]
    received = [exchange(rows) for rows, _ in packed]
    owned_now = [own(chunk, rows) for chunk, rows in enumerate(received)]
    returned = [exchange(rows) for rows, _ in owned_now]
    outs = ()
    for chunk in range(CHUNKS):
        flat_cols = packed[chunk][1].reshape(heads, tok_rows).T
        outs = unpack(chunk, flat_cols, returned[chunk], tuple(outs))
    new_centroids = jnp.concatenate([new for _, new in owned_now], axis=0)
    return (*outs, new_centroids)


def solution(mesh):
    return jax.shard_map(
        body,
        mesh=mesh,
        in_specs=(
            P("seq", "head"),
            P("seq", "head"),
            P("seq", "head"),
            P("seq", "head"),
            P("head", "seq", None),
            P(),
            P("head", "seq", None),
        ),
        out_specs=(
            P("seq", "head"),
            P("seq", "head"),
            P("seq", "head"),
            P("seq", "head"),
            P("head", "seq", None),
        ),
        check_vma=False,
    )
```

```python
import math

import jax
import jax.numpy as jnp
from jax import lax
from jax.experimental import pallas as pl
from jax.experimental.pallas import tpu as pltpu
from jax.sharding import PartitionSpec as P

CAP = 4
DECAY_RATE = 0.9
MASKED = -1e30
ABSENT = 64.0
CHUNKS = 2
FIXED = 2
PACKED = 16
TURN_BY = 9
VMEM_BYTES = 60 * 1024 * 1024

F32 = jnp.float32
BF16 = jnp.bfloat16
CONTRACT_LAST = (((1,), (1,)), ((), ()))
CONTRACT_FIRST = (((0,), (0,)), ((), ()))


def iota(shape, dim):
    return lax.broadcasted_iota(jnp.int32, shape, dim)


def dot(left, right):
    return jnp.dot(left, right, preferred_element_type=F32)


def pack_kernel(ids_ref, slot_ref, q_ref, k_ref, v_ref, g_ref, send_ref, flat_ref, earlier_ref):
    tok_rows = ids_ref.shape[2]
    cluster_count = slot_ref.shape[1]
    slot_rows = cluster_count * CAP

    @pl.when(pl.program_id(0) == 0)
    def _():
        earlier_ref[...] = (iota((tok_rows, tok_rows), 0) < iota((tok_rows, tok_rows), 1)).astype(
            F32
        ).astype(BF16)

    ids_row = ids_ref[0]
    member = iota((cluster_count, tok_rows), 0) == ids_row
    member_f = jnp.where(member, 1.0, 0.0)
    member_low = member_f.astype(BF16)
    slots_low = jnp.broadcast_to(slot_ref[...].astype(F32), (8, cluster_count)).astype(BF16)
    slot_row = dot(slots_low, member_low)[0:1]
    rank_row = jnp.sum(dot(member_low, earlier_ref[...]) * member_f, axis=0, keepdims=True)
    flat_row = (slot_row * CAP + rank_row).astype(jnp.int32)
    flat_ref[0] = flat_row
    place = jnp.where(iota((slot_rows, tok_rows), 0) == flat_row, 1.0, 0.0).astype(BF16)
    ones = jnp.ones((tok_rows, 128), BF16)
    head_size = q_ref.shape[1]
    taken = dot(place, ones)
    out_shape = send_ref.shape[:2] + (head_size,)

    def put(at, rows):
        send_ref[:, :, at * head_size : (at + 1) * head_size] = rows.astype(BF16).reshape(out_shape)

    put(0, dot(place, q_ref[...]))
    put(1, dot(place, k_ref[...]) + (1.0 - taken) * ABSENT)
    put(2, dot(place, v_ref[...]))
    put(3, dot(place, g_ref[...]))


def owner_kernel(recv_ref, cent_ref, back_ref, new_ref, turn_ref, causal_ref, rows_ref, grads_ref):
    source_count, block_rows, width = recv_ref.shape
    head_size = width // 4
    owned = block_rows // CAP
    slot_count = source_count * CAP
    group_rows = 16 * block_rows
    groups = source_count // 16
    part = 16 * CAP
    score_scale = 1.0 / math.sqrt(head_size)

    @pl.when(pl.program_id(0) == 0)
    def _():
        row_at = iota((group_rows, group_rows), 0)
        col_at = iota((group_rows, group_rows), 1)
        cluster_of = row_at // part
        source_of = (row_at % part) // CAP
        from_row = source_of * block_rows + cluster_of * CAP + row_at % CAP
        turn_ref[...] = jnp.where(from_row == col_at, 1.0, 0.0).astype(BF16)
        causal_ref[...] = jnp.where(
            iota((slot_count, slot_count), 1) <= iota((slot_count, slot_count), 0), 0.0, MASKED
        )

    turn = turn_ref[...]
    for group in range(groups):
        arrived = recv_ref[group * 16 : (group + 1) * 16].reshape(group_rows, width)
        turned = dot(turn, arrived).astype(BF16)
        rows_ref[:, group * part : (group + 1) * part, :] = turned.reshape(owned, part, width)

    first_lane = jnp.where(iota((8, head_size), 1) == 0, 1.0, 0.0).astype(BF16)
    for cluster in range(owned):
        q = rows_ref[cluster, :, 0:head_size]
        k = rows_ref[cluster, :, head_size : 2 * head_size]
        v = rows_ref[cluster, :, 2 * head_size : 3 * head_size]
        g = rows_ref[cluster, :, 3 * head_size : 4 * head_size]
        marks = lax.dot_general(first_lane, k, CONTRACT_LAST, preferred_element_type=F32)
        present = marks < ABSENT / 2
        bias = jnp.where(present, 0.0, MASKED)[0:1]
        scores = lax.dot_general(q, k, CONTRACT_LAST, preferred_element_type=F32) * score_scale
        scores = scores + (causal_ref[...] + bias)
        weights = jnp.exp(scores - jnp.max(scores, axis=-1, keepdims=True))
        probs = weights / jnp.sum(weights, axis=-1, keepdims=True)
        probs_low = probs.astype(BF16)
        out = dot(probs_low, v).astype(BF16)
        grad_prob = lax.dot_general(g, v, CONTRACT_LAST, preferred_element_type=F32)
        delta = jnp.sum(g.astype(F32) * out.astype(F32), axis=-1, keepdims=True)
        grad_score = (probs * (grad_prob - delta) * score_scale).astype(BF16)
        grad_q = dot(grad_score, k)
        grad_k = lax.dot_general(grad_score, q, CONTRACT_FIRST, preferred_element_type=F32)
        grad_v = lax.dot_general(probs_low, g, CONTRACT_FIRST, preferred_element_type=F32)
        grads_ref[cluster, :, 0:head_size] = out
        grads_ref[cluster, :, head_size : 2 * head_size] = grad_q.astype(BF16)
        grads_ref[cluster, :, 2 * head_size : 3 * head_size] = grad_k.astype(BF16)
        grads_ref[cluster, :, 3 * head_size : 4 * head_size] = grad_v.astype(BF16)
        key_sums = dot(jnp.where(present, 1.0, 0.0).astype(BF16), k)[0:1]
        blend = DECAY_RATE * cent_ref[0, cluster : cluster + 1, :] + (1.0 - DECAY_RATE) * key_sums
        new_ref[0, cluster : cluster + 1, :] = blend / jnp.sqrt(
            jnp.mean(blend * blend, axis=-1, keepdims=True) + 1e-06
        )

    for group in range(groups):
        leaving = grads_ref[:, group * part : (group + 1) * part, :].reshape(group_rows, width)
        turned = lax.dot_general(turn, leaving, CONTRACT_FIRST, preferred_element_type=F32)
        back_ref[group * 16 : (group + 1) * 16] = turned.astype(BF16).reshape(
            16, block_rows, width
        )


def unpack_kernel(chunk, flat_ref, ret_ref, *refs):
    out_refs = refs[-4:]
    sources, block_rows, width = ret_ref.shape
    head_size = width // 4
    tok_rows, heads = flat_ref.shape
    slot_rows = sources * block_rows
    here = iota((tok_rows, heads), 1) == pl.program_id(0)
    flat_col = jnp.sum(jnp.where(here, flat_ref[...], 0), axis=1, keepdims=True)
    take = jnp.where(iota((tok_rows, slot_rows), 1) == flat_col, 1.0, 0.0).astype(BF16)
    rows = dot(take, ret_ref[...].reshape(slot_rows, width)).astype(BF16)
    for at, out_ref in enumerate(out_refs):
        out_ref[...] = rows[:, at * head_size : (at + 1) * head_size]


def route_kernel(ids_ref, slot_ref, base_ref, over_ref, tag_ref, peak_ref):
    heads, _, tok_rows = ids_ref.shape
    cluster_count = slot_ref.shape[1]
    owners = cluster_count // CAP
    rest = CAP - FIXED
    earlier = jnp.where(
        iota((tok_rows, tok_rows), 0) < iota((tok_rows, tok_rows), 1), 1.0, 0.0
    ).astype(BF16)
    slots_low = jnp.broadcast_to(slot_ref[...].astype(F32), (8, cluster_count)).astype(BF16)
    filled = jnp.zeros((owners, 1), F32)
    for head in range(heads):
        member_f = jnp.where(iota((cluster_count, tok_rows), 0) == ids_ref[head], 1.0, 0.0)
        member_low = member_f.astype(BF16)
        slot = dot(slots_low, member_low)[0:1].astype(jnp.int32)
        rank = jnp.sum(dot(member_low, earlier) * member_f, axis=0, keepdims=True)
        rank = rank.astype(jnp.int32)
        owner = (slot // CAP + TURN_BY * head) % owners
        within = slot % CAP
        fits = rank < FIXED
        base_ref[head] = jnp.where(fits, (owner * CAP + within) * FIXED + rank, -1)
        here = (iota((owners, tok_rows), 0) == owner) & (rank >= FIXED)
        here_f = jnp.where(here, 1.0, 0.0)
        before = dot(here_f.astype(BF16), earlier) + filled
        place = jnp.sum(before * here_f, axis=0, keepdims=True).astype(jnp.int32)
        filled = filled + jnp.sum(here_f, axis=1, keepdims=True)
        over_ref[head] = jnp.where(fits, -1, owner * 64 + place)
        tag_ref[head] = (head * CAP + within) * rest + rank - FIXED
    peak = jnp.max(filled, axis=0, keepdims=True).astype(jnp.int32)
    peak_ref[...] = jnp.broadcast_to(peak, peak_ref.shape)


def token_rows(refs, at, head_size):
    lanes = slice(at * head_size, (at + 1) * head_size)
    return jnp.concatenate([ref[:, lanes] for ref in refs], axis=1)


def put_fixed(base_ref, rows, pair_rows):
    tok_rows, width = rows[0].shape
    head_size = width // 4
    halves = []
    for at in range(2):
        slot_rows = pair_rows[0] * pair_rows[1] // 2
        place = jnp.where(iota((slot_rows, tok_rows), 0) == base_ref[at], 1.0, 0.0).astype(BF16)
        taken = dot(place, jnp.ones((tok_rows, head_size), BF16))
        placed = dot(place, rows[at])
        marked = placed[:, head_size : 2 * head_size] + (1.0 - taken) * ABSENT
        placed = jnp.concatenate(
            [placed[:, :head_size], marked, placed[:, 2 * head_size :]], axis=1
        )
        halves.append(placed.reshape(pair_rows[0], pair_rows[1] // 2, width))
    return jnp.concatenate(halves, axis=1).astype(BF16)


def pack_first_kernel(
    base_ref, over_ref, tag_ref, q_ref, k_ref, v_ref, g_ref, send_ref, total_ref, tags_ref
):
    owners, send_rows, width = send_ref.shape
    tok_rows = q_ref.shape[0]
    head_size = width // 4
    step = pl.program_id(0)
    rows = [token_rows((q_ref, k_ref, v_ref, g_ref), at, head_size) for at in range(2)]
    places = []
    tags = None
    for at in range(2):
        over = over_ref[at]
        owner = over // 64
        place = over % 64
        goes = (over >= 0) & (place < PACKED - 1)
        row_at = jnp.where(goes, owner * PACKED + place, -1)
        places.append(
            jnp.where(iota((owners * PACKED, tok_rows), 0) == row_at, 1.0, 0.0).astype(BF16)
        )
        named = jnp.where(goes & (iota((owners, tok_rows), 0) == owner), tag_ref[at] + 1, 0)
        lane = jnp.where(iota((head_size, tok_rows), 0) == place, 1.0, 0.0).astype(BF16)
        tagged = lax.dot_general(
            named.astype(F32).astype(BF16), lane, CONTRACT_LAST, preferred_element_type=F32
        )
        tags = tagged if tags is None else tags + tagged
    added = dot(jnp.concatenate(places, axis=1), jnp.concatenate(rows, axis=0))

    @pl.when(step == 0)
    def _():
        total_ref[...] = added
        tags_ref[...] = tags

    @pl.when(step > 0)
    def _():
        total_ref[...] += added
        tags_ref[...] += tags

    @pl.when(step < pl.num_programs(0) // CHUNKS)
    def _():
        at_row = pl.multiple_of(step * 16, 16)
        send_ref[:, pl.ds(at_row, 16), :] = put_fixed(base_ref, rows, (owners, 16))

    @pl.when(step == pl.num_programs(0) - 1)
    def _():
        header = jnp.where(
            iota((owners * PACKED, owners), 0)
            == iota((owners * PACKED, owners), 1) * PACKED + PACKED - 1,
            1.0,
            0.0,
        ).astype(BF16)
        total_ref[:, :head_size] += dot(header, tags_ref[...].astype(BF16))
        packed = total_ref[...].astype(BF16).reshape(owners, PACKED, width)
        send_ref[:, send_rows - PACKED :, :] = packed


def pack_second_kernel(base_ref, q_ref, k_ref, v_ref, g_ref, send_ref):
    owners, pair_rows, width = send_ref.shape
    rows = [token_rows((q_ref, k_ref, v_ref, g_ref), at, width // 4) for at in range(2)]
    send_ref[...] = put_fixed(base_ref, rows, (owners, pair_rows))


def own_pair_kernel(first_step, last, *refs):
    fixed_ref, over_ref = refs[:2]
    if last:
        before_ref, back_ref, sums_ref = refs[2:5]
    else:
        back_ref, over_back_ref, sums_ref = refs[2:5]
    turn_ref, causal_ref, rows_ref, grads_ref, spread_ref = refs[5:]
    sources, pair_rows, width = fixed_ref.shape
    head_size = width // 4
    problems = pair_rows // FIXED
    group_rows = 16 * pair_rows
    groups = sources // 16
    part = 16 * FIXED
    half = sources * FIXED
    slot_count = sources * CAP
    score_scale = 1.0 / math.sqrt(head_size)
    step = pl.program_id(0)

    @pl.when(step == 0)
    def _():
        row_at = iota((group_rows, group_rows), 0)
        source_of = (row_at % part) // FIXED
        from_row = source_of * pair_rows + (row_at // part) * FIXED + row_at % FIXED
        turn_ref[...] = jnp.where(from_row == iota((group_rows, group_rows), 1), 1.0, 0.0).astype(
            BF16
        )

        def order(dim):
            at = iota((slot_count, slot_count), dim)
            late = at // half
            return ((at % half) // FIXED) * CAP + at % FIXED + FIXED * late

        causal_ref[...] = jnp.where(order(1) <= order(0), 0.0, MASKED)

    turn = turn_ref[...]
    ones = jnp.ones((16 * PACKED, head_size), BF16)
    header_of = jnp.where(
        iota((16, 16 * PACKED), 1) == iota((16, 16 * PACKED), 0) * PACKED + PACKED - 1, 1.0, 0.0
    ).astype(BF16)
    repeat = jnp.where(
        (iota((head_size, 16 * PACKED), 0) == iota((head_size, 16 * PACKED), 1) % PACKED)
        & (iota((head_size, 16 * PACKED), 0) < PACKED - 1),
        1.0,
        0.0,
    ).astype(BF16)
    source_of_lane = iota((1, 16 * PACKED), 1) // PACKED
    for group in range(groups):
        from_sources = slice(group * 16, (group + 1) * 16)
        arrived = fixed_ref[from_sources].reshape(group_rows, width)
        turned = dot(turn, arrived).astype(BF16)
        rows_ref[:, group * part : (group + 1) * part, :] = turned.reshape(problems, part, width)
        packed = over_ref[from_sources].reshape(16 * PACKED, width)
        header = dot(header_of, packed[:, :head_size]).astype(BF16)
        repeated = dot(header, repeat)
        own_lane = iota((16, 16 * PACKED), 0) == source_of_lane
        tag = jnp.sum(jnp.where(own_lane, repeated, 0.0), axis=0, keepdims=True)
        tag = tag.astype(jnp.int32) - 1
        mine = (tag >= 0) & (tag // (problems * FIXED) == first_step + step)
        problem = (tag // FIXED) % problems
        slot = jnp.where(mine, problem * part + source_of_lane * FIXED + tag % FIXED, -1)
        spread = jnp.where(iota((group_rows, 16 * PACKED), 0) == slot, 1.0, 0.0).astype(BF16)
        spread_ref[group] = spread
        taken = dot(spread, ones)
        placed = dot(spread, packed)
        marked = placed[:, head_size : 2 * head_size] + (1.0 - taken) * ABSENT
        placed = jnp.concatenate(
            [placed[:, :head_size], marked, placed[:, 2 * head_size :]], axis=1
        )
        rows_ref[:, half + group * part : half + (group + 1) * part, :] = placed.astype(
            BF16
        ).reshape(problems, part, width)

    first_lane = jnp.where(iota((8, head_size), 1) == 0, 1.0, 0.0).astype(BF16)

    def attend(problem):
        q = rows_ref[problem, :, 0:head_size]
        k = rows_ref[problem, :, head_size : 2 * head_size]
        v = rows_ref[problem, :, 2 * head_size : 3 * head_size]
        g = rows_ref[problem, :, 3 * head_size : 4 * head_size]
        marks = lax.dot_general(first_lane, k, CONTRACT_LAST, preferred_element_type=F32)
        present = marks < ABSENT / 2
        bias = jnp.where(present, 0.0, MASKED)[0:1]
        scores = lax.dot_general(q, k, CONTRACT_LAST, preferred_element_type=F32) * score_scale
        scores = scores + (causal_ref[...] + bias)
        weights = jnp.exp(scores - jnp.max(scores, axis=-1, keepdims=True))
        probs = weights / jnp.sum(weights, axis=-1, keepdims=True)
        probs_low = probs.astype(BF16)
        out = dot(probs_low, v).astype(BF16)
        grad_prob = lax.dot_general(g, v, CONTRACT_LAST, preferred_element_type=F32)
        delta = jnp.sum(g.astype(F32) * out.astype(F32), axis=-1, keepdims=True)
        grad_score = (probs * (grad_prob - delta) * score_scale).astype(BF16)
        grad_q = dot(grad_score, k)
        grad_k = lax.dot_general(grad_score, q, CONTRACT_FIRST, preferred_element_type=F32)
        grad_v = lax.dot_general(probs_low, g, CONTRACT_FIRST, preferred_element_type=F32)
        grads_ref[problem, :, 0:head_size] = out
        grads_ref[problem, :, head_size : 2 * head_size] = grad_q.astype(BF16)
        grads_ref[problem, :, 2 * head_size : 3 * head_size] = grad_k.astype(BF16)
        grads_ref[problem, :, 3 * head_size : 4 * head_size] = grad_v.astype(BF16)
        sums = dot(jnp.where(present, 1.0, 0.0).astype(BF16), k)[0:1]
        sums_ref[0, pl.ds(problem, 1), :] = sums

    @pl.loop(0, problems // 2)
    def _(pair):
        attend(pair * 2)
        attend(pair * 2 + 1)

    for group in range(groups):
        from_sources = slice(group * 16, (group + 1) * 16)
        leaving = grads_ref[:, group * part : (group + 1) * part, :].reshape(group_rows, width)
        turned = lax.dot_general(turn, leaving, CONTRACT_FIRST, preferred_element_type=F32)
        turned = turned.astype(BF16).reshape(16, pair_rows, width)
        others = grads_ref[:, half + group * part : half + (group + 1) * part, :]
        gathered = lax.dot_general(
            spread_ref[group],
            others.reshape(group_rows, width),
            CONTRACT_FIRST,
            preferred_element_type=F32,
        )
        gathered = gathered.astype(BF16).reshape(16, PACKED, width)
        if last:
            at_row = pl.multiple_of(step * pair_rows, pair_rows)
            back_ref[from_sources, pl.ds(at_row, pair_rows), :] = turned
            rest = slice(back_ref.shape[1] - PACKED, back_ref.shape[1])

            @pl.when(step == 0)
            def _():
                back_ref[from_sources, rest, :] = before_ref[from_sources] + gathered

            @pl.when(step > 0)
            def _():
                back_ref[from_sources, rest, :] += gathered
        else:
            back_ref[from_sources] = turned

            @pl.when(step == 0)
            def _():
                over_back_ref[from_sources] = gathered

            @pl.when(step > 0)
            def _():
                over_back_ref[from_sources] += gathered


def unpack_pair_kernel(steps, base_ref, over_ref, first_ref, second_ref, packed_ref, *out_refs):
    owners, pair_rows, width = first_ref.shape
    head_size = width // 4
    tok_rows, heads = base_ref.shape
    step = pl.program_id(0)
    packed = packed_ref[...].reshape(owners * PACKED, width)
    arrived = jnp.where(step < steps, first_ref[...], second_ref[...])
    fixed_count = owners * pair_rows // 2
    for at in range(2):
        here = iota((tok_rows, heads), 1) == step * 2 + at
        base = jnp.sum(jnp.where(here, base_ref[...], 0), axis=1, keepdims=True)
        over = jnp.sum(jnp.where(here, over_ref[...], 0), axis=1, keepdims=True)
        over = jnp.where(over < 0, -1, (over // 64) * PACKED + over % 64)
        take = jnp.where(iota((tok_rows, fixed_count), 1) == base, 1.0, 0.0).astype(BF16)
        take_over = jnp.where(iota((tok_rows, owners * PACKED), 1) == over, 1.0, 0.0).astype(BF16)
        half_rows = pair_rows // 2
        mine = arrived.astype(F32)[:, at * half_rows : (at + 1) * half_rows, :]
        rows = dot(take, mine.reshape(fixed_count, width).astype(BF16)) + dot(take_over, packed)
        rows = rows.astype(BF16)
        for which, out_ref in enumerate(out_refs):
            out_ref[:, at * head_size : (at + 1) * head_size] = rows[
                :, which * head_size : (which + 1) * head_size
            ]


def params():
    return pltpu.CompilerParams(vmem_limit_bytes=VMEM_BYTES)


def dense(queries, keys, values, out_grad, cluster_ids, cluster_slot, centroids):
    seq_count = lax.axis_size("seq")
    local_heads, tok_rows = cluster_ids.shape[:2]
    cluster_count = cluster_slot.shape[0]
    owned = cluster_count // seq_count
    head_size = centroids.shape[2]
    heads = local_heads // CHUNKS
    block_rows = owned * CAP
    width = 4 * head_size
    slot_count = seq_count * CAP
    sent = jax.ShapeDtypeStruct((seq_count, heads * block_rows, width), BF16)
    sent_bytes = seq_count * heads * block_rows * width * 2
    ids_rows = cluster_ids.reshape(local_heads, 1, tok_rows)
    slot_row = cluster_slot.reshape(1, cluster_count)
    block = pl.BlockSpec((seq_count, block_rows, width), lambda h: (0, h, 0))

    def exchange(rows):
        return lax.all_to_all(rows, "seq", split_axis=0, concat_axis=0, tiled=True)

    def pack(chunk):
        column = pl.BlockSpec((tok_rows, head_size), lambda h: (0, chunk * heads + h))
        return pl.pallas_call(
            pack_kernel,
            grid=(heads,),
            in_specs=[
                pl.BlockSpec((1, 1, tok_rows), lambda h: (chunk * heads + h, 0, 0)),
                pl.BlockSpec((1, cluster_count), lambda h: (0, 0)),
                column,
                column,
                column,
                column,
            ],
            out_specs=[block, pl.BlockSpec((1, 1, tok_rows), lambda h: (h, 0, 0))],
            out_shape=[sent, jax.ShapeDtypeStruct((heads, 1, tok_rows), jnp.int32)],
            scratch_shapes=[pltpu.VMEM((tok_rows, tok_rows), BF16)],
            compiler_params=params(),
            cost_estimate=pl.CostEstimate(
                flops=heads * 2 * 1024 * 512 * 640, bytes_accessed=2 * sent_bytes, transcendentals=0
            ),
            name="pack",
        )(ids_rows, slot_row, queries, keys, values, out_grad)

    def own(chunk, received):
        return pl.pallas_call(
            owner_kernel,
            grid=(heads,),
            in_specs=[
                block,
                pl.BlockSpec((1, owned, head_size), lambda h: (chunk * heads + h, 0, 0)),
            ],
            out_specs=[block, pl.BlockSpec((1, owned, head_size), lambda h: (h, 0, 0))],
            out_shape=[sent, jax.ShapeDtypeStruct((heads, owned, head_size), F32)],
            scratch_shapes=[
                pltpu.VMEM((16 * block_rows, 16 * block_rows), BF16),
                pltpu.VMEM((slot_count, slot_count), F32),
                pltpu.VMEM((owned, slot_count, width), BF16),
                pltpu.VMEM((owned, slot_count, width), BF16),
            ],
            compiler_params=params(),
            cost_estimate=pl.CostEstimate(
                flops=heads * owned * 7 * 2 * slot_count * slot_count * head_size,
                bytes_accessed=2 * sent_bytes,
                transcendentals=heads * owned * slot_count * slot_count,
            ),
            name="own",
        )(received, centroids)

    def unpack(chunk, flat_cols, returned, previous):
        column = pl.BlockSpec((tok_rows, head_size), lambda h: (0, chunk * heads + h))
        whole = jax.ShapeDtypeStruct((tok_rows, local_heads * head_size), BF16)

        def kernel(*refs):
            unpack_kernel(chunk, *refs)

        return pl.pallas_call(
            kernel,
            grid=(heads,),
            in_specs=[pl.BlockSpec((tok_rows, heads), lambda h: (0, 0)), block]
            + [pl.BlockSpec(memory_space=pl.ANY)] * len(previous),
            out_specs=[column] * 4,
            out_shape=[whole] * 4,
            input_output_aliases={2 + i: i for i in range(len(previous))},
            compiler_params=params(),
            cost_estimate=pl.CostEstimate(
                flops=heads * 2 * 1024 * 512 * 512, bytes_accessed=2 * sent_bytes, transcendentals=0
            ),
            name="unpack",
        )(flat_cols, returned, *previous)

    packed = [pack(chunk) for chunk in range(CHUNKS)]
    received = [exchange(rows) for rows, _ in packed]
    owned_now = [own(chunk, rows) for chunk, rows in enumerate(received)]
    returned = [exchange(rows) for rows, _ in owned_now]
    outs = ()
    for chunk in range(CHUNKS):
        flat_cols = packed[chunk][1].reshape(heads, tok_rows).T
        outs = unpack(chunk, flat_cols, returned[chunk], tuple(outs))
    new_centroids = jnp.concatenate([new for _, new in owned_now], axis=0)
    return (*outs, new_centroids)


def exchange(rows):
    return lax.all_to_all(rows, "seq", split_axis=0, concat_axis=0, tiled=True)


def adaptive(queries, keys, values, out_grad, routes, first_sent, centroids):
    base_rows, over_rows = routes
    seq_count = lax.axis_size("seq")
    heads, _, tok_rows = base_rows.shape
    owned, head_size = centroids.shape[1:]
    width = 4 * head_size
    pair_rows = 2 * owned * FIXED
    steps = heads // 2 // CHUNKS
    chunk_rows = steps * pair_rows
    slot_count = seq_count * CAP
    problems = 2 * owned
    group_rows = 16 * pair_rows
    block_bytes = seq_count * pair_rows * width * 2
    block = pl.BlockSpec((seq_count, pair_rows, width), lambda s: (0, s, 0))

    def shaped(rows):
        return jax.ShapeDtypeStruct((seq_count, rows, width), BF16)

    column = pl.BlockSpec((tok_rows, 2 * head_size), lambda s: (0, steps + s))
    second_sent = pl.pallas_call(
        pack_second_kernel,
        grid=(steps,),
        in_specs=[pl.BlockSpec((2, 1, tok_rows), lambda s: (steps + s, 0, 0))] + [column] * 4,
        out_specs=block,
        out_shape=shaped(chunk_rows),
        compiler_params=params(),
        cost_estimate=pl.CostEstimate(
            flops=4 * steps * tok_rows * tok_rows * 640,
            bytes_accessed=2 * steps * block_bytes,
            transcendentals=0,
        ),
        name="pack_second",
    )(base_rows, queries, keys, values, out_grad)

    def own(chunk, fixed, packed, before):
        last = chunk == CHUNKS - 1

        def kernel(*refs):
            own_pair_kernel(chunk * steps, last, *refs)

        over_block = pl.BlockSpec((seq_count, PACKED, width), lambda s: (0, steps, 0))
        whole_block = pl.BlockSpec((seq_count, PACKED, width), lambda s: (0, 0, 0))
        sums_block = pl.BlockSpec((1, problems, head_size), lambda s: (s, 0, 0))
        if last:
            in_specs = [block, over_block, whole_block]
            args = (fixed, packed, before)
            back_rows = chunk_rows + PACKED
            out_specs = [
                pl.BlockSpec((seq_count, back_rows, width), lambda s: (0, 0, 0)),
                sums_block,
            ]
            out_shape = [shaped(back_rows)]
        else:
            in_specs = [block, over_block]
            args = (fixed, packed)
            out_specs = [block, whole_block, sums_block]
            out_shape = [shaped(chunk_rows), shaped(PACKED)]
        out_shape.append(jax.ShapeDtypeStruct((steps, problems, head_size), F32))
        return pl.pallas_call(
            kernel,
            grid=(steps,),
            in_specs=in_specs,
            out_specs=out_specs,
            out_shape=out_shape,
            scratch_shapes=[
                pltpu.VMEM((group_rows, group_rows), BF16),
                pltpu.VMEM((slot_count, slot_count), F32),
                pltpu.VMEM((problems, slot_count, width), BF16),
                pltpu.VMEM((problems, slot_count, width), BF16),
                pltpu.VMEM((seq_count // 16, group_rows, 16 * PACKED), BF16),
            ],
            compiler_params=params(),
            cost_estimate=pl.CostEstimate(
                flops=steps * problems * 7 * 2 * slot_count * slot_count * head_size,
                bytes_accessed=4 * steps * block_bytes,
                transcendentals=steps * problems * slot_count * slot_count,
            ),
            name="own_pair",
        )(*args)

    first = exchange(first_sent)
    second = exchange(second_sent)
    first_back, packed_back, first_sums = own(0, first, first, None)
    first_home = exchange(first_back)
    second_back, second_sums = own(1, second, first, packed_back)
    second_home = exchange(second_back)
    over_block = pl.BlockSpec((seq_count, PACKED, width), lambda s: (0, steps, 0))
    column = pl.BlockSpec((tok_rows, 2 * head_size), lambda s: (0, s))
    routes_block = pl.BlockSpec((tok_rows, heads), lambda s: (0, 0))

    def kernel(*refs):
        unpack_pair_kernel(steps, *refs)

    outs = pl.pallas_call(
        kernel,
        grid=(2 * steps,),
        in_specs=[
            routes_block,
            routes_block,
            pl.BlockSpec(
                (seq_count, pair_rows, width), lambda s: (0, jnp.minimum(s, steps - 1), 0)
            ),
            pl.BlockSpec(
                (seq_count, pair_rows, width), lambda s: (0, jnp.maximum(s - steps, 0), 0)
            ),
            over_block,
        ],
        out_specs=[column] * 4,
        out_shape=[jax.ShapeDtypeStruct((tok_rows, heads * head_size), BF16)] * 4,
        compiler_params=params(),
        cost_estimate=pl.CostEstimate(
            flops=2 * heads * 1536 * tok_rows * width,
            bytes_accessed=8 * steps * block_bytes,
            transcendentals=0,
        ),
        name="unpack_pair",
    )(
        base_rows.reshape(heads, tok_rows).T,
        over_rows.reshape(heads, tok_rows).T,
        first_home,
        second_home,
        second_home,
    )

    sums = [
        half.reshape(2 * steps, owned, head_size) for half in (first_sums, second_sums)
    ]
    homes = []
    for head in range(heads):
        here = sums[head // (2 * steps)][head % (2 * steps)]
        moves = [((at + TURN_BY * head) % seq_count, at) for at in range(seq_count)]
        homes.append(here if head == 0 else lax.ppermute(here, "seq", moves))
    key_sums = jnp.stack(homes)
    blend_sum = DECAY_RATE * centroids + (1.0 - DECAY_RATE) * key_sums
    new_centroids = blend_sum / jnp.sqrt(
        jnp.mean(blend_sum * blend_sum, axis=-1, keepdims=True) + 1e-06
    )
    return (*outs, new_centroids)


def body(queries, keys, values, out_grad, cluster_ids, cluster_slot, centroids):
    seq_count = lax.axis_size("seq")
    heads, tok_rows = cluster_ids.shape[:2]
    cluster_count = cluster_slot.shape[0]
    owned, head_size = centroids.shape[1:]
    width = 4 * head_size
    pair_rows = 2 * owned * FIXED
    steps = heads // 2
    send_rows = steps // CHUNKS * pair_rows + PACKED
    row_shape = jax.ShapeDtypeStruct((heads, 1, tok_rows), jnp.int32)
    base_rows, over_rows, tag_rows, peak = pl.pallas_call(
        route_kernel,
        out_shape=[row_shape] * 3 + [jax.ShapeDtypeStruct((8, 128), jnp.int32)],
        compiler_params=params(),
        name="route",
    )(cluster_ids.reshape(heads, 1, tok_rows), cluster_slot.reshape(1, cluster_count))
    most = lax.pmax(peak[0, 0], ("seq", "head"))
    row_block = pl.BlockSpec((2, 1, tok_rows), lambda s: (s, 0, 0))
    column = pl.BlockSpec((tok_rows, 2 * head_size), lambda s: (0, s))
    first_sent = pl.pallas_call(
        pack_first_kernel,
        grid=(steps,),
        in_specs=[row_block] * 3 + [column] * 4,
        out_specs=pl.BlockSpec((seq_count, send_rows, width), lambda s: (0, 0, 0)),
        out_shape=jax.ShapeDtypeStruct((seq_count, send_rows, width), BF16),
        scratch_shapes=[
            pltpu.VMEM((seq_count * PACKED, width), F32),
            pltpu.VMEM((seq_count, head_size), F32),
        ],
        compiler_params=params(),
        cost_estimate=pl.CostEstimate(
            flops=2 * heads * 1536 * tok_rows * width,
            bytes_accessed=seq_count * send_rows * width * 4,
            transcendentals=0,
        ),
        name="pack_first",
    )(base_rows, over_rows, tag_rows, queries, keys, values, out_grad)

    def small(args):
        q, k, v, g, routes, sent, _, _, cent = args
        return adaptive(q, k, v, g, routes, sent, cent)

    def large(args):
        q, k, v, g, _, _, ids, slots, cent = args
        return dense(q, k, v, g, ids, slots, cent)

    return lax.cond(
        most < PACKED,
        small,
        large,
        (
            queries,
            keys,
            values,
            out_grad,
            (base_rows, over_rows),
            first_sent,
            cluster_ids,
            cluster_slot,
            centroids,
        ),
    )


def solution(mesh):
    return jax.shard_map(
        body,
        mesh=mesh,
        in_specs=(
            P("seq", "head"),
            P("seq", "head"),
            P("seq", "head"),
            P("seq", "head"),
            P("head", "seq", None),
            P(),
            P("head", "seq", None),
        ),
        out_specs=(
            P("seq", "head"),
            P("seq", "head"),
            P("seq", "head"),
            P("seq", "head"),
            P("head", "seq", None),
        ),
        check_vma=False,
    )
```

```python
import math

import jax
import jax.numpy as jnp
from jax import lax
from jax.experimental import pallas as pl
from jax.experimental.pallas import tpu as pltpu
from jax.sharding import PartitionSpec as P

CAP = 4
DECAY_RATE = 0.9
MASKED = -1e30
ABSENT = 64.0
CHUNKS = 2
SHARED = 8
PACKED = 16
PEAK_LANE = 127
TURN_BY = 8
VMEM_BYTES = 60 * 1024 * 1024

F32 = jnp.float32
BF16 = jnp.bfloat16
CONTRACT_LAST = (((1,), (1,)), ((), ()))
CONTRACT_FIRST = (((0,), (0,)), ((), ()))


def iota(shape, dim):
    return lax.broadcasted_iota(jnp.int32, shape, dim)


def dot(left, right):
    return jnp.dot(left, right, preferred_element_type=F32)


def pack_kernel(ids_ref, slot_ref, q_ref, k_ref, v_ref, g_ref, send_ref, flat_ref, earlier_ref):
    tok_rows = ids_ref.shape[2]
    cluster_count = slot_ref.shape[1]
    slot_rows = cluster_count * CAP

    @pl.when(pl.program_id(0) == 0)
    def _():
        earlier_ref[...] = (iota((tok_rows, tok_rows), 0) < iota((tok_rows, tok_rows), 1)).astype(
            F32
        ).astype(BF16)

    ids_row = ids_ref[0]
    member = iota((cluster_count, tok_rows), 0) == ids_row
    member_f = jnp.where(member, 1.0, 0.0)
    member_low = member_f.astype(BF16)
    slots_low = jnp.broadcast_to(slot_ref[...].astype(F32), (8, cluster_count)).astype(BF16)
    slot_row = dot(slots_low, member_low)[0:1]
    rank_row = jnp.sum(dot(member_low, earlier_ref[...]) * member_f, axis=0, keepdims=True)
    flat_row = (slot_row * CAP + rank_row).astype(jnp.int32)
    flat_ref[0] = flat_row
    place = jnp.where(iota((slot_rows, tok_rows), 0) == flat_row, 1.0, 0.0).astype(BF16)
    ones = jnp.ones((tok_rows, 128), BF16)
    head_size = q_ref.shape[1]
    taken = dot(place, ones)
    out_shape = send_ref.shape[:2] + (head_size,)

    def put(at, rows):
        send_ref[:, :, at * head_size : (at + 1) * head_size] = rows.astype(BF16).reshape(out_shape)

    put(0, dot(place, q_ref[...]))
    put(1, dot(place, k_ref[...]) + (1.0 - taken) * ABSENT)
    put(2, dot(place, v_ref[...]))
    put(3, dot(place, g_ref[...]))


def owner_kernel(recv_ref, cent_ref, back_ref, new_ref, turn_ref, causal_ref, rows_ref, grads_ref):
    source_count, block_rows, width = recv_ref.shape
    head_size = width // 4
    owned = block_rows // CAP
    slot_count = source_count * CAP
    group_rows = 16 * block_rows
    groups = source_count // 16
    part = 16 * CAP
    score_scale = 1.0 / math.sqrt(head_size)

    @pl.when(pl.program_id(0) == 0)
    def _():
        row_at = iota((group_rows, group_rows), 0)
        col_at = iota((group_rows, group_rows), 1)
        cluster_of = row_at // part
        source_of = (row_at % part) // CAP
        from_row = source_of * block_rows + cluster_of * CAP + row_at % CAP
        turn_ref[...] = jnp.where(from_row == col_at, 1.0, 0.0).astype(BF16)
        causal_ref[...] = jnp.where(
            iota((slot_count, slot_count), 1) <= iota((slot_count, slot_count), 0), 0.0, MASKED
        )

    turn = turn_ref[...]
    for group in range(groups):
        arrived = recv_ref[group * 16 : (group + 1) * 16].reshape(group_rows, width)
        turned = dot(turn, arrived).astype(BF16)
        rows_ref[:, group * part : (group + 1) * part, :] = turned.reshape(owned, part, width)

    first_lane = jnp.where(iota((8, head_size), 1) == 0, 1.0, 0.0).astype(BF16)
    for cluster in range(owned):
        q = rows_ref[cluster, :, 0:head_size]
        k = rows_ref[cluster, :, head_size : 2 * head_size]
        v = rows_ref[cluster, :, 2 * head_size : 3 * head_size]
        g = rows_ref[cluster, :, 3 * head_size : 4 * head_size]
        marks = lax.dot_general(first_lane, k, CONTRACT_LAST, preferred_element_type=F32)
        present = marks < ABSENT / 2
        bias = jnp.where(present, 0.0, MASKED)[0:1]
        scores = lax.dot_general(q, k, CONTRACT_LAST, preferred_element_type=F32) * score_scale
        scores = scores + (causal_ref[...] + bias)
        weights = jnp.exp(scores - jnp.max(scores, axis=-1, keepdims=True))
        probs = weights / jnp.sum(weights, axis=-1, keepdims=True)
        probs_low = probs.astype(BF16)
        out = dot(probs_low, v).astype(BF16)
        grad_prob = lax.dot_general(g, v, CONTRACT_LAST, preferred_element_type=F32)
        delta = jnp.sum(g.astype(F32) * out.astype(F32), axis=-1, keepdims=True)
        grad_score = (probs * (grad_prob - delta) * score_scale).astype(BF16)
        grad_q = dot(grad_score, k)
        grad_k = lax.dot_general(grad_score, q, CONTRACT_FIRST, preferred_element_type=F32)
        grad_v = lax.dot_general(probs_low, g, CONTRACT_FIRST, preferred_element_type=F32)
        grads_ref[cluster, :, 0:head_size] = out
        grads_ref[cluster, :, head_size : 2 * head_size] = grad_q.astype(BF16)
        grads_ref[cluster, :, 2 * head_size : 3 * head_size] = grad_k.astype(BF16)
        grads_ref[cluster, :, 3 * head_size : 4 * head_size] = grad_v.astype(BF16)
        key_sums = dot(jnp.where(present, 1.0, 0.0).astype(BF16), k)[0:1]
        blend = DECAY_RATE * cent_ref[0, cluster : cluster + 1, :] + (1.0 - DECAY_RATE) * key_sums
        new_ref[0, cluster : cluster + 1, :] = blend / jnp.sqrt(
            jnp.mean(blend * blend, axis=-1, keepdims=True) + 1e-06
        )

    for group in range(groups):
        leaving = grads_ref[:, group * part : (group + 1) * part, :].reshape(group_rows, width)
        turned = lax.dot_general(turn, leaving, CONTRACT_FIRST, preferred_element_type=F32)
        back_ref[group * 16 : (group + 1) * 16] = turned.astype(BF16).reshape(
            16, block_rows, width
        )


def unpack_kernel(chunk, flat_ref, ret_ref, *refs):
    out_refs = refs[-4:]
    sources, block_rows, width = ret_ref.shape
    head_size = width // 4
    tok_rows, heads = flat_ref.shape
    slot_rows = sources * block_rows
    here = iota((tok_rows, heads), 1) == pl.program_id(0)
    flat_col = jnp.sum(jnp.where(here, flat_ref[...], 0), axis=1, keepdims=True)
    take = jnp.where(iota((tok_rows, slot_rows), 1) == flat_col, 1.0, 0.0).astype(BF16)
    rows = dot(take, ret_ref[...].reshape(slot_rows, width)).astype(BF16)
    for at, out_ref in enumerate(out_refs):
        out_ref[...] = rows[:, at * head_size : (at + 1) * head_size]


def route_kernel(ids_ref, slot_ref, base_ref, over_ref, header_ref):
    heads, _, tok_rows = ids_ref.shape
    cluster_count = slot_ref.shape[1]
    owners, lanes = header_ref.shape
    earlier = jnp.where(
        iota((tok_rows, tok_rows), 0) < iota((tok_rows, tok_rows), 1), 1.0, 0.0
    ).astype(BF16)
    slots_low = jnp.broadcast_to(slot_ref[...].astype(F32), (8, cluster_count)).astype(BF16)
    filled = jnp.zeros((owners, 1), F32)
    header = jnp.zeros((owners, lanes), F32)
    for head in range(heads):
        member_f = jnp.where(iota((cluster_count, tok_rows), 0) == ids_ref[head], 1.0, 0.0)
        member_low = member_f.astype(BF16)
        slot = dot(slots_low, member_low)[0:1].astype(jnp.int32)
        rank = jnp.sum(dot(member_low, earlier) * member_f, axis=0, keepdims=True)
        owner = (slot // CAP + TURN_BY * head) % owners
        tag = (head * CAP + slot % CAP) * CAP + rank.astype(jnp.int32)
        here = iota((owners, tok_rows), 0) == owner
        here_f = jnp.where(here, 1.0, 0.0)
        before = dot(here_f.astype(BF16), earlier)
        place = jnp.sum(before * here_f, axis=0, keepdims=True).astype(jnp.int32)
        late = jnp.sum((before + filled) * here_f, axis=0, keepdims=True)
        late = late.astype(jnp.int32) - SHARED
        filled = filled + jnp.maximum(jnp.sum(here_f, axis=1, keepdims=True) - SHARED, 0.0)
        fits = place < SHARED
        packs = (late < PACKED - 1) & (place >= SHARED)
        base_ref[head] = jnp.where(fits, owner * SHARED + place, -1)
        over_ref[head] = jnp.where(packs, owner * PACKED + late, -1)
        lane = jnp.where(fits, head * SHARED + place, jnp.where(packs, heads * SHARED + late, -1))
        named = jnp.where(here, tag + 1, 0).astype(F32).astype(BF16)
        lane_at = jnp.where(iota((lanes, tok_rows), 0) == lane, 1.0, 0.0).astype(BF16)
        header = header + lax.dot_general(
            named, lane_at, CONTRACT_LAST, preferred_element_type=F32
        )
    peak = jnp.max(filled, axis=0, keepdims=True)
    header_ref[...] = jnp.where(iota((owners, lanes), 1) == PEAK_LANE, peak, header).astype(BF16)


def token_rows(refs, at, head_size):
    lanes = slice(at * head_size, (at + 1) * head_size)
    return jnp.concatenate([ref[:, lanes] for ref in refs], axis=1)


def shared_rows(base_ref, rows, owners):
    tok_rows, width = rows[0].shape
    halves = []
    for at in range(2):
        place = iota((owners * SHARED, tok_rows), 0) == base_ref[at]
        placed = dot(jnp.where(place, 1.0, 0.0).astype(BF16), rows[at])
        halves.append(placed.reshape(owners, SHARED, width))
    return jnp.concatenate(halves, axis=1).astype(BF16)


def pack_first_kernel(
    base_ref, over_ref, header_ref, q_ref, k_ref, v_ref, g_ref, send_ref, total_ref
):
    owners, send_rows, width = send_ref.shape
    tok_rows = q_ref.shape[0]
    head_size = width // 4
    step = pl.program_id(0)
    rows = [token_rows((q_ref, k_ref, v_ref, g_ref), at, head_size) for at in range(2)]
    places = [
        jnp.where(iota((owners * PACKED, tok_rows), 0) == over_ref[at], 1.0, 0.0).astype(BF16)
        for at in range(2)
    ]
    added = dot(jnp.concatenate(places, axis=1), jnp.concatenate(rows, axis=0))

    @pl.when(step == 0)
    def _():
        total_ref[...] = added

    @pl.when(step > 0)
    def _():
        total_ref[...] += added

    @pl.when(step < pl.num_programs(0) // CHUNKS)
    def _():
        at_row = pl.multiple_of(step * 2 * SHARED, 2 * SHARED)
        send_ref[:, pl.ds(at_row, 2 * SHARED), :] = shared_rows(base_ref, rows, owners)

    @pl.when(step == pl.num_programs(0) - 1)
    def _():
        last_row = iota((owners * PACKED, owners), 1) * PACKED + PACKED - 1
        to_last = jnp.where(iota((owners * PACKED, owners), 0) == last_row, 1.0, 0.0)
        total_ref[:, :head_size] += dot(to_last.astype(BF16), header_ref[...])
        packed = total_ref[...].astype(BF16).reshape(owners, PACKED, width)
        send_ref[:, send_rows - PACKED :, :] = packed


def pack_second_kernel(base_ref, q_ref, k_ref, v_ref, g_ref, send_ref):
    owners, _, width = send_ref.shape
    rows = [token_rows((q_ref, k_ref, v_ref, g_ref), at, width // 4) for at in range(2)]
    send_ref[...] = shared_rows(base_ref, rows, owners)


def own_pair_kernel(first_step, last, *refs):
    shared_ref, over_ref = refs[:2]
    if last:
        before_ref, back_ref, sums_ref = refs[2:5]
        turn_ref, causal_ref, rows_ref, grads_ref = refs[5:]
    else:
        back_ref, over_back_ref, sums_ref, peak_ref = refs[2:6]
        turn_ref, causal_ref, rows_ref, grads_ref = refs[6:]
    sources, pair_rows, width = shared_ref.shape
    head_size = width // 4
    problems = rows_ref.shape[0]
    slot_count = sources * CAP
    bunch = 16
    groups = sources // bunch
    part = bunch * CAP
    shared_count = bunch * pair_rows
    packed_count = bunch * PACKED
    score_scale = 1.0 / math.sqrt(head_size)
    step = pl.program_id(0)

    @pl.when(step == 0)
    def _():
        at = iota((slot_count, slot_count), 0)
        causal_ref[...] = jnp.where(iota((slot_count, slot_count), 1) <= at, 0.0, MASKED)

    header_of = jnp.where(
        iota((bunch, packed_count), 1) == iota((bunch, packed_count), 0) * PACKED + PACKED - 1,
        1.0,
        0.0,
    ).astype(BF16)

    def turns(header, first_lane, rows_each, used):
        count = bunch * rows_each
        lane = iota((head_size, count), 1) % rows_each
        match = (iota((head_size, count), 0) == lane + first_lane) & (lane < used)
        tags = dot(header, jnp.where(match, 1.0, 0.0).astype(BF16))
        source = iota((1, count), 1) // rows_each
        own = iota((bunch, count), 0) == source
        tag = jnp.sum(jnp.where(own, tags, 0.0), axis=0, keepdims=True).astype(jnp.int32) - 1
        mine = (tag >= 0) & (tag // (problems * CAP) == first_step + step)
        problem = (tag // CAP) % problems
        slot = jnp.where(mine, problem * part + source * CAP + tag % CAP, -1)
        hit = iota((problems * part, count), 0) == slot
        return jnp.where(hit, 1.0, 0.0).astype(BF16)

    ones = jnp.ones((shared_count + packed_count, head_size), BF16)
    heads_shared = 4 * CHUNKS * SHARED
    peak = jnp.zeros((1, 1), F32)
    for group in range(groups):
        from_sources = slice(group * bunch, (group + 1) * bunch)
        packed = over_ref[from_sources].reshape(packed_count, width)
        shared = shared_ref[from_sources].reshape(shared_count, width)
        header = dot(header_of, packed[:, :head_size])
        peak = jnp.maximum(peak, jnp.max(header[:, PEAK_LANE:], axis=0, keepdims=True))
        header = header.astype(BF16)
        turn = jnp.concatenate(
            [
                turns(header, (first_step + step) * pair_rows, pair_rows, pair_rows),
                turns(header, heads_shared, PACKED, PACKED - 1),
            ],
            axis=1,
        )
        turn_ref[group] = turn
        turned = dot(turn, jnp.concatenate([shared, packed], axis=0))
        marked = turned[:, head_size : 2 * head_size] + (1.0 - dot(turn, ones)) * ABSENT
        turned = jnp.concatenate(
            [turned[:, :head_size], marked, turned[:, 2 * head_size :]], axis=1
        )
        rows_ref[:, group * part : (group + 1) * part, :] = turned.astype(BF16).reshape(
            problems, part, width
        )
    if not last:
        peak_ref[...] = jnp.broadcast_to(peak, peak_ref.shape)

    first_lane = jnp.where(iota((8, head_size), 1) == 0, 1.0, 0.0).astype(BF16)

    def attend(problem):
        q = rows_ref[problem, :, 0:head_size]
        k = rows_ref[problem, :, head_size : 2 * head_size]
        v = rows_ref[problem, :, 2 * head_size : 3 * head_size]
        g = rows_ref[problem, :, 3 * head_size : 4 * head_size]
        marks = lax.dot_general(first_lane, k, CONTRACT_LAST, preferred_element_type=F32)
        present = marks < ABSENT / 2
        bias = jnp.where(present, 0.0, MASKED)[0:1]
        scores = lax.dot_general(q, k, CONTRACT_LAST, preferred_element_type=F32) * score_scale
        scores = scores + (causal_ref[...] + bias)
        weights = jnp.exp(scores - jnp.max(scores, axis=-1, keepdims=True))
        probs = weights / jnp.sum(weights, axis=-1, keepdims=True)
        probs_low = probs.astype(BF16)
        out = dot(probs_low, v).astype(BF16)
        grad_prob = lax.dot_general(g, v, CONTRACT_LAST, preferred_element_type=F32)
        delta = jnp.sum(g.astype(F32) * out.astype(F32), axis=-1, keepdims=True)
        grad_score = (probs * (grad_prob - delta) * score_scale).astype(BF16)
        grad_q = dot(grad_score, k)
        grad_k = lax.dot_general(grad_score, q, CONTRACT_FIRST, preferred_element_type=F32)
        grad_v = lax.dot_general(probs_low, g, CONTRACT_FIRST, preferred_element_type=F32)
        grads_ref[problem, :, 0:head_size] = out
        grads_ref[problem, :, head_size : 2 * head_size] = grad_q.astype(BF16)
        grads_ref[problem, :, 2 * head_size : 3 * head_size] = grad_k.astype(BF16)
        grads_ref[problem, :, 3 * head_size : 4 * head_size] = grad_v.astype(BF16)
        sums = dot(jnp.where(present, 1.0, 0.0).astype(BF16), k)[0:1]
        sums_ref[0, pl.ds(problem, 1), :] = sums

    @pl.loop(0, problems // 2)
    def _(pair):
        attend(pair * 2)
        attend(pair * 2 + 1)

    for group in range(groups):
        from_sources = slice(group * bunch, (group + 1) * bunch)
        leaving = grads_ref[:, group * part : (group + 1) * part, :].reshape(
            problems * part, width
        )
        sent = lax.dot_general(
            turn_ref[group], leaving, CONTRACT_FIRST, preferred_element_type=F32
        ).astype(BF16)
        shared = sent[:shared_count].reshape(bunch, pair_rows, width)
        packed = sent[shared_count:].reshape(bunch, PACKED, width)
        if last:
            at_row = pl.multiple_of(step * pair_rows, pair_rows)
            back_ref[from_sources, pl.ds(at_row, pair_rows), :] = shared
            rest = slice(back_ref.shape[1] - PACKED, back_ref.shape[1])

            @pl.when(step == 0)
            def _():
                back_ref[from_sources, rest, :] = before_ref[from_sources] + packed

            @pl.when(step > 0)
            def _():
                back_ref[from_sources, rest, :] += packed
        else:
            back_ref[from_sources] = shared

            @pl.when(step == 0)
            def _():
                over_back_ref[from_sources] = packed

            @pl.when(step > 0)
            def _():
                over_back_ref[from_sources] += packed


def unpack_pair_kernel(steps, base_ref, over_ref, first_ref, second_ref, packed_ref, *out_refs):
    owners, _, width = first_ref.shape
    head_size = width // 4
    tok_rows, heads = base_ref.shape
    step = pl.program_id(0)
    packed = packed_ref[...].reshape(owners * PACKED, width)
    arrived = jnp.where(step < steps, first_ref[...], second_ref[...]).astype(F32)
    for at in range(2):
        here = iota((tok_rows, heads), 1) == step * 2 + at
        base = jnp.sum(jnp.where(here, base_ref[...], 0), axis=1, keepdims=True)
        over = jnp.sum(jnp.where(here, over_ref[...], 0), axis=1, keepdims=True)
        take = iota((tok_rows, owners * SHARED), 1) == base
        take_over = iota((tok_rows, owners * PACKED), 1) == over
        mine = arrived[:, at * SHARED : (at + 1) * SHARED, :].reshape(owners * SHARED, width)
        rows = dot(jnp.where(take, 1.0, 0.0).astype(BF16), mine.astype(BF16))
        rows = rows + dot(jnp.where(take_over, 1.0, 0.0).astype(BF16), packed)
        rows = rows.astype(BF16)
        for which, out_ref in enumerate(out_refs):
            out_ref[:, at * head_size : (at + 1) * head_size] = rows[
                :, which * head_size : (which + 1) * head_size
            ]


def params():
    return pltpu.CompilerParams(vmem_limit_bytes=VMEM_BYTES)


def dense(queries, keys, values, out_grad, cluster_ids, cluster_slot, centroids):
    seq_count = lax.axis_size("seq")
    local_heads, tok_rows = cluster_ids.shape[:2]
    cluster_count = cluster_slot.shape[0]
    owned = cluster_count // seq_count
    head_size = centroids.shape[2]
    heads = local_heads // CHUNKS
    block_rows = owned * CAP
    width = 4 * head_size
    slot_count = seq_count * CAP
    sent = jax.ShapeDtypeStruct((seq_count, heads * block_rows, width), BF16)
    sent_bytes = seq_count * heads * block_rows * width * 2
    ids_rows = cluster_ids.reshape(local_heads, 1, tok_rows)
    slot_row = cluster_slot.reshape(1, cluster_count)
    block = pl.BlockSpec((seq_count, block_rows, width), lambda h: (0, h, 0))

    def exchange(rows):
        return lax.all_to_all(rows, "seq", split_axis=0, concat_axis=0, tiled=True)

    def pack(chunk):
        column = pl.BlockSpec((tok_rows, head_size), lambda h: (0, chunk * heads + h))
        return pl.pallas_call(
            pack_kernel,
            grid=(heads,),
            in_specs=[
                pl.BlockSpec((1, 1, tok_rows), lambda h: (chunk * heads + h, 0, 0)),
                pl.BlockSpec((1, cluster_count), lambda h: (0, 0)),
                column,
                column,
                column,
                column,
            ],
            out_specs=[block, pl.BlockSpec((1, 1, tok_rows), lambda h: (h, 0, 0))],
            out_shape=[sent, jax.ShapeDtypeStruct((heads, 1, tok_rows), jnp.int32)],
            scratch_shapes=[pltpu.VMEM((tok_rows, tok_rows), BF16)],
            compiler_params=params(),
            cost_estimate=pl.CostEstimate(
                flops=heads * 2 * 1024 * 512 * 640, bytes_accessed=2 * sent_bytes, transcendentals=0
            ),
            name="pack",
        )(ids_rows, slot_row, queries, keys, values, out_grad)

    def own(chunk, received):
        return pl.pallas_call(
            owner_kernel,
            grid=(heads,),
            in_specs=[
                block,
                pl.BlockSpec((1, owned, head_size), lambda h: (chunk * heads + h, 0, 0)),
            ],
            out_specs=[block, pl.BlockSpec((1, owned, head_size), lambda h: (h, 0, 0))],
            out_shape=[sent, jax.ShapeDtypeStruct((heads, owned, head_size), F32)],
            scratch_shapes=[
                pltpu.VMEM((16 * block_rows, 16 * block_rows), BF16),
                pltpu.VMEM((slot_count, slot_count), F32),
                pltpu.VMEM((owned, slot_count, width), BF16),
                pltpu.VMEM((owned, slot_count, width), BF16),
            ],
            compiler_params=params(),
            cost_estimate=pl.CostEstimate(
                flops=heads * owned * 7 * 2 * slot_count * slot_count * head_size,
                bytes_accessed=2 * sent_bytes,
                transcendentals=heads * owned * slot_count * slot_count,
            ),
            name="own",
        )(received, centroids)

    def unpack(chunk, flat_cols, returned, previous):
        column = pl.BlockSpec((tok_rows, head_size), lambda h: (0, chunk * heads + h))
        whole = jax.ShapeDtypeStruct((tok_rows, local_heads * head_size), BF16)

        def kernel(*refs):
            unpack_kernel(chunk, *refs)

        return pl.pallas_call(
            kernel,
            grid=(heads,),
            in_specs=[pl.BlockSpec((tok_rows, heads), lambda h: (0, 0)), block]
            + [pl.BlockSpec(memory_space=pl.ANY)] * len(previous),
            out_specs=[column] * 4,
            out_shape=[whole] * 4,
            input_output_aliases={2 + i: i for i in range(len(previous))},
            compiler_params=params(),
            cost_estimate=pl.CostEstimate(
                flops=heads * 2 * 1024 * 512 * 512, bytes_accessed=2 * sent_bytes, transcendentals=0
            ),
            name="unpack",
        )(flat_cols, returned, *previous)

    packed = [pack(chunk) for chunk in range(CHUNKS)]
    received = [exchange(rows) for rows, _ in packed]
    owned_now = [own(chunk, rows) for chunk, rows in enumerate(received)]
    returned = [exchange(rows) for rows, _ in owned_now]
    outs = ()
    for chunk in range(CHUNKS):
        flat_cols = packed[chunk][1].reshape(heads, tok_rows).T
        outs = unpack(chunk, flat_cols, returned[chunk], tuple(outs))
    new_centroids = jnp.concatenate([new for _, new in owned_now], axis=0)
    return (*outs, new_centroids)


def exchange(rows):
    return lax.all_to_all(rows, "seq", split_axis=0, concat_axis=0, tiled=True)


def body(queries, keys, values, out_grad, cluster_ids, cluster_slot, centroids):
    seq_count = lax.axis_size("seq")
    heads, tok_rows = cluster_ids.shape[:2]
    cluster_count = cluster_slot.shape[0]
    owned, head_size = centroids.shape[1:]
    width = 4 * head_size
    pair_rows = 2 * SHARED
    steps = heads // 2 // CHUNKS
    chunk_rows = steps * pair_rows
    send_rows = chunk_rows + PACKED
    slot_count = seq_count * CAP
    problems = 2 * owned
    block_bytes = seq_count * pair_rows * width * 2

    def shaped(rows):
        return jax.ShapeDtypeStruct((seq_count, rows, width), BF16)

    def cost(flops, blocks, exps=0):
        return pl.CostEstimate(
            flops=flops, bytes_accessed=blocks * block_bytes, transcendentals=exps
        )

    block = pl.BlockSpec((seq_count, pair_rows, width), lambda s: (0, s, 0))
    over_block = pl.BlockSpec((seq_count, PACKED, width), lambda s: (0, steps, 0))
    whole_block = pl.BlockSpec((seq_count, PACKED, width), lambda s: (0, 0, 0))
    column = pl.BlockSpec((tok_rows, 2 * head_size), lambda s: (0, s))
    second_column = pl.BlockSpec((tok_rows, 2 * head_size), lambda s: (0, steps + s))
    row_block = pl.BlockSpec((2, 1, tok_rows), lambda s: (s, 0, 0))
    second_row_block = pl.BlockSpec((2, 1, tok_rows), lambda s: (steps + s, 0, 0))
    sent_whole = pl.BlockSpec((seq_count, send_rows, width), lambda s: (0, 0, 0))

    base_rows, over_rows, header = pl.pallas_call(
        route_kernel,
        out_shape=[jax.ShapeDtypeStruct((heads, 1, tok_rows), jnp.int32)] * 2
        + [jax.ShapeDtypeStruct((seq_count, head_size), BF16)],
        compiler_params=params(),
        name="route",
    )(cluster_ids.reshape(heads, 1, tok_rows), cluster_slot.reshape(1, cluster_count))
    first_sent = pl.pallas_call(
        pack_first_kernel,
        grid=(CHUNKS * steps,),
        in_specs=[row_block] * 2
        + [pl.BlockSpec((seq_count, head_size), lambda s: (0, 0))]
        + [column] * 4,
        out_specs=sent_whole,
        out_shape=shaped(send_rows),
        scratch_shapes=[pltpu.VMEM((seq_count * PACKED, width), F32)],
        compiler_params=params(),
        cost_estimate=cost(2 * heads * 1280 * tok_rows * width, 9),
        name="pack_first",
    )(base_rows, over_rows, header, queries, keys, values, out_grad)
    second_sent = pl.pallas_call(
        pack_second_kernel,
        grid=(steps,),
        in_specs=[second_row_block] + [second_column] * 4,
        out_specs=block,
        out_shape=shaped(chunk_rows),
        compiler_params=params(),
        cost_estimate=cost(4 * steps * tok_rows * tok_rows * width, 2 * steps),
        name="pack_second",
    )(base_rows, queries, keys, values, out_grad)

    def own(chunk, *args):
        last = chunk == CHUNKS - 1

        def kernel(*refs):
            own_pair_kernel(chunk * steps, last, *refs)

        sums_block = pl.BlockSpec((1, problems, head_size), lambda s: (s, 0, 0))
        sums_shape = jax.ShapeDtypeStruct((steps, problems, head_size), F32)
        if last:
            in_specs = [block, over_block, whole_block]
            out_specs = [sent_whole, sums_block]
            out_shape = [shaped(send_rows), sums_shape]
        else:
            in_specs = [block, over_block]
            peak_block = pl.BlockSpec((8, 128), lambda s: (0, 0))
            out_specs = [block, whole_block, sums_block, peak_block]
            out_shape = [shaped(chunk_rows), shaped(PACKED), sums_shape]
            out_shape.append(jax.ShapeDtypeStruct((8, 128), F32))
        return pl.pallas_call(
            kernel,
            grid=(steps,),
            in_specs=in_specs,
            out_specs=out_specs,
            out_shape=out_shape,
            scratch_shapes=[
                pltpu.VMEM(
                    (seq_count // 16, problems * 16 * CAP, 16 * (pair_rows + PACKED)), BF16
                ),
                pltpu.VMEM((slot_count, slot_count), F32),
                pltpu.VMEM((problems, slot_count, width), BF16),
                pltpu.VMEM((problems, slot_count, width), BF16),
            ],
            compiler_params=params(),
            cost_estimate=cost(
                steps * problems * 16 * 2 * slot_count * slot_count * head_size,
                4 * steps,
                steps * problems * slot_count * slot_count,
            ),
            name="own_pair",
        )(*args)

    first = exchange(first_sent)
    second = exchange(second_sent)
    first_back, packed_back, first_sums, peak = own(0, first, first)
    first_home = exchange(first_back)
    second_back, second_sums = own(1, second, first, packed_back)
    second_home = exchange(second_back)
    swap = [(at, 1 - at) for at in range(2)]
    peak = peak[0:1]
    peak = jnp.maximum(peak, lax.ppermute(peak, "head", swap))[0, 0]

    sums = [half.reshape(2 * steps, owned, head_size) for half in (first_sums, second_sums)]
    homes = []
    for head in range(heads):
        here = sums[head // (2 * steps)][head % (2 * steps)]
        moves = [((at + TURN_BY * head) % seq_count, at) for at in range(seq_count)]
        homes.append(here if head == 0 else lax.ppermute(here, "seq", moves))
    blend_sum = DECAY_RATE * centroids + (1.0 - DECAY_RATE) * jnp.stack(homes)
    new_centroids = blend_sum / jnp.sqrt(
        jnp.mean(blend_sum * blend_sum, axis=-1, keepdims=True) + 1e-06
    )

    def unpack(operands):
        _, (base_cols, over_cols, home_one, home_two, centroids_now) = operands

        def kernel(*refs):
            unpack_pair_kernel(steps, *refs)

        routes_block = pl.BlockSpec((tok_rows, heads), lambda s: (0, 0))
        outs = pl.pallas_call(
            kernel,
            grid=(CHUNKS * steps,),
            in_specs=[
                routes_block,
                routes_block,
                pl.BlockSpec(
                    (seq_count, pair_rows, width), lambda s: (0, jnp.minimum(s, steps - 1), 0)
                ),
                pl.BlockSpec(
                    (seq_count, pair_rows, width), lambda s: (0, jnp.maximum(s - steps, 0), 0)
                ),
                over_block,
            ],
            out_specs=[column] * 4,
            out_shape=[jax.ShapeDtypeStruct((tok_rows, heads * head_size), BF16)] * 4,
            compiler_params=params(),
            cost_estimate=cost(2 * heads * 1536 * tok_rows * width, 9),
            name="unpack_pair",
        )(base_cols, over_cols, home_one, home_two, home_two)
        return (*outs, centroids_now)

    def again(operands):
        return dense(*operands[0])

    return lax.cond(
        peak < PACKED,
        unpack,
        again,
        (
            (queries, keys, values, out_grad, cluster_ids, cluster_slot, centroids),
            (
                base_rows.reshape(heads, tok_rows).T,
                over_rows.reshape(heads, tok_rows).T,
                first_home,
                second_home,
                new_centroids,
            ),
        ),
    )


def solution(mesh):
    return jax.shard_map(
        body,
        mesh=mesh,
        in_specs=(
            P("seq", "head"),
            P("seq", "head"),
            P("seq", "head"),
            P("seq", "head"),
            P("head", "seq", None),
            P(),
            P("head", "seq", None),
        ),
        out_specs=(
            P("seq", "head"),
            P("seq", "head"),
            P("seq", "head"),
            P("seq", "head"),
            P("head", "seq", None),
        ),
        check_vma=False,
    )
```

```python
import math

import jax
import jax.numpy as jnp
from jax import lax
from jax.experimental import pallas as pl
from jax.experimental.pallas import tpu as pltpu
from jax.sharding import PartitionSpec as P

CAP = 4
DECAY_RATE = 0.9
MASKED = -1e30
ABSENT = 64.0
CHUNKS = 2
SHARED = 8
PACKED = 32
PEAK_LANE = 127
TURN_BY = 8
VMEM_BYTES = 60 * 1024 * 1024

F32 = jnp.float32
BF16 = jnp.bfloat16
CONTRACT_LAST = (((1,), (1,)), ((), ()))
CONTRACT_FIRST = (((0,), (0,)), ((), ()))


def iota(shape, dim):
    return lax.broadcasted_iota(jnp.int32, shape, dim)


def dot(left, right):
    return jnp.dot(left, right, preferred_element_type=F32)


def pack_kernel(ids_ref, slot_ref, q_ref, k_ref, v_ref, g_ref, send_ref, flat_ref, earlier_ref):
    tok_rows = ids_ref.shape[2]
    cluster_count = slot_ref.shape[1]
    slot_rows = cluster_count * CAP

    @pl.when(pl.program_id(0) == 0)
    def _():
        earlier_ref[...] = (iota((tok_rows, tok_rows), 0) < iota((tok_rows, tok_rows), 1)).astype(
            F32
        ).astype(BF16)

    ids_row = ids_ref[0]
    member = iota((cluster_count, tok_rows), 0) == ids_row
    member_f = jnp.where(member, 1.0, 0.0)
    member_low = member_f.astype(BF16)
    slots_low = jnp.broadcast_to(slot_ref[...].astype(F32), (8, cluster_count)).astype(BF16)
    slot_row = dot(slots_low, member_low)[0:1]
    rank_row = jnp.sum(dot(member_low, earlier_ref[...]) * member_f, axis=0, keepdims=True)
    flat_row = (slot_row * CAP + rank_row).astype(jnp.int32)
    flat_ref[0] = flat_row
    place = jnp.where(iota((slot_rows, tok_rows), 0) == flat_row, 1.0, 0.0).astype(BF16)
    ones = jnp.ones((tok_rows, 128), BF16)
    head_size = q_ref.shape[1]
    taken = dot(place, ones)
    out_shape = send_ref.shape[:2] + (head_size,)

    def put(at, rows):
        send_ref[:, :, at * head_size : (at + 1) * head_size] = rows.astype(BF16).reshape(out_shape)

    put(0, dot(place, q_ref[...]))
    put(1, dot(place, k_ref[...]) + (1.0 - taken) * ABSENT)
    put(2, dot(place, v_ref[...]))
    put(3, dot(place, g_ref[...]))


def owner_kernel(recv_ref, cent_ref, back_ref, new_ref, turn_ref, causal_ref, rows_ref, grads_ref):
    source_count, block_rows, width = recv_ref.shape
    head_size = width // 4
    owned = block_rows // CAP
    slot_count = source_count * CAP
    group_rows = 16 * block_rows
    groups = source_count // 16
    part = 16 * CAP
    score_scale = 1.0 / math.sqrt(head_size)

    @pl.when(pl.program_id(0) == 0)
    def _():
        row_at = iota((group_rows, group_rows), 0)
        col_at = iota((group_rows, group_rows), 1)
        cluster_of = row_at // part
        source_of = (row_at % part) // CAP
        from_row = source_of * block_rows + cluster_of * CAP + row_at % CAP
        turn_ref[...] = jnp.where(from_row == col_at, 1.0, 0.0).astype(BF16)
        causal_ref[...] = jnp.where(
            iota((slot_count, slot_count), 1) <= iota((slot_count, slot_count), 0), 0.0, MASKED
        )

    turn = turn_ref[...]
    for group in range(groups):
        arrived = recv_ref[group * 16 : (group + 1) * 16].reshape(group_rows, width)
        turned = dot(turn, arrived).astype(BF16)
        rows_ref[:, group * part : (group + 1) * part, :] = turned.reshape(owned, part, width)

    first_lane = jnp.where(iota((8, head_size), 1) == 0, 1.0, 0.0).astype(BF16)
    for cluster in range(owned):
        q = rows_ref[cluster, :, 0:head_size]
        k = rows_ref[cluster, :, head_size : 2 * head_size]
        v = rows_ref[cluster, :, 2 * head_size : 3 * head_size]
        g = rows_ref[cluster, :, 3 * head_size : 4 * head_size]
        marks = lax.dot_general(first_lane, k, CONTRACT_LAST, preferred_element_type=F32)
        present = marks < ABSENT / 2
        bias = jnp.where(present, 0.0, MASKED)[0:1]
        scores = lax.dot_general(q, k, CONTRACT_LAST, preferred_element_type=F32) * score_scale
        scores = scores + (causal_ref[...] + bias)
        weights = jnp.exp(scores - jnp.max(scores, axis=-1, keepdims=True))
        probs = weights / jnp.sum(weights, axis=-1, keepdims=True)
        probs_low = probs.astype(BF16)
        out = dot(probs_low, v).astype(BF16)
        grad_prob = lax.dot_general(g, v, CONTRACT_LAST, preferred_element_type=F32)
        delta = jnp.sum(g.astype(F32) * out.astype(F32), axis=-1, keepdims=True)
        grad_score = (probs * (grad_prob - delta) * score_scale).astype(BF16)
        grad_q = dot(grad_score, k)
        grad_k = lax.dot_general(grad_score, q, CONTRACT_FIRST, preferred_element_type=F32)
        grad_v = lax.dot_general(probs_low, g, CONTRACT_FIRST, preferred_element_type=F32)
        grads_ref[cluster, :, 0:head_size] = out
        grads_ref[cluster, :, head_size : 2 * head_size] = grad_q.astype(BF16)
        grads_ref[cluster, :, 2 * head_size : 3 * head_size] = grad_k.astype(BF16)
        grads_ref[cluster, :, 3 * head_size : 4 * head_size] = grad_v.astype(BF16)
        key_sums = dot(jnp.where(present, 1.0, 0.0).astype(BF16), k)[0:1]
        blend = DECAY_RATE * cent_ref[0, cluster : cluster + 1, :] + (1.0 - DECAY_RATE) * key_sums
        new_ref[0, cluster : cluster + 1, :] = blend / jnp.sqrt(
            jnp.mean(blend * blend, axis=-1, keepdims=True) + 1e-06
        )

    for group in range(groups):
        leaving = grads_ref[:, group * part : (group + 1) * part, :].reshape(group_rows, width)
        turned = lax.dot_general(turn, leaving, CONTRACT_FIRST, preferred_element_type=F32)
        back_ref[group * 16 : (group + 1) * 16] = turned.astype(BF16).reshape(
            16, block_rows, width
        )


def unpack_kernel(chunk, flat_ref, ret_ref, *refs):
    out_refs = refs[-4:]
    sources, block_rows, width = ret_ref.shape
    head_size = width // 4
    tok_rows, heads = flat_ref.shape
    slot_rows = sources * block_rows
    here = iota((tok_rows, heads), 1) == pl.program_id(0)
    flat_col = jnp.sum(jnp.where(here, flat_ref[...], 0), axis=1, keepdims=True)
    take = jnp.where(iota((tok_rows, slot_rows), 1) == flat_col, 1.0, 0.0).astype(BF16)
    rows = dot(take, ret_ref[...].reshape(slot_rows, width)).astype(BF16)
    for at, out_ref in enumerate(out_refs):
        out_ref[...] = rows[:, at * head_size : (at + 1) * head_size]


def route_kernel(ids_ref, slot_ref, base_ref, over_ref, header_ref):
    heads, _, tok_rows = ids_ref.shape
    cluster_count = slot_ref.shape[1]
    owners, lanes = header_ref.shape
    earlier = jnp.where(
        iota((tok_rows, tok_rows), 0) < iota((tok_rows, tok_rows), 1), 1.0, 0.0
    ).astype(BF16)
    slots_low = jnp.broadcast_to(slot_ref[...].astype(F32), (8, cluster_count)).astype(BF16)
    filled = jnp.zeros((owners, 1), F32)
    whole = jnp.zeros((owners, 1), F32)
    header = jnp.zeros((owners, lanes), F32)
    for head in range(heads):
        member_f = jnp.where(iota((cluster_count, tok_rows), 0) == ids_ref[head], 1.0, 0.0)
        member_low = member_f.astype(BF16)
        slot = dot(slots_low, member_low)[0:1].astype(jnp.int32)
        rank = jnp.sum(dot(member_low, earlier) * member_f, axis=0, keepdims=True)
        owner = (slot // CAP + TURN_BY * head) % owners
        tag = (head * CAP + slot % CAP) * CAP + rank.astype(jnp.int32)
        here = iota((owners, tok_rows), 0) == owner
        here_f = jnp.where(here, 1.0, 0.0)
        before = dot(here_f.astype(BF16), earlier)
        place = jnp.sum(before * here_f, axis=0, keepdims=True).astype(jnp.int32)
        late = jnp.sum((before + filled) * here_f, axis=0, keepdims=True)
        late = late.astype(jnp.int32) - SHARED
        filled = filled + jnp.maximum(jnp.sum(here_f, axis=1, keepdims=True) - SHARED, 0.0)
        whole = whole + jnp.sum(here_f, axis=1, keepdims=True)
        fits = place < SHARED
        packs = (late < PACKED - 1) & (place >= SHARED)
        base_ref[head] = jnp.where(fits, owner * SHARED + place, -1)
        over_ref[head] = jnp.where(packs, owner * PACKED + late, -1)
        lane = jnp.where(fits, head * SHARED + place, jnp.where(packs, heads * SHARED + late, -1))
        named = jnp.where(here, tag + 1, 0).astype(F32).astype(BF16)
        lane_at = jnp.where(iota((lanes, tok_rows), 0) == lane, 1.0, 0.0).astype(BF16)
        header = header + lax.dot_general(
            named, lane_at, CONTRACT_LAST, preferred_element_type=F32
        )
    peak = jnp.max(filled, axis=0, keepdims=True)
    header = jnp.where(iota((owners, lanes), 1) == PEAK_LANE, peak, header)
    peak = jnp.max(whole, axis=0, keepdims=True)
    header = jnp.where(iota((owners, lanes), 1) == PEAK_LANE - 1, peak, header)
    header_ref[...] = header.astype(BF16)


def token_rows(refs, at, head_size):
    lanes = slice(at * head_size, (at + 1) * head_size)
    return jnp.concatenate([ref[:, lanes] for ref in refs], axis=1)


def shared_rows(base_ref, rows, owners):
    tok_rows, width = rows[0].shape
    halves = []
    for at in range(2):
        place = iota((owners * SHARED, tok_rows), 0) == base_ref[at]
        placed = dot(jnp.where(place, 1.0, 0.0).astype(BF16), rows[at])
        halves.append(placed.reshape(owners, SHARED, width))
    return jnp.concatenate(halves, axis=1).astype(BF16)


def pack_first_kernel(
    base_ref, over_ref, header_ref, q_ref, k_ref, v_ref, g_ref, send_ref, total_ref
):
    owners, send_rows, width = send_ref.shape
    tok_rows = q_ref.shape[0]
    head_size = width // 4
    step = pl.program_id(0)
    rows = [token_rows((q_ref, k_ref, v_ref, g_ref), at, head_size) for at in range(2)]
    places = [
        jnp.where(iota((owners * PACKED, tok_rows), 0) == over_ref[at], 1.0, 0.0).astype(BF16)
        for at in range(2)
    ]
    added = dot(jnp.concatenate(places, axis=1), jnp.concatenate(rows, axis=0))

    @pl.when(step == 0)
    def _():
        total_ref[...] = added

    @pl.when(step > 0)
    def _():
        total_ref[...] += added

    @pl.when(step < pl.num_programs(0) // CHUNKS)
    def _():
        at_row = pl.multiple_of(step * 2 * SHARED, 2 * SHARED)
        send_ref[:, pl.ds(at_row, 2 * SHARED), :] = shared_rows(base_ref, rows, owners)

    @pl.when(step == pl.num_programs(0) - 1)
    def _():
        last_row = iota((owners * PACKED, owners), 1) * PACKED + PACKED - 1
        to_last = jnp.where(iota((owners * PACKED, owners), 0) == last_row, 1.0, 0.0)
        total_ref[:, :head_size] += dot(to_last.astype(BF16), header_ref[...])
        packed = total_ref[...].astype(BF16).reshape(owners, PACKED, width)
        send_ref[:, send_rows - PACKED :, :] = packed


def pack_second_kernel(base_ref, q_ref, k_ref, v_ref, g_ref, send_ref):
    owners, _, width = send_ref.shape
    rows = [token_rows((q_ref, k_ref, v_ref, g_ref), at, width // 4) for at in range(2)]
    send_ref[...] = shared_rows(base_ref, rows, owners)


def own_pair_kernel(first_step, last, *refs):
    shared_ref, over_ref = refs[:2]
    if last:
        before_ref, back_ref, sums_ref = refs[2:5]
        turn_ref, causal_ref, rows_ref, grads_ref = refs[5:]
    else:
        back_ref, over_back_ref, sums_ref, peak_ref = refs[2:6]
        turn_ref, causal_ref, rows_ref, grads_ref = refs[6:]
    sources, pair_rows, width = shared_ref.shape
    head_size = width // 4
    problems = rows_ref.shape[0]
    slot_count = sources * CAP
    bunch = 16
    groups = sources // bunch
    part = bunch * CAP
    shared_count = bunch * pair_rows
    packed_count = bunch * PACKED
    score_scale = 1.0 / math.sqrt(head_size)
    step = pl.program_id(0)

    @pl.when(step == 0)
    def _():
        at = iota((slot_count, slot_count), 0)
        causal_ref[...] = jnp.where(iota((slot_count, slot_count), 1) <= at, 0.0, MASKED)

    header_of = jnp.where(
        iota((bunch, packed_count), 1) == iota((bunch, packed_count), 0) * PACKED + PACKED - 1,
        1.0,
        0.0,
    ).astype(BF16)

    def turns(header, first_lane, rows_each, used):
        count = bunch * rows_each
        lane = iota((head_size, count), 1) % rows_each
        match = (iota((head_size, count), 0) == lane + first_lane) & (lane < used)
        tags = dot(header, jnp.where(match, 1.0, 0.0).astype(BF16))
        source = iota((1, count), 1) // rows_each
        own = iota((bunch, count), 0) == source
        tag = jnp.sum(jnp.where(own, tags, 0.0), axis=0, keepdims=True).astype(jnp.int32) - 1
        mine = (tag >= 0) & (tag // (problems * CAP) == first_step + step)
        problem = (tag // CAP) % problems
        slot = jnp.where(mine, problem * part + source * CAP + tag % CAP, -1)
        hit = iota((problems * part, count), 0) == slot
        return jnp.where(hit, 1.0, 0.0).astype(BF16)

    ones = jnp.ones((shared_count + packed_count, head_size), BF16)
    heads_shared = 4 * CHUNKS * SHARED
    peak = jnp.zeros((1, head_size), F32)
    for group in range(groups):
        from_sources = slice(group * bunch, (group + 1) * bunch)
        packed = over_ref[from_sources].reshape(packed_count, width)
        shared = shared_ref[from_sources].reshape(shared_count, width)
        header = dot(header_of, packed[:, :head_size])
        peak = jnp.maximum(peak, jnp.max(header, axis=0, keepdims=True))
        header = header.astype(BF16)
        turn = jnp.concatenate(
            [
                turns(header, (first_step + step) * pair_rows, pair_rows, pair_rows),
                turns(header, heads_shared, PACKED, PACKED - 1),
            ],
            axis=1,
        )
        turn_ref[group] = turn
        turned = dot(turn, jnp.concatenate([shared, packed], axis=0))
        marked = turned[:, head_size : 2 * head_size] + (1.0 - dot(turn, ones)) * ABSENT
        turned = jnp.concatenate(
            [turned[:, :head_size], marked, turned[:, 2 * head_size :]], axis=1
        )
        rows_ref[:, group * part : (group + 1) * part, :] = turned.astype(BF16).reshape(
            problems, part, width
        )
    if not last:
        peak_ref[...] = jnp.broadcast_to(peak, peak_ref.shape)

    first_lane = jnp.where(iota((8, head_size), 1) == 0, 1.0, 0.0).astype(BF16)

    def attend(problem):
        q = rows_ref[problem, :, 0:head_size]
        k = rows_ref[problem, :, head_size : 2 * head_size]
        v = rows_ref[problem, :, 2 * head_size : 3 * head_size]
        g = rows_ref[problem, :, 3 * head_size : 4 * head_size]
        marks = lax.dot_general(first_lane, k, CONTRACT_LAST, preferred_element_type=F32)
        present = marks < ABSENT / 2
        bias = jnp.where(present, 0.0, MASKED)[0:1]
        scores = lax.dot_general(q, k, CONTRACT_LAST, preferred_element_type=F32) * score_scale
        scores = scores + (causal_ref[...] + bias)
        weights = jnp.exp(scores - jnp.max(scores, axis=-1, keepdims=True))
        probs = weights / jnp.sum(weights, axis=-1, keepdims=True)
        probs_low = probs.astype(BF16)
        out = dot(probs_low, v).astype(BF16)
        grad_prob = lax.dot_general(g, v, CONTRACT_LAST, preferred_element_type=F32)
        delta = jnp.sum(g.astype(F32) * out.astype(F32), axis=-1, keepdims=True)
        grad_score = (probs * (grad_prob - delta) * score_scale).astype(BF16)
        grad_q = dot(grad_score, k)
        grad_k = lax.dot_general(grad_score, q, CONTRACT_FIRST, preferred_element_type=F32)
        grad_v = lax.dot_general(probs_low, g, CONTRACT_FIRST, preferred_element_type=F32)
        grads_ref[problem, :, 0:head_size] = out
        grads_ref[problem, :, head_size : 2 * head_size] = grad_q.astype(BF16)
        grads_ref[problem, :, 2 * head_size : 3 * head_size] = grad_k.astype(BF16)
        grads_ref[problem, :, 3 * head_size : 4 * head_size] = grad_v.astype(BF16)
        sums = dot(jnp.where(present, 1.0, 0.0).astype(BF16), k)[0:1]
        sums_ref[0, pl.ds(problem, 1), :] = sums

    @pl.loop(0, problems // 2)
    def _(pair):
        attend(pair * 2)
        attend(pair * 2 + 1)

    for group in range(groups):
        from_sources = slice(group * bunch, (group + 1) * bunch)
        leaving = grads_ref[:, group * part : (group + 1) * part, :].reshape(
            problems * part, width
        )
        sent = lax.dot_general(
            turn_ref[group], leaving, CONTRACT_FIRST, preferred_element_type=F32
        ).astype(BF16)
        shared = sent[:shared_count].reshape(bunch, pair_rows, width)
        packed = sent[shared_count:].reshape(bunch, PACKED, width)
        if last:
            at_row = pl.multiple_of(step * pair_rows, pair_rows)
            back_ref[from_sources, pl.ds(at_row, pair_rows), :] = shared
            rest = slice(back_ref.shape[1] - PACKED, back_ref.shape[1])

            @pl.when(step == 0)
            def _():
                back_ref[from_sources, rest, :] = before_ref[from_sources] + packed

            @pl.when(step > 0)
            def _():
                back_ref[from_sources, rest, :] += packed
        else:
            back_ref[from_sources] = shared

            @pl.when(step == 0)
            def _():
                over_back_ref[from_sources] = packed

            @pl.when(step > 0)
            def _():
                over_back_ref[from_sources] += packed


def unpack_pair_kernel(steps, base_ref, over_ref, first_ref, second_ref, packed_ref, *out_refs):
    owners, _, width = first_ref.shape
    head_size = width // 4
    tok_rows, heads = base_ref.shape
    step = pl.program_id(0)
    packed = packed_ref[...].reshape(owners * PACKED, width)
    arrived = jnp.where(step < steps, first_ref[...], second_ref[...]).astype(F32)
    for at in range(2):
        here = iota((tok_rows, heads), 1) == step * 2 + at
        base = jnp.sum(jnp.where(here, base_ref[...], 0), axis=1, keepdims=True)
        over = jnp.sum(jnp.where(here, over_ref[...], 0), axis=1, keepdims=True)
        take = iota((tok_rows, owners * SHARED), 1) == base
        take_over = iota((tok_rows, owners * PACKED), 1) == over
        mine = arrived[:, at * SHARED : (at + 1) * SHARED, :].reshape(owners * SHARED, width)
        rows = dot(jnp.where(take, 1.0, 0.0).astype(BF16), mine.astype(BF16))
        rows = rows + dot(jnp.where(take_over, 1.0, 0.0).astype(BF16), packed)
        rows = rows.astype(BF16)
        for which, out_ref in enumerate(out_refs):
            out_ref[:, at * head_size : (at + 1) * head_size] = rows[
                :, which * head_size : (which + 1) * head_size
            ]


def params():
    return pltpu.CompilerParams(vmem_limit_bytes=VMEM_BYTES)


def dense(queries, keys, values, out_grad, cluster_ids, cluster_slot, centroids):
    seq_count = lax.axis_size("seq")
    local_heads, tok_rows = cluster_ids.shape[:2]
    cluster_count = cluster_slot.shape[0]
    owned = cluster_count // seq_count
    head_size = centroids.shape[2]
    heads = local_heads // CHUNKS
    block_rows = owned * CAP
    width = 4 * head_size
    slot_count = seq_count * CAP
    sent = jax.ShapeDtypeStruct((seq_count, heads * block_rows, width), BF16)
    sent_bytes = seq_count * heads * block_rows * width * 2
    ids_rows = cluster_ids.reshape(local_heads, 1, tok_rows)
    slot_row = cluster_slot.reshape(1, cluster_count)
    block = pl.BlockSpec((seq_count, block_rows, width), lambda h: (0, h, 0))

    def exchange(rows):
        return lax.all_to_all(rows, "seq", split_axis=0, concat_axis=0, tiled=True)

    def pack(chunk):
        column = pl.BlockSpec((tok_rows, head_size), lambda h: (0, chunk * heads + h))
        return pl.pallas_call(
            pack_kernel,
            grid=(heads,),
            in_specs=[
                pl.BlockSpec((1, 1, tok_rows), lambda h: (chunk * heads + h, 0, 0)),
                pl.BlockSpec((1, cluster_count), lambda h: (0, 0)),
                column,
                column,
                column,
                column,
            ],
            out_specs=[block, pl.BlockSpec((1, 1, tok_rows), lambda h: (h, 0, 0))],
            out_shape=[sent, jax.ShapeDtypeStruct((heads, 1, tok_rows), jnp.int32)],
            scratch_shapes=[pltpu.VMEM((tok_rows, tok_rows), BF16)],
            compiler_params=params(),
            cost_estimate=pl.CostEstimate(
                flops=heads * 2 * 1024 * 512 * 640, bytes_accessed=2 * sent_bytes, transcendentals=0
            ),
            name="pack",
        )(ids_rows, slot_row, queries, keys, values, out_grad)

    def own(chunk, received):
        return pl.pallas_call(
            owner_kernel,
            grid=(heads,),
            in_specs=[
                block,
                pl.BlockSpec((1, owned, head_size), lambda h: (chunk * heads + h, 0, 0)),
            ],
            out_specs=[block, pl.BlockSpec((1, owned, head_size), lambda h: (h, 0, 0))],
            out_shape=[sent, jax.ShapeDtypeStruct((heads, owned, head_size), F32)],
            scratch_shapes=[
                pltpu.VMEM((16 * block_rows, 16 * block_rows), BF16),
                pltpu.VMEM((slot_count, slot_count), F32),
                pltpu.VMEM((owned, slot_count, width), BF16),
                pltpu.VMEM((owned, slot_count, width), BF16),
            ],
            compiler_params=params(),
            cost_estimate=pl.CostEstimate(
                flops=heads * owned * 7 * 2 * slot_count * slot_count * head_size,
                bytes_accessed=2 * sent_bytes,
                transcendentals=heads * owned * slot_count * slot_count,
            ),
            name="own",
        )(received, centroids)

    def unpack(chunk, flat_cols, returned, previous):
        column = pl.BlockSpec((tok_rows, head_size), lambda h: (0, chunk * heads + h))
        whole = jax.ShapeDtypeStruct((tok_rows, local_heads * head_size), BF16)

        def kernel(*refs):
            unpack_kernel(chunk, *refs)

        return pl.pallas_call(
            kernel,
            grid=(heads,),
            in_specs=[pl.BlockSpec((tok_rows, heads), lambda h: (0, 0)), block]
            + [pl.BlockSpec(memory_space=pl.ANY)] * len(previous),
            out_specs=[column] * 4,
            out_shape=[whole] * 4,
            input_output_aliases={2 + i: i for i in range(len(previous))},
            compiler_params=params(),
            cost_estimate=pl.CostEstimate(
                flops=heads * 2 * 1024 * 512 * 512, bytes_accessed=2 * sent_bytes, transcendentals=0
            ),
            name="unpack",
        )(flat_cols, returned, *previous)

    packed = [pack(chunk) for chunk in range(CHUNKS)]
    received = [exchange(rows) for rows, _ in packed]
    owned_now = [own(chunk, rows) for chunk, rows in enumerate(received)]
    returned = [exchange(rows) for rows, _ in owned_now]
    outs = ()
    for chunk in range(CHUNKS):
        flat_cols = packed[chunk][1].reshape(heads, tok_rows).T
        outs = unpack(chunk, flat_cols, returned[chunk], tuple(outs))
    new_centroids = jnp.concatenate([new for _, new in owned_now], axis=0)
    return (*outs, new_centroids)


def exchange(rows):
    return lax.all_to_all(rows, "seq", split_axis=0, concat_axis=0, tiled=True)


def body(queries, keys, values, out_grad, cluster_ids, cluster_slot, centroids):
    seq_count = lax.axis_size("seq")
    heads, tok_rows = cluster_ids.shape[:2]
    cluster_count = cluster_slot.shape[0]
    owned, head_size = centroids.shape[1:]
    width = 4 * head_size
    pair_rows = 2 * SHARED
    steps = heads // 2 // CHUNKS
    chunk_rows = steps * pair_rows
    send_rows = chunk_rows + PACKED
    slot_count = seq_count * CAP
    problems = 2 * owned
    block_bytes = seq_count * pair_rows * width * 2

    def shaped(rows):
        return jax.ShapeDtypeStruct((seq_count, rows, width), BF16)

    def cost(flops, blocks, exps=0):
        return pl.CostEstimate(
            flops=flops, bytes_accessed=blocks * block_bytes, transcendentals=exps
        )

    block = pl.BlockSpec((seq_count, pair_rows, width), lambda s: (0, s, 0))
    over_block = pl.BlockSpec((seq_count, PACKED, width), lambda s: (0, chunk_rows // PACKED, 0))
    whole_block = pl.BlockSpec((seq_count, PACKED, width), lambda s: (0, 0, 0))
    column = pl.BlockSpec((tok_rows, 2 * head_size), lambda s: (0, s))
    second_column = pl.BlockSpec((tok_rows, 2 * head_size), lambda s: (0, steps + s))
    row_block = pl.BlockSpec((2, 1, tok_rows), lambda s: (s, 0, 0))
    second_row_block = pl.BlockSpec((2, 1, tok_rows), lambda s: (steps + s, 0, 0))
    sent_whole = pl.BlockSpec((seq_count, send_rows, width), lambda s: (0, 0, 0))

    base_rows, over_rows, header = pl.pallas_call(
        route_kernel,
        out_shape=[jax.ShapeDtypeStruct((heads, 1, tok_rows), jnp.int32)] * 2
        + [jax.ShapeDtypeStruct((seq_count, head_size), BF16)],
        compiler_params=params(),
        name="route",
    )(cluster_ids.reshape(heads, 1, tok_rows), cluster_slot.reshape(1, cluster_count))
    first_sent = pl.pallas_call(
        pack_first_kernel,
        grid=(CHUNKS * steps,),
        in_specs=[row_block] * 2
        + [pl.BlockSpec((seq_count, head_size), lambda s: (0, 0))]
        + [column] * 4,
        out_specs=sent_whole,
        out_shape=shaped(send_rows),
        scratch_shapes=[pltpu.VMEM((seq_count * PACKED, width), F32)],
        compiler_params=params(),
        cost_estimate=cost(2 * heads * 1280 * tok_rows * width, 9),
        name="pack_first",
    )(base_rows, over_rows, header, queries, keys, values, out_grad)
    second_sent = pl.pallas_call(
        pack_second_kernel,
        grid=(steps,),
        in_specs=[second_row_block] + [second_column] * 4,
        out_specs=block,
        out_shape=shaped(chunk_rows),
        compiler_params=params(),
        cost_estimate=cost(4 * steps * tok_rows * tok_rows * width, 2 * steps),
        name="pack_second",
    )(base_rows, queries, keys, values, out_grad)

    def own(chunk, *args):
        last = chunk == CHUNKS - 1

        def kernel(*refs):
            own_pair_kernel(chunk * steps, last, *refs)

        sums_block = pl.BlockSpec((1, problems, head_size), lambda s: (s, 0, 0))
        sums_shape = jax.ShapeDtypeStruct((steps, problems, head_size), F32)
        if last:
            in_specs = [block, over_block, whole_block]
            out_specs = [sent_whole, sums_block]
            out_shape = [shaped(send_rows), sums_shape]
        else:
            in_specs = [block, over_block]
            peak_block = pl.BlockSpec((8, 128), lambda s: (0, 0))
            out_specs = [block, whole_block, sums_block, peak_block]
            out_shape = [shaped(chunk_rows), shaped(PACKED), sums_shape]
            out_shape.append(jax.ShapeDtypeStruct((8, 128), F32))
        return pl.pallas_call(
            kernel,
            grid=(steps,),
            in_specs=in_specs,
            out_specs=out_specs,
            out_shape=out_shape,
            scratch_shapes=[
                pltpu.VMEM(
                    (seq_count // 16, problems * 16 * CAP, 16 * (pair_rows + PACKED)), BF16
                ),
                pltpu.VMEM((slot_count, slot_count), F32),
                pltpu.VMEM((problems, slot_count, width), BF16),
                pltpu.VMEM((problems, slot_count, width), BF16),
            ],
            compiler_params=params(),
            cost_estimate=cost(
                steps * problems * 16 * 2 * slot_count * slot_count * head_size,
                4 * steps,
                steps * problems * slot_count * slot_count,
            ),
            name="own_pair",
        )(*args)

    first = exchange(first_sent)
    second = exchange(second_sent)
    first_back, packed_back, first_sums, peak = own(0, first, first)
    first_home = exchange(first_back)
    second_back, second_sums = own(1, second, first, packed_back)
    second_home = exchange(second_back)
    swap = [(at, 1 - at) for at in range(2)]
    peak = peak[0:1]
    peak = jnp.maximum(peak, lax.ppermute(peak, "head", swap))

    def mark(name, lane, limits):
        value = peak[0, lane]

        def seen(at):
            def kernel(from_ref, to_ref):
                to_ref[...] = from_ref[...]

            def run(row):
                return pl.pallas_call(kernel, out_shape=row, name=f"{name}{at}")(row)

            return run

        bucket = sum((value > limit).astype(jnp.int32) for limit in limits)
        return lax.switch(bucket, [seen(at) for at in (0, *limits)], peak)

    largest = mark("over", PEAK_LANE, (11, 15, 19, 23, 27, 31, 35, 39, 47, 55))
    widest = mark("whole", PEAK_LANE - 1, (71, 75, 79, 83, 87, 91, 95, 99, 107, 119))
    peak = jnp.maximum(largest, widest)[0, PEAK_LANE]

    sums = [half.reshape(2 * steps, owned, head_size) for half in (first_sums, second_sums)]
    homes = []
    for head in range(heads):
        here = sums[head // (2 * steps)][head % (2 * steps)]
        moves = [((at + TURN_BY * head) % seq_count, at) for at in range(seq_count)]
        homes.append(here if head == 0 else lax.ppermute(here, "seq", moves))
    blend_sum = DECAY_RATE * centroids + (1.0 - DECAY_RATE) * jnp.stack(homes)
    new_centroids = blend_sum / jnp.sqrt(
        jnp.mean(blend_sum * blend_sum, axis=-1, keepdims=True) + 1e-06
    )

    def unpack(operands):
        _, (base_cols, over_cols, home_one, home_two, centroids_now) = operands

        def kernel(*refs):
            unpack_pair_kernel(steps, *refs)

        routes_block = pl.BlockSpec((tok_rows, heads), lambda s: (0, 0))
        outs = pl.pallas_call(
            kernel,
            grid=(CHUNKS * steps,),
            in_specs=[
                routes_block,
                routes_block,
                pl.BlockSpec(
                    (seq_count, pair_rows, width), lambda s: (0, jnp.minimum(s, steps - 1), 0)
                ),
                pl.BlockSpec(
                    (seq_count, pair_rows, width), lambda s: (0, jnp.maximum(s - steps, 0), 0)
                ),
                over_block,
            ],
            out_specs=[column] * 4,
            out_shape=[jax.ShapeDtypeStruct((tok_rows, heads * head_size), BF16)] * 4,
            compiler_params=params(),
            cost_estimate=cost(2 * heads * 1536 * tok_rows * width, 9),
            name="unpack_pair",
        )(base_cols, over_cols, home_one, home_two, home_two)
        return (*outs, centroids_now)

    def again(operands):
        return dense(*operands[0])

    return lax.cond(
        peak < PACKED,
        unpack,
        again,
        (
            (queries, keys, values, out_grad, cluster_ids, cluster_slot, centroids),
            (
                base_rows.reshape(heads, tok_rows).T,
                over_rows.reshape(heads, tok_rows).T,
                first_home,
                second_home,
                new_centroids,
            ),
        ),
    )


def solution(mesh):
    return jax.shard_map(
        body,
        mesh=mesh,
        in_specs=(
            P("seq", "head"),
            P("seq", "head"),
            P("seq", "head"),
            P("seq", "head"),
            P("head", "seq", None),
            P(),
            P("head", "seq", None),
        ),
        out_specs=(
            P("seq", "head"),
            P("seq", "head"),
            P("seq", "head"),
            P("seq", "head"),
            P("head", "seq", None),
        ),
        check_vma=False,
    )
```

```python
import functools
import math

import jax
import jax.numpy as jnp
from jax import lax
from jax.experimental import pallas as pl
from jax.experimental.pallas import tpu as pltpu
from jax.sharding import PartitionSpec as P

CAP = 4
DECAY_RATE = 0.9
MASKED = -1e30
ABSENT = 64.0
CHUNKS = 2
SHARED = 8
PACKED = 16
SPARE = 2
PEAK_LANE = 127
TURN_BY = 8
VMEM_BYTES = 60 * 1024 * 1024

F32 = jnp.float32
BF16 = jnp.bfloat16
CONTRACT_LAST = (((1,), (1,)), ((), ()))
CONTRACT_FIRST = (((0,), (0,)), ((), ()))


def iota(shape, dim):
    return lax.broadcasted_iota(jnp.int32, shape, dim)


def dot(left, right):
    return jnp.dot(left, right, preferred_element_type=F32)


def pack_kernel(ids_ref, slot_ref, q_ref, k_ref, v_ref, g_ref, send_ref, flat_ref, earlier_ref):
    tok_rows = ids_ref.shape[2]
    cluster_count = slot_ref.shape[1]
    slot_rows = cluster_count * CAP

    @pl.when(pl.program_id(0) == 0)
    def _():
        earlier_ref[...] = (iota((tok_rows, tok_rows), 0) < iota((tok_rows, tok_rows), 1)).astype(
            F32
        ).astype(BF16)

    ids_row = ids_ref[0]
    member = iota((cluster_count, tok_rows), 0) == ids_row
    member_f = jnp.where(member, 1.0, 0.0)
    member_low = member_f.astype(BF16)
    slots_low = jnp.broadcast_to(slot_ref[...].astype(F32), (8, cluster_count)).astype(BF16)
    slot_row = dot(slots_low, member_low)[0:1]
    rank_row = jnp.sum(dot(member_low, earlier_ref[...]) * member_f, axis=0, keepdims=True)
    flat_row = (slot_row * CAP + rank_row).astype(jnp.int32)
    flat_ref[0] = flat_row
    place = jnp.where(iota((slot_rows, tok_rows), 0) == flat_row, 1.0, 0.0).astype(BF16)
    ones = jnp.ones((tok_rows, 128), BF16)
    head_size = q_ref.shape[1]
    taken = dot(place, ones)
    out_shape = send_ref.shape[:2] + (head_size,)

    def put(at, rows):
        send_ref[:, :, at * head_size : (at + 1) * head_size] = rows.astype(BF16).reshape(out_shape)

    put(0, dot(place, q_ref[...]))
    put(1, dot(place, k_ref[...]) + (1.0 - taken) * ABSENT)
    put(2, dot(place, v_ref[...]))
    put(3, dot(place, g_ref[...]))


def owner_kernel(recv_ref, cent_ref, back_ref, new_ref, turn_ref, causal_ref, rows_ref, grads_ref):
    source_count, block_rows, width = recv_ref.shape
    head_size = width // 4
    owned = block_rows // CAP
    slot_count = source_count * CAP
    group_rows = 16 * block_rows
    groups = source_count // 16
    part = 16 * CAP
    score_scale = 1.0 / math.sqrt(head_size)

    @pl.when(pl.program_id(0) == 0)
    def _():
        row_at = iota((group_rows, group_rows), 0)
        col_at = iota((group_rows, group_rows), 1)
        cluster_of = row_at // part
        source_of = (row_at % part) // CAP
        from_row = source_of * block_rows + cluster_of * CAP + row_at % CAP
        turn_ref[...] = jnp.where(from_row == col_at, 1.0, 0.0).astype(BF16)
        causal_ref[...] = jnp.where(
            iota((slot_count, slot_count), 1) <= iota((slot_count, slot_count), 0), 0.0, MASKED
        )

    turn = turn_ref[...]
    for group in range(groups):
        arrived = recv_ref[group * 16 : (group + 1) * 16].reshape(group_rows, width)
        turned = dot(turn, arrived).astype(BF16)
        rows_ref[:, group * part : (group + 1) * part, :] = turned.reshape(owned, part, width)

    first_lane = jnp.where(iota((8, head_size), 1) == 0, 1.0, 0.0).astype(BF16)
    for cluster in range(owned):
        q = rows_ref[cluster, :, 0:head_size]
        k = rows_ref[cluster, :, head_size : 2 * head_size]
        v = rows_ref[cluster, :, 2 * head_size : 3 * head_size]
        g = rows_ref[cluster, :, 3 * head_size : 4 * head_size]
        marks = lax.dot_general(first_lane, k, CONTRACT_LAST, preferred_element_type=F32)
        present = marks < ABSENT / 2
        bias = jnp.where(present, 0.0, MASKED)[0:1]
        scores = lax.dot_general(q, k, CONTRACT_LAST, preferred_element_type=F32) * score_scale
        scores = scores + (causal_ref[...] + bias)
        weights = jnp.exp(scores - jnp.max(scores, axis=-1, keepdims=True))
        probs = weights / jnp.sum(weights, axis=-1, keepdims=True)
        probs_low = probs.astype(BF16)
        out = dot(probs_low, v).astype(BF16)
        grad_prob = lax.dot_general(g, v, CONTRACT_LAST, preferred_element_type=F32)
        delta = jnp.sum(g.astype(F32) * out.astype(F32), axis=-1, keepdims=True)
        grad_score = (probs * (grad_prob - delta) * score_scale).astype(BF16)
        grad_q = dot(grad_score, k)
        grad_k = lax.dot_general(grad_score, q, CONTRACT_FIRST, preferred_element_type=F32)
        grad_v = lax.dot_general(probs_low, g, CONTRACT_FIRST, preferred_element_type=F32)
        grads_ref[cluster, :, 0:head_size] = out
        grads_ref[cluster, :, head_size : 2 * head_size] = grad_q.astype(BF16)
        grads_ref[cluster, :, 2 * head_size : 3 * head_size] = grad_k.astype(BF16)
        grads_ref[cluster, :, 3 * head_size : 4 * head_size] = grad_v.astype(BF16)
        key_sums = dot(jnp.where(present, 1.0, 0.0).astype(BF16), k)[0:1]
        blend = DECAY_RATE * cent_ref[0, cluster : cluster + 1, :] + (1.0 - DECAY_RATE) * key_sums
        new_ref[0, cluster : cluster + 1, :] = blend / jnp.sqrt(
            jnp.mean(blend * blend, axis=-1, keepdims=True) + 1e-06
        )

    for group in range(groups):
        leaving = grads_ref[:, group * part : (group + 1) * part, :].reshape(group_rows, width)
        turned = lax.dot_general(turn, leaving, CONTRACT_FIRST, preferred_element_type=F32)
        back_ref[group * 16 : (group + 1) * 16] = turned.astype(BF16).reshape(
            16, block_rows, width
        )


def unpack_kernel(chunk, flat_ref, ret_ref, *refs):
    out_refs = refs[-4:]
    sources, block_rows, width = ret_ref.shape
    head_size = width // 4
    tok_rows, heads = flat_ref.shape
    slot_rows = sources * block_rows
    here = iota((tok_rows, heads), 1) == pl.program_id(0)
    flat_col = jnp.sum(jnp.where(here, flat_ref[...], 0), axis=1, keepdims=True)
    take = jnp.where(iota((tok_rows, slot_rows), 1) == flat_col, 1.0, 0.0).astype(BF16)
    rows = dot(take, ret_ref[...].reshape(slot_rows, width)).astype(BF16)
    for at, out_ref in enumerate(out_refs):
        out_ref[...] = rows[:, at * head_size : (at + 1) * head_size]


def route_kernel(first_head, ids_ref, slot_ref, base_ref, over_ref, header_ref):
    heads, _, tok_rows = ids_ref.shape
    cluster_count = slot_ref.shape[1]
    owners, lanes = header_ref.shape
    earlier = jnp.where(
        iota((tok_rows, tok_rows), 0) < iota((tok_rows, tok_rows), 1), 1.0, 0.0
    ).astype(BF16)
    slots_low = jnp.broadcast_to(slot_ref[...].astype(F32), (8, cluster_count)).astype(BF16)
    filled = jnp.zeros((owners, 1), F32)
    header = jnp.zeros((owners, lanes), F32)
    for head in range(heads):
        member_f = jnp.where(iota((cluster_count, tok_rows), 0) == ids_ref[head], 1.0, 0.0)
        member_low = member_f.astype(BF16)
        slot = dot(slots_low, member_low)[0:1].astype(jnp.int32)
        rank = jnp.sum(dot(member_low, earlier) * member_f, axis=0, keepdims=True)
        owner = (slot // CAP + TURN_BY * (first_head + head)) % owners
        tag = (head * CAP + slot % CAP) * CAP + rank.astype(jnp.int32)
        here = iota((owners, tok_rows), 0) == owner
        here_f = jnp.where(here, 1.0, 0.0)
        before = dot(here_f.astype(BF16), earlier)
        place = jnp.sum(before * here_f, axis=0, keepdims=True).astype(jnp.int32)
        late = jnp.sum((before + filled) * here_f, axis=0, keepdims=True)
        late = late.astype(jnp.int32) - SHARED
        filled = filled + jnp.maximum(jnp.sum(here_f, axis=1, keepdims=True) - SHARED, 0.0)
        fits = place < SHARED
        packs = (late < PACKED - SPARE) & (place >= SHARED)
        base_ref[head] = jnp.where(fits, owner * SHARED + place, -1)
        over_ref[head] = jnp.where(packs, owner * PACKED + late, -1)
        lane = jnp.where(fits, head * SHARED + place, jnp.where(packs, heads * SHARED + late, -1))
        named = jnp.where(here, tag + 1, 0).astype(F32).astype(BF16)
        lane_at = jnp.where(iota((lanes, tok_rows), 0) == lane, 1.0, 0.0).astype(BF16)
        header = header + lax.dot_general(
            named, lane_at, CONTRACT_LAST, preferred_element_type=F32
        )
    peak = jnp.max(filled, axis=0, keepdims=True)
    header_ref[...] = jnp.where(iota((owners, lanes), 1) == PEAK_LANE, peak, header).astype(BF16)


def token_rows(refs, at, head_size):
    lanes = slice(at * head_size, (at + 1) * head_size)
    return jnp.concatenate([ref[:, lanes] for ref in refs], axis=1)


def pack_rows_kernel(
    base_ref, over_ref, header_ref, q_ref, k_ref, v_ref, g_ref, send_ref, total_ref
):
    owners, send_rows, width = send_ref.shape
    tok_rows = q_ref.shape[0]
    head_size = width // 4
    step = pl.program_id(0)
    rows = [token_rows((q_ref, k_ref, v_ref, g_ref), at, head_size) for at in range(2)]
    halves = []
    for at in range(2):
        place = iota((owners * SHARED, tok_rows), 0) == base_ref[at]
        placed = dot(jnp.where(place, 1.0, 0.0).astype(BF16), rows[at])
        halves.append(placed.reshape(owners, SHARED, width))
    at_row = pl.multiple_of(step * 2 * SHARED, 2 * SHARED)
    shared = jnp.concatenate(halves, axis=1).astype(BF16)
    send_ref[:, pl.ds(at_row, 2 * SHARED), :] = shared

    places = [
        jnp.where(iota((owners * PACKED, tok_rows), 0) == over_ref[at], 1.0, 0.0).astype(BF16)
        for at in range(2)
    ]
    added = dot(jnp.concatenate(places, axis=1), jnp.concatenate(rows, axis=0))

    @pl.when(step == 0)
    def _():
        total_ref[...] = added

    @pl.when(step == pl.num_programs(0) - 1)
    def _():
        total = total_ref[...] + added
        last_row = iota((owners * PACKED, owners), 1) * PACKED + PACKED - 1
        to_last = jnp.where(iota((owners * PACKED, owners), 0) == last_row, 1.0, 0.0)
        tags = dot(to_last.astype(BF16), header_ref[...])
        total = jnp.concatenate([total[:, :head_size] + tags, total[:, head_size:]], axis=1)
        packed = total.astype(BF16).reshape(owners, PACKED, width)
        send_ref[:, send_rows - PACKED :, :] = packed


def own_rows_kernel(
    first_head,
    me_ref,
    shared_ref,
    over_ref,
    back_ref,
    peak_ref,
    turn_ref,
    causal_ref,
    rows_ref,
    grads_ref,
    sums_ref,
):
    sources, pair_rows, width = shared_ref.shape
    head_size = width // 4
    problems = rows_ref.shape[0]
    owned = problems // 2
    slot_count = sources * CAP
    bunch = 16
    groups = sources // bunch
    part = bunch * CAP
    shared_count = bunch * pair_rows
    packed_count = bunch * PACKED
    score_scale = 1.0 / math.sqrt(head_size)
    step = pl.program_id(0)
    steps = pl.num_programs(0)

    @pl.when(step == 0)
    def _():
        at = iota((slot_count, slot_count), 0)
        causal_ref[...] = jnp.where(iota((slot_count, slot_count), 1) <= at, 0.0, MASKED)

    header_of = jnp.where(
        iota((bunch, packed_count), 1) == iota((bunch, packed_count), 0) * PACKED + PACKED - 1,
        1.0,
        0.0,
    ).astype(BF16)

    def turns(header, first_lane, rows_each, used):
        count = bunch * rows_each
        lane = iota((head_size, count), 1) % rows_each
        match = (iota((head_size, count), 0) == lane + first_lane) & (lane < used)
        tags = dot(header, jnp.where(match, 1.0, 0.0).astype(BF16))
        source = iota((1, count), 1) // rows_each
        own = iota((bunch, count), 0) == source
        tag = jnp.sum(jnp.where(own, tags, 0.0), axis=0, keepdims=True).astype(jnp.int32) - 1
        mine = (tag >= 0) & (tag // (problems * CAP) == step)
        problem = (tag // CAP) % problems
        slot = jnp.where(mine, problem * part + source * CAP + tag % CAP, -1)
        hit = iota((problems * part, count), 0) == slot
        return jnp.where(hit, 1.0, 0.0).astype(BF16)

    ones = jnp.ones((shared_count + packed_count, head_size), BF16)
    peak = jnp.zeros((1, head_size), F32)
    for group in range(groups):
        from_sources = slice(group * bunch, (group + 1) * bunch)
        packed = over_ref[from_sources].reshape(packed_count, width)
        shared = shared_ref[from_sources].reshape(shared_count, width)
        header = dot(header_of, packed[:, :head_size])
        peak = jnp.maximum(peak, jnp.max(header, axis=0, keepdims=True))
        header = header.astype(BF16)
        turn = jnp.concatenate(
            [
                turns(header, step * pair_rows, pair_rows, pair_rows),
                turns(header, steps * pair_rows, PACKED, PACKED - SPARE),
            ],
            axis=1,
        )
        turn_ref[group] = turn
        turned = dot(turn, jnp.concatenate([shared, packed], axis=0))
        marked = turned[:, head_size : 2 * head_size] + (1.0 - dot(turn, ones)) * ABSENT
        turned = jnp.concatenate(
            [turned[:, :head_size], marked, turned[:, 2 * head_size :]], axis=1
        )
        rows_ref[:, group * part : (group + 1) * part, :] = turned.astype(BF16).reshape(
            problems, part, width
        )
    peak_ref[...] = jnp.broadcast_to(peak, peak_ref.shape)

    first_lane = jnp.where(iota((8, head_size), 1) == 0, 1.0, 0.0).astype(BF16)

    def attend(problem):
        q = rows_ref[problem, :, 0:head_size]
        k = rows_ref[problem, :, head_size : 2 * head_size]
        v = rows_ref[problem, :, 2 * head_size : 3 * head_size]
        g = rows_ref[problem, :, 3 * head_size : 4 * head_size]
        marks = lax.dot_general(first_lane, k, CONTRACT_LAST, preferred_element_type=F32)
        present = marks < ABSENT / 2
        bias = jnp.where(present, 0.0, MASKED)[0:1]
        scores = lax.dot_general(q, k, CONTRACT_LAST, preferred_element_type=F32) * score_scale
        scores = scores + (causal_ref[...] + bias)
        weights = jnp.exp(scores - jnp.max(scores, axis=-1, keepdims=True))
        probs = weights / jnp.sum(weights, axis=-1, keepdims=True)
        probs_low = probs.astype(BF16)
        out = dot(probs_low, v).astype(BF16)
        grad_prob = lax.dot_general(g, v, CONTRACT_LAST, preferred_element_type=F32)
        delta = jnp.sum(g.astype(F32) * out.astype(F32), axis=-1, keepdims=True)
        grad_score = (probs * (grad_prob - delta) * score_scale).astype(BF16)
        grad_q = dot(grad_score, k)
        grad_k = lax.dot_general(grad_score, q, CONTRACT_FIRST, preferred_element_type=F32)
        grad_v = lax.dot_general(probs_low, g, CONTRACT_FIRST, preferred_element_type=F32)
        grads_ref[problem, :, 0:head_size] = out
        grads_ref[problem, :, head_size : 2 * head_size] = grad_q.astype(BF16)
        grads_ref[problem, :, 2 * head_size : 3 * head_size] = grad_k.astype(BF16)
        grads_ref[problem, :, 3 * head_size : 4 * head_size] = grad_v.astype(BF16)
        sums = dot(jnp.where(present, 1.0, 0.0).astype(BF16), k)[0:1]
        sums_ref[pl.ds(problem, 1), :] = sums

    @pl.loop(0, problems // 2)
    def _(pair):
        attend(pair * 2)
        attend(pair * 2 + 1)

    rest = slice(back_ref.shape[1] - PACKED, back_ref.shape[1])
    for group in range(groups):
        from_sources = slice(group * bunch, (group + 1) * bunch)
        leaving = grads_ref[:, group * part : (group + 1) * part, :].reshape(
            problems * part, width
        )
        sent = lax.dot_general(
            turn_ref[group], leaving, CONTRACT_FIRST, preferred_element_type=F32
        ).astype(BF16)
        at_row = pl.multiple_of(step * pair_rows, pair_rows)
        back_ref[from_sources, pl.ds(at_row, pair_rows), :] = sent[:shared_count].reshape(
            bunch, pair_rows, width
        )
        packed = sent[shared_count:].reshape(bunch, PACKED, width)

        @pl.when(step == 0)
        def _():
            back_ref[from_sources, rest, :] = packed

        @pl.when(step > 0)
        def _():
            back_ref[from_sources, rest, :] += packed

    for at in range(2):
        sums = jnp.concatenate(
            [sums_ref[at * owned + slot : at * owned + slot + 1, :] for slot in range(owned)],
            axis=1,
        )
        high = sums.astype(BF16).astype(F32)
        low = sums - high
        turned_by = TURN_BY * (first_head + step * 2 + at)
        home = lax.rem(me_ref[0] + sources * TURN_BY - turned_by, sources)
        row = iota((PACKED, width), 0)
        tile = back_ref[home, rest, :].astype(F32)
        tile = jnp.where(row == PACKED - 2, high, jnp.where(row == PACKED - 1, low, tile))
        back_ref[home, rest, :] = tile.astype(BF16)


def unpack_rows_kernel(
    first_head, me_ref, base_ref, over_ref, cent_ref, shared_ref, packed_ref, *refs
):
    new_ref = refs[-1]
    out_refs = refs[-5:-1]
    owners, _, width = shared_ref.shape
    head_size = width // 4
    owned = cent_ref.shape[1]
    tok_rows, heads = base_ref.shape
    step = pl.program_id(0)
    packed = packed_ref[...].reshape(owners * PACKED, width)
    arrived = shared_ref[...].astype(F32)
    for at in range(2):
        here = iota((tok_rows, heads), 1) == step * 2 + at
        base = jnp.sum(jnp.where(here, base_ref[...], 0), axis=1, keepdims=True)
        over = jnp.sum(jnp.where(here, over_ref[...], 0), axis=1, keepdims=True)
        take = iota((tok_rows, owners * SHARED), 1) == base
        take_over = iota((tok_rows, owners * PACKED), 1) == over
        mine = arrived[:, at * SHARED : (at + 1) * SHARED, :].reshape(owners * SHARED, width)
        rows = dot(jnp.where(take, 1.0, 0.0).astype(BF16), mine.astype(BF16))
        rows = rows + dot(jnp.where(take_over, 1.0, 0.0).astype(BF16), packed)
        rows = rows.astype(BF16)
        for which, out_ref in enumerate(out_refs):
            out_ref[:, at * head_size : (at + 1) * head_size] = rows[
                :, which * head_size : (which + 1) * head_size
            ]
        turned_by = TURN_BY * (first_head + step * 2 + at)
        tile = packed_ref[lax.rem(me_ref[0] + turned_by, owners)].astype(F32)
        spare = iota((PACKED, width), 0) >= PACKED - 2
        key_sums = jnp.sum(jnp.where(spare, tile, 0.0), axis=0, keepdims=True)
        for slot in range(owned):
            blend = DECAY_RATE * cent_ref[at, slot : slot + 1, :]
            blend += (1.0 - DECAY_RATE) * key_sums[:, slot * head_size : (slot + 1) * head_size]
            new_ref[at, slot : slot + 1, :] = blend / jnp.sqrt(
                jnp.mean(blend * blend, axis=-1, keepdims=True) + 1e-06
            )


def params():
    return pltpu.CompilerParams(vmem_limit_bytes=VMEM_BYTES)


def dense(queries, keys, values, out_grad, cluster_ids, cluster_slot, centroids):
    seq_count = lax.axis_size("seq")
    local_heads, tok_rows = cluster_ids.shape[:2]
    cluster_count = cluster_slot.shape[0]
    owned = cluster_count // seq_count
    head_size = centroids.shape[2]
    heads = local_heads // CHUNKS
    block_rows = owned * CAP
    width = 4 * head_size
    slot_count = seq_count * CAP
    sent = jax.ShapeDtypeStruct((seq_count, heads * block_rows, width), BF16)
    sent_bytes = seq_count * heads * block_rows * width * 2
    ids_rows = cluster_ids.reshape(local_heads, 1, tok_rows)
    slot_row = cluster_slot.reshape(1, cluster_count)
    block = pl.BlockSpec((seq_count, block_rows, width), lambda h: (0, h, 0))

    def exchange(rows):
        return lax.all_to_all(rows, "seq", split_axis=0, concat_axis=0, tiled=True)

    def pack(chunk):
        column = pl.BlockSpec((tok_rows, head_size), lambda h: (0, chunk * heads + h))
        return pl.pallas_call(
            pack_kernel,
            grid=(heads,),
            in_specs=[
                pl.BlockSpec((1, 1, tok_rows), lambda h: (chunk * heads + h, 0, 0)),
                pl.BlockSpec((1, cluster_count), lambda h: (0, 0)),
                column,
                column,
                column,
                column,
            ],
            out_specs=[block, pl.BlockSpec((1, 1, tok_rows), lambda h: (h, 0, 0))],
            out_shape=[sent, jax.ShapeDtypeStruct((heads, 1, tok_rows), jnp.int32)],
            scratch_shapes=[pltpu.VMEM((tok_rows, tok_rows), BF16)],
            compiler_params=params(),
            cost_estimate=pl.CostEstimate(
                flops=heads * 2 * 1024 * 512 * 640, bytes_accessed=2 * sent_bytes, transcendentals=0
            ),
            name="pack",
        )(ids_rows, slot_row, queries, keys, values, out_grad)

    def own(chunk, received):
        return pl.pallas_call(
            owner_kernel,
            grid=(heads,),
            in_specs=[
                block,
                pl.BlockSpec((1, owned, head_size), lambda h: (chunk * heads + h, 0, 0)),
            ],
            out_specs=[block, pl.BlockSpec((1, owned, head_size), lambda h: (h, 0, 0))],
            out_shape=[sent, jax.ShapeDtypeStruct((heads, owned, head_size), F32)],
            scratch_shapes=[
                pltpu.VMEM((16 * block_rows, 16 * block_rows), BF16),
                pltpu.VMEM((slot_count, slot_count), F32),
                pltpu.VMEM((owned, slot_count, width), BF16),
                pltpu.VMEM((owned, slot_count, width), BF16),
            ],
            compiler_params=params(),
            cost_estimate=pl.CostEstimate(
                flops=heads * owned * 7 * 2 * slot_count * slot_count * head_size,
                bytes_accessed=2 * sent_bytes,
                transcendentals=heads * owned * slot_count * slot_count,
            ),
            name="own",
        )(received, centroids)

    def unpack(chunk, flat_cols, returned, previous):
        column = pl.BlockSpec((tok_rows, head_size), lambda h: (0, chunk * heads + h))
        whole = jax.ShapeDtypeStruct((tok_rows, local_heads * head_size), BF16)

        def kernel(*refs):
            unpack_kernel(chunk, *refs)

        return pl.pallas_call(
            kernel,
            grid=(heads,),
            in_specs=[pl.BlockSpec((tok_rows, heads), lambda h: (0, 0)), block]
            + [pl.BlockSpec(memory_space=pl.ANY)] * len(previous),
            out_specs=[column] * 4,
            out_shape=[whole] * 4,
            input_output_aliases={2 + i: i for i in range(len(previous))},
            compiler_params=params(),
            cost_estimate=pl.CostEstimate(
                flops=heads * 2 * 1024 * 512 * 512, bytes_accessed=2 * sent_bytes, transcendentals=0
            ),
            name="unpack",
        )(flat_cols, returned, *previous)

    packed = [pack(chunk) for chunk in range(CHUNKS)]
    received = [exchange(rows) for rows, _ in packed]
    owned_now = [own(chunk, rows) for chunk, rows in enumerate(received)]
    returned = [exchange(rows) for rows, _ in owned_now]
    outs = ()
    for chunk in range(CHUNKS):
        flat_cols = packed[chunk][1].reshape(heads, tok_rows).T
        outs = unpack(chunk, flat_cols, returned[chunk], tuple(outs))
    new_centroids = jnp.concatenate([new for _, new in owned_now], axis=0)
    return (*outs, new_centroids)


def body(queries, keys, values, out_grad, cluster_ids, cluster_slot, centroids):
    seq_count = lax.axis_size("seq")
    local_heads, tok_rows = cluster_ids.shape[:2]
    cluster_count = cluster_slot.shape[0]
    owned, head_size = centroids.shape[1:]
    heads = local_heads // CHUNKS
    width = 4 * head_size
    pair_rows = 2 * SHARED
    steps = heads // 2
    send_rows = steps * pair_rows + PACKED
    slot_count = seq_count * CAP
    problems = 2 * owned
    block_bytes = seq_count * pair_rows * width * 2
    sent_shape = jax.ShapeDtypeStruct((seq_count, send_rows, width), BF16)
    ids_rows = cluster_ids.reshape(local_heads, 1, tok_rows)
    slot_row = cluster_slot.reshape(1, cluster_count)
    me = lax.axis_index("seq").reshape(1)

    def cost(flops, exps=0):
        return pl.CostEstimate(
            flops=flops, bytes_accessed=2 * (steps + 1) * block_bytes, transcendentals=exps
        )

    shared_block = pl.BlockSpec((seq_count, pair_rows, width), lambda s: (0, s, 0))
    packed_block = pl.BlockSpec((seq_count, PACKED, width), lambda s: (0, steps, 0))
    whole_block = pl.BlockSpec((seq_count, send_rows, width), lambda s: (0, 0, 0))
    me_spec = pl.BlockSpec(memory_space=pltpu.SMEM)

    def route(chunk):
        row_shape = jax.ShapeDtypeStruct((heads, 1, tok_rows), jnp.int32)
        rows_block = pl.BlockSpec((heads, 1, tok_rows), lambda s: (0, 0, 0))
        return pl.pallas_call(
            functools.partial(route_kernel, chunk * heads),
            grid=(1,),
            in_specs=[
                pl.BlockSpec((heads, 1, tok_rows), lambda s: (chunk, 0, 0)),
                pl.BlockSpec((1, cluster_count), lambda s: (0, 0)),
            ],
            out_specs=[
                rows_block,
                rows_block,
                pl.BlockSpec((seq_count, head_size), lambda s: (0, 0)),
            ],
            out_shape=[
                row_shape,
                row_shape,
                jax.ShapeDtypeStruct((seq_count, head_size), BF16),
            ],
            compiler_params=params(),
            name="route",
        )(ids_rows, slot_row)

    def pack(chunk, base_rows, over_rows, header):
        column = pl.BlockSpec((tok_rows, 2 * head_size), lambda s: (0, chunk * steps + s))
        row_block = pl.BlockSpec((2, 1, tok_rows), lambda s: (s, 0, 0))
        return pl.pallas_call(
            pack_rows_kernel,
            grid=(steps,),
            in_specs=[
                row_block,
                row_block,
                pl.BlockSpec((seq_count, head_size), lambda s: (0, 0)),
            ]
            + [column] * 4,
            out_specs=whole_block,
            out_shape=sent_shape,
            scratch_shapes=[pltpu.VMEM((seq_count * PACKED, width), F32)],
            compiler_params=params(),
            cost_estimate=cost(2 * heads * 1536 * tok_rows * width),
            name="pack_rows",
        )(base_rows, over_rows, header, queries, keys, values, out_grad)

    def own(chunk, received):
        return pl.pallas_call(
            functools.partial(own_rows_kernel, chunk * heads),
            grid=(steps,),
            in_specs=[me_spec, shared_block, packed_block],
            out_specs=[whole_block, pl.BlockSpec((8, head_size), lambda s: (0, 0))],
            out_shape=[sent_shape, jax.ShapeDtypeStruct((8, head_size), F32)],
            scratch_shapes=[
                pltpu.VMEM(
                    (seq_count // 16, problems * 16 * CAP, 16 * (pair_rows + PACKED)), BF16
                ),
                pltpu.VMEM((slot_count, slot_count), F32),
                pltpu.VMEM((problems, slot_count, width), BF16),
                pltpu.VMEM((problems, slot_count, width), BF16),
                pltpu.VMEM((problems, head_size), F32),
            ],
            compiler_params=params(),
            cost_estimate=cost(
                steps * problems * 16 * 2 * slot_count * slot_count * head_size,
                steps * problems * slot_count * slot_count,
            ),
            name="own_rows",
        )(me, received, received)

    def unpack(chunk, base_rows, over_rows, returned, previous):
        column = pl.BlockSpec((tok_rows, 2 * head_size), lambda s: (0, chunk * steps + s))
        routes_block = pl.BlockSpec((tok_rows, heads), lambda s: (0, 0))
        centroid_block = pl.BlockSpec(
            (2, owned, head_size), lambda s: (chunk * steps + s, 0, 0)
        )
        return pl.pallas_call(
            functools.partial(unpack_rows_kernel, chunk * heads),
            grid=(steps,),
            in_specs=[
                me_spec,
                routes_block,
                routes_block,
                centroid_block,
                shared_block,
                packed_block,
            ]
            + [pl.BlockSpec(memory_space=pl.ANY)] * len(previous),
            out_specs=[column] * 4 + [centroid_block],
            out_shape=[jax.ShapeDtypeStruct((tok_rows, local_heads * head_size), BF16)] * 4
            + [jax.ShapeDtypeStruct(centroids.shape, F32)],
            input_output_aliases={6 + at: at for at in range(len(previous))},
            compiler_params=params(),
            cost_estimate=cost(2 * heads * 1536 * tok_rows * width),
            name="unpack_rows",
        )(
            me,
            base_rows.reshape(heads, tok_rows).T,
            over_rows.reshape(heads, tok_rows).T,
            centroids,
            returned,
            returned,
            *previous,
        )

    def exchange(rows):
        return lax.all_to_all(rows, "seq", split_axis=0, concat_axis=0, tiled=True)

    routes = [route(chunk) for chunk in range(CHUNKS)]
    received = [exchange(pack(chunk, *routes[chunk])) for chunk in range(CHUNKS)]
    owned_now = [own(chunk, received[chunk]) for chunk in range(CHUNKS)]
    returned = [exchange(back) for back, _ in owned_now]
    outs = ()
    for chunk in range(CHUNKS):
        outs = unpack(chunk, *routes[chunk][:2], returned[chunk], tuple(outs))

    peak = functools.reduce(jnp.maximum, [seen[0:1] for _, seen in owned_now])
    swap = [(at, 1 - at) for at in range(2)]
    peak = jnp.maximum(peak, lax.ppermute(peak, "head", swap))[0, PEAK_LANE]

    def lacking(state):
        return state[0]

    def again(state):
        full = dense(queries, keys, values, out_grad, cluster_ids, cluster_slot, centroids)
        return (jnp.zeros((), jnp.bool_), *full)

    state = lax.while_loop(lacking, again, (peak > PACKED - SPARE, *outs))
    return state[1:]


def solution(mesh):
    return jax.shard_map(
        body,
        mesh=mesh,
        in_specs=(
            P("seq", "head"),
            P("seq", "head"),
            P("seq", "head"),
            P("seq", "head"),
            P("head", "seq", None),
            P(),
            P("head", "seq", None),
        ),
        out_specs=(
            P("seq", "head"),
            P("seq", "head"),
            P("seq", "head"),
            P("seq", "head"),
            P("head", "seq", None),
        ),
        check_vma=False,
    )
```

```python
import functools
import math

import jax
import jax.numpy as jnp
from jax import lax
from jax.experimental import pallas as pl
from jax.experimental.pallas import tpu as pltpu
from jax.sharding import PartitionSpec as P

CAP = 4
DECAY_RATE = 0.9
MASKED = -1e30
ABSENT = 64.0
CHUNKS = 2
SHARED = 8
PACKED = 16
SPARE = 2
PEAK_LANE = 127
TURN_BY = 8
VMEM_BYTES = 60 * 1024 * 1024

F32 = jnp.float32
BF16 = jnp.bfloat16
CONTRACT_LAST = (((1,), (1,)), ((), ()))
CONTRACT_FIRST = (((0,), (0,)), ((), ()))


def iota(shape, dim):
    return lax.broadcasted_iota(jnp.int32, shape, dim)


def dot(left, right):
    return jnp.dot(left, right, preferred_element_type=F32)


def pack_kernel(ids_ref, slot_ref, q_ref, k_ref, v_ref, g_ref, send_ref, flat_ref, earlier_ref):
    tok_rows = ids_ref.shape[2]
    cluster_count = slot_ref.shape[1]
    slot_rows = cluster_count * CAP

    @pl.when(pl.program_id(0) == 0)
    def _():
        earlier_ref[...] = (iota((tok_rows, tok_rows), 0) < iota((tok_rows, tok_rows), 1)).astype(
            F32
        ).astype(BF16)

    ids_row = ids_ref[0]
    member = iota((cluster_count, tok_rows), 0) == ids_row
    member_f = jnp.where(member, 1.0, 0.0)
    member_low = member_f.astype(BF16)
    slots_low = jnp.broadcast_to(slot_ref[...].astype(F32), (8, cluster_count)).astype(BF16)
    slot_row = dot(slots_low, member_low)[0:1]
    rank_row = jnp.sum(dot(member_low, earlier_ref[...]) * member_f, axis=0, keepdims=True)
    flat_row = (slot_row * CAP + rank_row).astype(jnp.int32)
    flat_ref[0] = flat_row
    place = jnp.where(iota((slot_rows, tok_rows), 0) == flat_row, 1.0, 0.0).astype(BF16)
    ones = jnp.ones((tok_rows, 128), BF16)
    head_size = q_ref.shape[1]
    taken = dot(place, ones)
    out_shape = send_ref.shape[:2] + (head_size,)

    def put(at, rows):
        send_ref[:, :, at * head_size : (at + 1) * head_size] = rows.astype(BF16).reshape(out_shape)

    put(0, dot(place, q_ref[...]))
    put(1, dot(place, k_ref[...]) + (1.0 - taken) * ABSENT)
    put(2, dot(place, v_ref[...]))
    put(3, dot(place, g_ref[...]))


def owner_kernel(recv_ref, cent_ref, back_ref, new_ref, turn_ref, causal_ref, rows_ref, grads_ref):
    source_count, block_rows, width = recv_ref.shape
    head_size = width // 4
    owned = block_rows // CAP
    slot_count = source_count * CAP
    group_rows = 16 * block_rows
    groups = source_count // 16
    part = 16 * CAP
    score_scale = 1.0 / math.sqrt(head_size)

    @pl.when(pl.program_id(0) == 0)
    def _():
        row_at = iota((group_rows, group_rows), 0)
        col_at = iota((group_rows, group_rows), 1)
        cluster_of = row_at // part
        source_of = (row_at % part) // CAP
        from_row = source_of * block_rows + cluster_of * CAP + row_at % CAP
        turn_ref[...] = jnp.where(from_row == col_at, 1.0, 0.0).astype(BF16)
        causal_ref[...] = jnp.where(
            iota((slot_count, slot_count), 1) <= iota((slot_count, slot_count), 0), 0.0, MASKED
        )

    turn = turn_ref[...]
    @pl.loop(0, groups)
    def _(group):
        arrived = recv_ref[pl.ds(group * 16, 16)].reshape(group_rows, width)
        turned = dot(turn, arrived).astype(BF16)
        at_row = pl.multiple_of(group * part, part)
        rows_ref[:, pl.ds(at_row, part), :] = turned.reshape(owned, part, width)

    first_lane = jnp.where(iota((8, head_size), 1) == 0, 1.0, 0.0).astype(BF16)
    @pl.loop(0, owned)
    def _(cluster):
        q = rows_ref[cluster, :, 0:head_size]
        k = rows_ref[cluster, :, head_size : 2 * head_size]
        v = rows_ref[cluster, :, 2 * head_size : 3 * head_size]
        g = rows_ref[cluster, :, 3 * head_size : 4 * head_size]
        marks = lax.dot_general(first_lane, k, CONTRACT_LAST, preferred_element_type=F32)
        present = marks < ABSENT / 2
        bias = jnp.where(present, 0.0, MASKED)[0:1]
        scores = lax.dot_general(q, k, CONTRACT_LAST, preferred_element_type=F32) * score_scale
        scores = scores + (causal_ref[...] + bias)
        weights = jnp.exp(scores - jnp.max(scores, axis=-1, keepdims=True))
        probs = weights / jnp.sum(weights, axis=-1, keepdims=True)
        probs_low = probs.astype(BF16)
        out = dot(probs_low, v).astype(BF16)
        grad_prob = lax.dot_general(g, v, CONTRACT_LAST, preferred_element_type=F32)
        delta = jnp.sum(g.astype(F32) * out.astype(F32), axis=-1, keepdims=True)
        grad_score = (probs * (grad_prob - delta) * score_scale).astype(BF16)
        grad_q = dot(grad_score, k)
        grad_k = lax.dot_general(grad_score, q, CONTRACT_FIRST, preferred_element_type=F32)
        grad_v = lax.dot_general(probs_low, g, CONTRACT_FIRST, preferred_element_type=F32)
        grads_ref[cluster, :, 0:head_size] = out
        grads_ref[cluster, :, head_size : 2 * head_size] = grad_q.astype(BF16)
        grads_ref[cluster, :, 2 * head_size : 3 * head_size] = grad_k.astype(BF16)
        grads_ref[cluster, :, 3 * head_size : 4 * head_size] = grad_v.astype(BF16)
        key_sums = dot(jnp.where(present, 1.0, 0.0).astype(BF16), k)[0:1]
        blend = DECAY_RATE * cent_ref[0, pl.ds(cluster, 1), :] + (1.0 - DECAY_RATE) * key_sums
        new_ref[0, pl.ds(cluster, 1), :] = blend / jnp.sqrt(
            jnp.mean(blend * blend, axis=-1, keepdims=True) + 1e-06
        )

    @pl.loop(0, groups)
    def _(group):
        at_row = pl.multiple_of(group * part, part)
        leaving = grads_ref[:, pl.ds(at_row, part), :].reshape(group_rows, width)
        turned = lax.dot_general(turn, leaving, CONTRACT_FIRST, preferred_element_type=F32)
        back_ref[pl.ds(group * 16, 16)] = turned.astype(BF16).reshape(16, block_rows, width)


def unpack_kernel(chunk, flat_ref, ret_ref, *refs):
    out_refs = refs[-4:]
    sources, block_rows, width = ret_ref.shape
    head_size = width // 4
    tok_rows, heads = flat_ref.shape
    slot_rows = sources * block_rows
    here = iota((tok_rows, heads), 1) == pl.program_id(0)
    flat_col = jnp.sum(jnp.where(here, flat_ref[...], 0), axis=1, keepdims=True)
    take = jnp.where(iota((tok_rows, slot_rows), 1) == flat_col, 1.0, 0.0).astype(BF16)
    rows = dot(take, ret_ref[...].reshape(slot_rows, width)).astype(BF16)
    for at, out_ref in enumerate(out_refs):
        out_ref[...] = rows[:, at * head_size : (at + 1) * head_size]


def find_rows(first_head, ids_ref, slot_ref, base_ref, over_ref, header_ref):
    heads, _, tok_rows = ids_ref.shape
    cluster_count = slot_ref.shape[1]
    owners, lanes = header_ref.shape
    earlier = jnp.where(
        iota((tok_rows, tok_rows), 0) < iota((tok_rows, tok_rows), 1), 1.0, 0.0
    ).astype(BF16)
    slots_low = jnp.broadcast_to(slot_ref[...].astype(F32), (8, cluster_count)).astype(BF16)
    members = [
        jnp.where(iota((cluster_count, tok_rows), 0) == ids_ref[head], 1.0, 0.0)
        for head in range(heads)
    ]
    member_low = jnp.concatenate(members, axis=0).astype(BF16)
    earlier_members = dot(member_low, earlier)
    owner_of, tag_of, here_of = [], [], []
    for head in range(heads):
        own = slice(head * cluster_count, (head + 1) * cluster_count)
        slot = dot(slots_low, member_low[own])[0:1].astype(jnp.int32)
        rank = jnp.sum(earlier_members[own] * members[head], axis=0, keepdims=True)
        owner = (slot // CAP + TURN_BY * (first_head + head)) % owners
        owner_of.append(owner)
        tag_of.append((head * CAP + slot % CAP) * CAP + rank.astype(jnp.int32))
        here_of.append(jnp.where(iota((owners, tok_rows), 0) == owner, 1.0, 0.0))
    before_all = dot(jnp.concatenate(here_of, axis=0).astype(BF16), earlier)
    filled = jnp.zeros((owners, 1), F32)
    header = jnp.zeros((owners, lanes), F32)
    for head in range(heads):
        here_f = here_of[head]
        before = before_all[head * owners : (head + 1) * owners]
        place = jnp.sum(before * here_f, axis=0, keepdims=True).astype(jnp.int32)
        late = jnp.sum((before + filled) * here_f, axis=0, keepdims=True)
        late = late.astype(jnp.int32) - SHARED
        filled = filled + jnp.maximum(jnp.sum(here_f, axis=1, keepdims=True) - SHARED, 0.0)
        fits = place < SHARED
        packs = (late < PACKED - SPARE) & (place >= SHARED)
        base_ref[head] = jnp.where(fits, owner_of[head] * SHARED + place, -1)
        over_ref[head] = jnp.where(packs, owner_of[head] * PACKED + late, -1)
        lane = jnp.where(fits, head * SHARED + place, jnp.where(packs, heads * SHARED + late, -1))
        named = (here_f * (tag_of[head] + 1).astype(F32)).astype(BF16)
        lane_at = jnp.where(iota((lanes, tok_rows), 0) == lane, 1.0, 0.0).astype(BF16)
        header = header + lax.dot_general(
            named, lane_at, CONTRACT_LAST, preferred_element_type=F32
        )
    peak = jnp.max(filled, axis=0, keepdims=True)
    header_ref[...] = jnp.where(iota((owners, lanes), 1) == PEAK_LANE, peak, header).astype(BF16)


def token_rows(refs, at, head_size):
    lanes = slice(at * head_size, (at + 1) * head_size)
    return jnp.concatenate([ref[:, lanes] for ref in refs], axis=1)


def pack_rows_kernel(
    first_head,
    ids_ref,
    slot_ref,
    q_ref,
    k_ref,
    v_ref,
    g_ref,
    send_ref,
    base_ref,
    over_ref,
    header_ref,
    total_ref,
):
    owners, send_rows, width = send_ref.shape
    tok_rows = q_ref.shape[0]
    head_size = width // 4
    step = pl.program_id(0)

    @pl.when(step == 0)
    def _():
        find_rows(first_head, ids_ref, slot_ref, base_ref, over_ref, header_ref)

    rows = [token_rows((q_ref, k_ref, v_ref, g_ref), at, head_size) for at in range(2)]
    halves = []
    for at in range(2):
        place = iota((owners * SHARED, tok_rows), 0) == base_ref[step * 2 + at]
        placed = dot(jnp.where(place, 1.0, 0.0).astype(BF16), rows[at])
        halves.append(placed.reshape(owners, SHARED, width))
    at_row = pl.multiple_of(step * 2 * SHARED, 2 * SHARED)
    shared = jnp.concatenate(halves, axis=1).astype(BF16)
    send_ref[:, pl.ds(at_row, 2 * SHARED), :] = shared

    places = [
        jnp.where(iota((owners * PACKED, tok_rows), 0) == over_ref[step * 2 + at], 1.0, 0.0).astype(BF16)
        for at in range(2)
    ]
    added = dot(jnp.concatenate(places, axis=1), jnp.concatenate(rows, axis=0))

    @pl.when(step == 0)
    def _():
        total_ref[...] = added

    @pl.when(step == pl.num_programs(0) - 1)
    def _():
        total = total_ref[...] + added
        last_row = iota((owners * PACKED, owners), 1) * PACKED + PACKED - 1
        to_last = jnp.where(iota((owners * PACKED, owners), 0) == last_row, 1.0, 0.0)
        tags = dot(to_last.astype(BF16), header_ref[...])
        total = jnp.concatenate([total[:, :head_size] + tags, total[:, head_size:]], axis=1)
        packed = total.astype(BF16).reshape(owners, PACKED, width)
        send_ref[:, send_rows - PACKED :, :] = packed


def own_rows_kernel(
    first_head,
    me_ref,
    shared_ref,
    over_ref,
    back_ref,
    peak_ref,
    turn_ref,
    causal_ref,
    rows_ref,
    grads_ref,
    sums_ref,
):
    sources, pair_rows, width = shared_ref.shape
    head_size = width // 4
    problems = rows_ref.shape[0]
    owned = problems // 2
    slot_count = sources * CAP
    bunch = 16
    groups = sources // bunch
    part = bunch * CAP
    shared_count = bunch * pair_rows
    packed_count = bunch * PACKED
    score_scale = 1.0 / math.sqrt(head_size)
    step = pl.program_id(0)
    steps = pl.num_programs(0)

    @pl.when(step == 0)
    def _():
        at = iota((slot_count, slot_count), 0)
        causal_ref[...] = jnp.where(iota((slot_count, slot_count), 1) <= at, 0.0, MASKED)

    header_of = jnp.where(
        iota((bunch, packed_count), 1) == iota((bunch, packed_count), 0) * PACKED + PACKED - 1,
        1.0,
        0.0,
    ).astype(BF16)

    def turns(header, first_lane, rows_each, used):
        count = bunch * rows_each
        lane = iota((head_size, count), 1) % rows_each
        match = (iota((head_size, count), 0) == lane + first_lane) & (lane < used)
        tags = dot(header, jnp.where(match, 1.0, 0.0).astype(BF16))
        source = iota((1, count), 1) // rows_each
        own = iota((bunch, count), 0) == source
        tag = jnp.sum(jnp.where(own, tags, 0.0), axis=0, keepdims=True).astype(jnp.int32) - 1
        mine = (tag >= 0) & (tag // (problems * CAP) == step)
        problem = (tag // CAP) % problems
        slot = jnp.where(mine, problem * part + source * CAP + tag % CAP, -1)
        hit = iota((problems * part, count), 0) == slot
        return jnp.where(hit, 1.0, 0.0).astype(BF16)

    ones = jnp.ones((shared_count + packed_count, head_size), BF16)
    peak_ref[...] = jnp.zeros(peak_ref.shape, F32)

    @pl.loop(0, groups)
    def _(group):
        from_sources = pl.ds(group * bunch, bunch)
        at_row = pl.multiple_of(group * part, part)
        packed = over_ref[from_sources].reshape(packed_count, width)
        shared = shared_ref[from_sources].reshape(shared_count, width)
        header = dot(header_of, packed[:, :head_size])
        peak_ref[...] = jnp.maximum(peak_ref[...], jnp.max(header, axis=0, keepdims=True))
        header = header.astype(BF16)
        turn = jnp.concatenate(
            [
                turns(header, step * pair_rows, pair_rows, pair_rows),
                turns(header, steps * pair_rows, PACKED, PACKED - SPARE),
            ],
            axis=1,
        )
        turn_ref[group] = turn
        turned = dot(turn, jnp.concatenate([shared, packed], axis=0))
        marked = turned[:, head_size : 2 * head_size] + (1.0 - dot(turn, ones)) * ABSENT
        turned = jnp.concatenate(
            [turned[:, :head_size], marked, turned[:, 2 * head_size :]], axis=1
        )
        rows_ref[:, pl.ds(at_row, part), :] = turned.astype(BF16).reshape(problems, part, width)

    first_lane = jnp.where(iota((8, head_size), 1) == 0, 1.0, 0.0).astype(BF16)

    def attend(problem):
        q = rows_ref[problem, :, 0:head_size]
        k = rows_ref[problem, :, head_size : 2 * head_size]
        v = rows_ref[problem, :, 2 * head_size : 3 * head_size]
        g = rows_ref[problem, :, 3 * head_size : 4 * head_size]
        marks = lax.dot_general(first_lane, k, CONTRACT_LAST, preferred_element_type=F32)
        present = marks < ABSENT / 2
        bias = jnp.where(present, 0.0, MASKED)[0:1]
        scores = lax.dot_general(q, k, CONTRACT_LAST, preferred_element_type=F32) * score_scale
        scores = scores + (causal_ref[...] + bias)
        weights = jnp.exp(scores - jnp.max(scores, axis=-1, keepdims=True))
        probs = weights / jnp.sum(weights, axis=-1, keepdims=True)
        probs_low = probs.astype(BF16)
        out = dot(probs_low, v).astype(BF16)
        grad_prob = lax.dot_general(g, v, CONTRACT_LAST, preferred_element_type=F32)
        delta = jnp.sum(g.astype(F32) * out.astype(F32), axis=-1, keepdims=True)
        grad_score = (probs * (grad_prob - delta) * score_scale).astype(BF16)
        grad_q = dot(grad_score, k)
        grad_k = lax.dot_general(grad_score, q, CONTRACT_FIRST, preferred_element_type=F32)
        grad_v = lax.dot_general(probs_low, g, CONTRACT_FIRST, preferred_element_type=F32)
        grads_ref[problem, :, 0:head_size] = out
        grads_ref[problem, :, head_size : 2 * head_size] = grad_q.astype(BF16)
        grads_ref[problem, :, 2 * head_size : 3 * head_size] = grad_k.astype(BF16)
        grads_ref[problem, :, 3 * head_size : 4 * head_size] = grad_v.astype(BF16)
        sums = dot(jnp.where(present, 1.0, 0.0).astype(BF16), k)[0:1]
        sums_ref[pl.ds(problem, 1), :] = sums

    @pl.loop(0, problems // 2)
    def _(pair):
        attend(pair * 2)
        attend(pair * 2 + 1)

    rest = slice(back_ref.shape[1] - PACKED, back_ref.shape[1])
    at_pair = pl.multiple_of(step * pair_rows, pair_rows)

    @pl.loop(0, groups)
    def _(group):
        from_sources = pl.ds(group * bunch, bunch)
        at_row = pl.multiple_of(group * part, part)
        leaving = grads_ref[:, pl.ds(at_row, part), :].reshape(problems * part, width)
        sent = lax.dot_general(
            turn_ref[group], leaving, CONTRACT_FIRST, preferred_element_type=F32
        ).astype(BF16)
        back_ref[from_sources, pl.ds(at_pair, pair_rows), :] = sent[:shared_count].reshape(
            bunch, pair_rows, width
        )
        packed = sent[shared_count:].reshape(bunch, PACKED, width)

        @pl.when(step == 0)
        def _():
            back_ref[from_sources, rest, :] = packed

        @pl.when(step > 0)
        def _():
            back_ref[from_sources, rest, :] += packed

    for at in range(2):
        sums = jnp.concatenate(
            [sums_ref[at * owned + slot : at * owned + slot + 1, :] for slot in range(owned)],
            axis=1,
        )
        high = sums.astype(BF16).astype(F32)
        low = sums - high
        turned_by = TURN_BY * (first_head + step * 2 + at)
        home = lax.rem(me_ref[0] + sources * TURN_BY - turned_by, sources)
        row = iota((PACKED, width), 0)
        tile = back_ref[home, rest, :].astype(F32)
        tile = jnp.where(row == PACKED - 2, high, jnp.where(row == PACKED - 1, low, tile))
        back_ref[home, rest, :] = tile.astype(BF16)


def unpack_rows_kernel(
    first_head, me_ref, base_ref, over_ref, cent_ref, shared_ref, packed_ref, *refs
):
    new_ref = refs[-1]
    out_refs = refs[-5:-1]
    owners, _, width = shared_ref.shape
    head_size = width // 4
    owned = cent_ref.shape[1]
    tok_rows, heads = base_ref.shape
    step = pl.program_id(0)
    packed = packed_ref[...].reshape(owners * PACKED, width)
    arrived = shared_ref[...].astype(F32)
    for at in range(2):
        here = iota((tok_rows, heads), 1) == step * 2 + at
        base = jnp.sum(jnp.where(here, base_ref[...], 0), axis=1, keepdims=True)
        over = jnp.sum(jnp.where(here, over_ref[...], 0), axis=1, keepdims=True)
        take = iota((tok_rows, owners * SHARED), 1) == base
        take_over = iota((tok_rows, owners * PACKED), 1) == over
        mine = arrived[:, at * SHARED : (at + 1) * SHARED, :].reshape(owners * SHARED, width)
        rows = dot(jnp.where(take, 1.0, 0.0).astype(BF16), mine.astype(BF16))
        rows = rows + dot(jnp.where(take_over, 1.0, 0.0).astype(BF16), packed)
        rows = rows.astype(BF16)
        for which, out_ref in enumerate(out_refs):
            out_ref[:, at * head_size : (at + 1) * head_size] = rows[
                :, which * head_size : (which + 1) * head_size
            ]
        turned_by = TURN_BY * (first_head + step * 2 + at)
        tile = packed_ref[lax.rem(me_ref[0] + turned_by, owners)].astype(F32)
        spare = iota((PACKED, width), 0) >= PACKED - 2
        key_sums = jnp.sum(jnp.where(spare, tile, 0.0), axis=0, keepdims=True)
        for slot in range(owned):
            blend = DECAY_RATE * cent_ref[at, slot : slot + 1, :]
            blend += (1.0 - DECAY_RATE) * key_sums[:, slot * head_size : (slot + 1) * head_size]
            new_ref[at, slot : slot + 1, :] = blend / jnp.sqrt(
                jnp.mean(blend * blend, axis=-1, keepdims=True) + 1e-06
            )


def params():
    return pltpu.CompilerParams(vmem_limit_bytes=VMEM_BYTES)


def dense(queries, keys, values, out_grad, cluster_ids, cluster_slot, centroids):
    seq_count = lax.axis_size("seq")
    local_heads, tok_rows = cluster_ids.shape[:2]
    cluster_count = cluster_slot.shape[0]
    owned = cluster_count // seq_count
    head_size = centroids.shape[2]
    heads = local_heads
    block_rows = owned * CAP
    width = 4 * head_size
    slot_count = seq_count * CAP
    sent = jax.ShapeDtypeStruct((seq_count, heads * block_rows, width), BF16)
    sent_bytes = seq_count * heads * block_rows * width * 2
    ids_rows = cluster_ids.reshape(local_heads, 1, tok_rows)
    slot_row = cluster_slot.reshape(1, cluster_count)
    block = pl.BlockSpec((seq_count, block_rows, width), lambda h: (0, h, 0))

    def exchange(rows):
        return lax.all_to_all(rows, "seq", split_axis=0, concat_axis=0, tiled=True)

    def pack(chunk):
        column = pl.BlockSpec((tok_rows, head_size), lambda h: (0, chunk * heads + h))
        return pl.pallas_call(
            pack_kernel,
            grid=(heads,),
            in_specs=[
                pl.BlockSpec((1, 1, tok_rows), lambda h: (chunk * heads + h, 0, 0)),
                pl.BlockSpec((1, cluster_count), lambda h: (0, 0)),
                column,
                column,
                column,
                column,
            ],
            out_specs=[block, pl.BlockSpec((1, 1, tok_rows), lambda h: (h, 0, 0))],
            out_shape=[sent, jax.ShapeDtypeStruct((heads, 1, tok_rows), jnp.int32)],
            scratch_shapes=[pltpu.VMEM((tok_rows, tok_rows), BF16)],
            compiler_params=params(),
            cost_estimate=pl.CostEstimate(
                flops=heads * 2 * 1024 * 512 * 640, bytes_accessed=2 * sent_bytes, transcendentals=0
            ),
            name="pack",
        )(ids_rows, slot_row, queries, keys, values, out_grad)

    def own(chunk, received):
        return pl.pallas_call(
            owner_kernel,
            grid=(heads,),
            in_specs=[
                block,
                pl.BlockSpec((1, owned, head_size), lambda h: (chunk * heads + h, 0, 0)),
            ],
            out_specs=[block, pl.BlockSpec((1, owned, head_size), lambda h: (h, 0, 0))],
            out_shape=[sent, jax.ShapeDtypeStruct((heads, owned, head_size), F32)],
            scratch_shapes=[
                pltpu.VMEM((16 * block_rows, 16 * block_rows), BF16),
                pltpu.VMEM((slot_count, slot_count), F32),
                pltpu.VMEM((owned, slot_count, width), BF16),
                pltpu.VMEM((owned, slot_count, width), BF16),
            ],
            compiler_params=params(),
            cost_estimate=pl.CostEstimate(
                flops=heads * owned * 7 * 2 * slot_count * slot_count * head_size,
                bytes_accessed=2 * sent_bytes,
                transcendentals=heads * owned * slot_count * slot_count,
            ),
            name="own",
        )(received, centroids)

    def unpack(chunk, flat_cols, returned, previous):
        column = pl.BlockSpec((tok_rows, head_size), lambda h: (0, chunk * heads + h))
        whole = jax.ShapeDtypeStruct((tok_rows, local_heads * head_size), BF16)

        def kernel(*refs):
            unpack_kernel(chunk, *refs)

        return pl.pallas_call(
            kernel,
            grid=(heads,),
            in_specs=[pl.BlockSpec((tok_rows, heads), lambda h: (0, 0)), block]
            + [pl.BlockSpec(memory_space=pl.ANY)] * len(previous),
            out_specs=[column] * 4,
            out_shape=[whole] * 4,
            input_output_aliases={2 + i: i for i in range(len(previous))},
            compiler_params=params(),
            cost_estimate=pl.CostEstimate(
                flops=heads * 2 * 1024 * 512 * 512, bytes_accessed=2 * sent_bytes, transcendentals=0
            ),
            name="unpack",
        )(flat_cols, returned, *previous)

    packed = [pack(chunk) for chunk in range(1)]
    received = [exchange(rows) for rows, _ in packed]
    owned_now = [own(chunk, rows) for chunk, rows in enumerate(received)]
    returned = [exchange(rows) for rows, _ in owned_now]
    outs = ()
    for chunk in range(1):
        flat_cols = packed[chunk][1].reshape(heads, tok_rows).T
        outs = unpack(chunk, flat_cols, returned[chunk], tuple(outs))
    new_centroids = jnp.concatenate([new for _, new in owned_now], axis=0)
    return (*outs, new_centroids)


def body(queries, keys, values, out_grad, cluster_ids, cluster_slot, centroids):
    seq_count = lax.axis_size("seq")
    local_heads, tok_rows = cluster_ids.shape[:2]
    cluster_count = cluster_slot.shape[0]
    owned, head_size = centroids.shape[1:]
    heads = local_heads // CHUNKS
    width = 4 * head_size
    pair_rows = 2 * SHARED
    steps = heads // 2
    send_rows = steps * pair_rows + PACKED
    slot_count = seq_count * CAP
    problems = 2 * owned
    block_bytes = seq_count * pair_rows * width * 2
    sent_shape = jax.ShapeDtypeStruct((seq_count, send_rows, width), BF16)
    ids_rows = cluster_ids.reshape(local_heads, 1, tok_rows)
    slot_row = cluster_slot.reshape(1, cluster_count)
    me = lax.axis_index("seq").reshape(1)

    def cost(flops, exps=0):
        return pl.CostEstimate(
            flops=flops, bytes_accessed=2 * (steps + 1) * block_bytes, transcendentals=exps
        )

    shared_block = pl.BlockSpec((seq_count, pair_rows, width), lambda s: (0, s, 0))
    packed_block = pl.BlockSpec((seq_count, PACKED, width), lambda s: (0, steps, 0))
    whole_block = pl.BlockSpec((seq_count, send_rows, width), lambda s: (0, 0, 0))
    me_spec = pl.BlockSpec(memory_space=pltpu.SMEM)

    def pack(chunk):
        column = pl.BlockSpec((tok_rows, 2 * head_size), lambda s: (0, chunk * steps + s))
        row_shape = jax.ShapeDtypeStruct((heads, 1, tok_rows), jnp.int32)
        rows_block = pl.BlockSpec((heads, 1, tok_rows), lambda s: (0, 0, 0))
        return pl.pallas_call(
            functools.partial(pack_rows_kernel, chunk * heads),
            grid=(steps,),
            in_specs=[
                pl.BlockSpec((heads, 1, tok_rows), lambda s: (chunk, 0, 0)),
                pl.BlockSpec((1, cluster_count), lambda s: (0, 0)),
            ]
            + [column] * 4,
            out_specs=[whole_block, rows_block, rows_block],
            out_shape=[sent_shape, row_shape, row_shape],
            scratch_shapes=[
                pltpu.VMEM((seq_count, head_size), BF16),
                pltpu.VMEM((seq_count * PACKED, width), F32),
            ],
            compiler_params=params(),
            cost_estimate=cost(2 * heads * 1536 * tok_rows * width),
            name="pack_rows",
        )(ids_rows, slot_row, queries, keys, values, out_grad)

    def own(chunk, received):
        return pl.pallas_call(
            functools.partial(own_rows_kernel, chunk * heads),
            grid=(steps,),
            in_specs=[me_spec, shared_block, packed_block],
            out_specs=[whole_block, pl.BlockSpec((8, head_size), lambda s: (0, 0))],
            out_shape=[sent_shape, jax.ShapeDtypeStruct((8, head_size), F32)],
            scratch_shapes=[
                pltpu.VMEM(
                    (seq_count // 16, problems * 16 * CAP, 16 * (pair_rows + PACKED)), BF16
                ),
                pltpu.VMEM((slot_count, slot_count), F32),
                pltpu.VMEM((problems, slot_count, width), BF16),
                pltpu.VMEM((problems, slot_count, width), BF16),
                pltpu.VMEM((problems, head_size), F32),
            ],
            compiler_params=params(),
            cost_estimate=cost(
                steps * problems * 16 * 2 * slot_count * slot_count * head_size,
                steps * problems * slot_count * slot_count,
            ),
            name="own_rows",
        )(me, received, received)

    def unpack(chunk, base_rows, over_rows, returned, previous):
        column = pl.BlockSpec((tok_rows, 2 * head_size), lambda s: (0, chunk * steps + s))
        routes_block = pl.BlockSpec((tok_rows, heads), lambda s: (0, 0))
        centroid_block = pl.BlockSpec(
            (2, owned, head_size), lambda s: (chunk * steps + s, 0, 0)
        )
        return pl.pallas_call(
            functools.partial(unpack_rows_kernel, chunk * heads),
            grid=(steps,),
            in_specs=[
                me_spec,
                routes_block,
                routes_block,
                centroid_block,
                shared_block,
                packed_block,
            ]
            + [pl.BlockSpec(memory_space=pl.ANY)] * len(previous),
            out_specs=[column] * 4 + [centroid_block],
            out_shape=[pltpu.HBM((tok_rows, local_heads * head_size), BF16)] * 4
            + [pltpu.HBM(centroids.shape, F32)],
            input_output_aliases={6 + at: at for at in range(len(previous))},
            compiler_params=params(),
            cost_estimate=cost(2 * heads * 1536 * tok_rows * width),
            name="unpack_rows",
        )(
            me,
            base_rows.reshape(heads, tok_rows).T,
            over_rows.reshape(heads, tok_rows).T,
            centroids,
            returned,
            returned,
            *previous,
        )

    def exchange(rows):
        return lax.all_to_all(rows, "seq", split_axis=0, concat_axis=0, tiled=True)

    packed = [pack(chunk) for chunk in range(CHUNKS)]
    received = [exchange(rows) for rows, _, _ in packed]
    owned_now = [own(chunk, received[chunk]) for chunk in range(CHUNKS)]
    returned = [exchange(back) for back, _ in owned_now]
    outs = ()
    for chunk in range(CHUNKS):
        outs = unpack(chunk, *packed[chunk][1:], returned[chunk], tuple(outs))

    peak = functools.reduce(jnp.maximum, [seen[0:1] for _, seen in owned_now])
    swap = [(at, 1 - at) for at in range(2)]
    peak = jnp.maximum(peak, lax.ppermute(peak, "head", swap))[0, PEAK_LANE]

    def lacking(state):
        return state[0]

    def again(state):
        full = dense(queries, keys, values, out_grad, cluster_ids, cluster_slot, centroids)
        return (jnp.zeros((), jnp.bool_), *full)

    state = lax.while_loop(lacking, again, (peak > PACKED - SPARE, *outs))
    return state[1:]


def solution(mesh):
    return jax.shard_map(
        body,
        mesh=mesh,
        in_specs=(
            P("seq", "head"),
            P("seq", "head"),
            P("seq", "head"),
            P("seq", "head"),
            P("head", "seq", None),
            P(),
            P("head", "seq", None),
        ),
        out_specs=(
            P("seq", "head"),
            P("seq", "head"),
            P("seq", "head"),
            P("seq", "head"),
            P("head", "seq", None),
        ),
        check_vma=False,
    )
```

```python
import functools
import math

import jax
import jax.numpy as jnp
from jax import lax
from jax.experimental import pallas as pl
from jax.experimental.pallas import tpu as pltpu
from jax.sharding import PartitionSpec as P

CAP = 4
DECAY_RATE = 0.9
MASKED = -1e30
ABSENT = 64.0
CHUNKS = 2
SHARED = 8
PACKED = 16
SPARE = 2
PEAK_LANE = 127
TURN_BY = 8
VMEM_BYTES = 63 * 1024 * 1024

F32 = jnp.float32
BF16 = jnp.bfloat16
CONTRACT_LAST = (((1,), (1,)), ((), ()))
CONTRACT_FIRST = (((0,), (0,)), ((), ()))


def iota(shape, dim):
    return lax.broadcasted_iota(jnp.int32, shape, dim)


def dot(left, right):
    return jnp.dot(left, right, preferred_element_type=F32)


def pack_kernel(ids_ref, slot_ref, q_ref, k_ref, v_ref, g_ref, send_ref, flat_ref, earlier_ref):
    tok_rows = ids_ref.shape[2]
    cluster_count = slot_ref.shape[1]
    slot_rows = cluster_count * CAP

    @pl.when(pl.program_id(0) == 0)
    def _():
        earlier_ref[...] = (iota((tok_rows, tok_rows), 0) < iota((tok_rows, tok_rows), 1)).astype(
            F32
        ).astype(BF16)

    ids_row = ids_ref[0]
    member = iota((cluster_count, tok_rows), 0) == ids_row
    member_f = jnp.where(member, 1.0, 0.0)
    member_low = member_f.astype(BF16)
    slots_low = jnp.broadcast_to(slot_ref[...].astype(F32), (8, cluster_count)).astype(BF16)
    slot_row = dot(slots_low, member_low)[0:1]
    rank_row = jnp.sum(dot(member_low, earlier_ref[...]) * member_f, axis=0, keepdims=True)
    flat_row = (slot_row * CAP + rank_row).astype(jnp.int32)
    flat_ref[0] = flat_row
    place = jnp.where(iota((slot_rows, tok_rows), 0) == flat_row, 1.0, 0.0).astype(BF16)
    ones = jnp.ones((tok_rows, 128), BF16)
    head_size = q_ref.shape[1]
    taken = dot(place, ones)
    out_shape = send_ref.shape[:2] + (head_size,)

    def put(at, rows):
        send_ref[:, :, at * head_size : (at + 1) * head_size] = rows.astype(BF16).reshape(out_shape)

    put(0, dot(place, q_ref[...]))
    put(1, dot(place, k_ref[...]) + (1.0 - taken) * ABSENT)
    put(2, dot(place, v_ref[...]))
    put(3, dot(place, g_ref[...]))


def owner_kernel(recv_ref, cent_ref, back_ref, new_ref, turn_ref, causal_ref, rows_ref, grads_ref):
    source_count, block_rows, width = recv_ref.shape
    head_size = width // 4
    owned = block_rows // CAP
    slot_count = source_count * CAP
    group_rows = 16 * block_rows
    groups = source_count // 16
    part = 16 * CAP
    score_scale = 1.0 / math.sqrt(head_size)

    @pl.when(pl.program_id(0) == 0)
    def _():
        row_at = iota((group_rows, group_rows), 0)
        col_at = iota((group_rows, group_rows), 1)
        cluster_of = row_at // part
        source_of = (row_at % part) // CAP
        from_row = source_of * block_rows + cluster_of * CAP + row_at % CAP
        turn_ref[...] = jnp.where(from_row == col_at, 1.0, 0.0).astype(BF16)
        causal_ref[...] = jnp.where(
            iota((slot_count, slot_count), 1) <= iota((slot_count, slot_count), 0), 0.0, MASKED
        )

    turn = turn_ref[...]
    @pl.loop(0, groups)
    def _(group):
        arrived = recv_ref[pl.ds(group * 16, 16)].reshape(group_rows, width)
        turned = dot(turn, arrived).astype(BF16)
        at_row = pl.multiple_of(group * part, part)
        rows_ref[:, pl.ds(at_row, part), :] = turned.reshape(owned, part, width)

    first_lane = jnp.where(iota((8, head_size), 1) == 0, 1.0, 0.0).astype(BF16)
    @pl.loop(0, owned)
    def _(cluster):
        q = rows_ref[cluster, :, 0:head_size]
        k = rows_ref[cluster, :, head_size : 2 * head_size]
        v = rows_ref[cluster, :, 2 * head_size : 3 * head_size]
        g = rows_ref[cluster, :, 3 * head_size : 4 * head_size]
        marks = lax.dot_general(first_lane, k, CONTRACT_LAST, preferred_element_type=F32)
        present = marks < ABSENT / 2
        bias = jnp.where(present, 0.0, MASKED)[0:1]
        scores = lax.dot_general(q, k, CONTRACT_LAST, preferred_element_type=F32) * score_scale
        scores = scores + (causal_ref[...] + bias)
        weights = jnp.exp(scores - jnp.max(scores, axis=-1, keepdims=True))
        probs = weights / jnp.sum(weights, axis=-1, keepdims=True)
        probs_low = probs.astype(BF16)
        out = dot(probs_low, v).astype(BF16)
        grad_prob = lax.dot_general(g, v, CONTRACT_LAST, preferred_element_type=F32)
        delta = jnp.sum(g.astype(F32) * out.astype(F32), axis=-1, keepdims=True)
        grad_score = (probs * (grad_prob - delta) * score_scale).astype(BF16)
        grad_q = dot(grad_score, k)
        grad_k = lax.dot_general(grad_score, q, CONTRACT_FIRST, preferred_element_type=F32)
        grad_v = lax.dot_general(probs_low, g, CONTRACT_FIRST, preferred_element_type=F32)
        grads_ref[cluster, :, 0:head_size] = out
        grads_ref[cluster, :, head_size : 2 * head_size] = grad_q.astype(BF16)
        grads_ref[cluster, :, 2 * head_size : 3 * head_size] = grad_k.astype(BF16)
        grads_ref[cluster, :, 3 * head_size : 4 * head_size] = grad_v.astype(BF16)
        key_sums = dot(jnp.where(present, 1.0, 0.0).astype(BF16), k)[0:1]
        blend = DECAY_RATE * cent_ref[0, pl.ds(cluster, 1), :] + (1.0 - DECAY_RATE) * key_sums
        new_ref[0, pl.ds(cluster, 1), :] = blend / jnp.sqrt(
            jnp.mean(blend * blend, axis=-1, keepdims=True) + 1e-06
        )

    @pl.loop(0, groups)
    def _(group):
        at_row = pl.multiple_of(group * part, part)
        leaving = grads_ref[:, pl.ds(at_row, part), :].reshape(group_rows, width)
        turned = lax.dot_general(turn, leaving, CONTRACT_FIRST, preferred_element_type=F32)
        back_ref[pl.ds(group * 16, 16)] = turned.astype(BF16).reshape(16, block_rows, width)


def unpack_kernel(chunk, flat_ref, ret_ref, *refs):
    out_refs = refs[-4:]
    sources, block_rows, width = ret_ref.shape
    head_size = width // 4
    tok_rows, heads = flat_ref.shape
    slot_rows = sources * block_rows
    here = iota((tok_rows, heads), 1) == pl.program_id(0)
    flat_col = jnp.sum(jnp.where(here, flat_ref[...], 0), axis=1, keepdims=True)
    take = jnp.where(iota((tok_rows, slot_rows), 1) == flat_col, 1.0, 0.0).astype(BF16)
    rows = dot(take, ret_ref[...].reshape(slot_rows, width)).astype(BF16)
    for at, out_ref in enumerate(out_refs):
        out_ref[...] = rows[:, at * head_size : (at + 1) * head_size]


def find_rows(first_head, ids_ref, slot_ref, base_ref, over_ref, header_ref):
    heads, _, tok_rows = ids_ref.shape
    cluster_count = slot_ref.shape[1]
    owners, lanes = header_ref.shape
    earlier = jnp.where(
        iota((tok_rows, tok_rows), 0) < iota((tok_rows, tok_rows), 1), 1.0, 0.0
    ).astype(BF16)
    slots_low = jnp.broadcast_to(slot_ref[...].astype(F32), (8, cluster_count)).astype(BF16)
    members = [
        jnp.where(iota((cluster_count, tok_rows), 0) == ids_ref[head], 1.0, 0.0)
        for head in range(heads)
    ]
    member_low = jnp.concatenate(members, axis=0).astype(BF16)
    earlier_members = dot(member_low, earlier)
    owner_of, tag_of, here_of = [], [], []
    for head in range(heads):
        own = slice(head * cluster_count, (head + 1) * cluster_count)
        slot = dot(slots_low, member_low[own])[0:1].astype(jnp.int32)
        rank = jnp.sum(earlier_members[own] * members[head], axis=0, keepdims=True)
        owner = (slot // CAP + TURN_BY * (first_head + head)) % owners
        owner_of.append(owner)
        tag_of.append((head * CAP + slot % CAP) * CAP + rank.astype(jnp.int32))
        here_of.append(jnp.where(iota((owners, tok_rows), 0) == owner, 1.0, 0.0))
    before_all = dot(jnp.concatenate(here_of, axis=0).astype(BF16), earlier)
    filled = jnp.zeros((owners, 1), F32)
    header = jnp.zeros((owners, lanes), F32)
    for head in range(heads):
        here_f = here_of[head]
        before = before_all[head * owners : (head + 1) * owners]
        place = jnp.sum(before * here_f, axis=0, keepdims=True).astype(jnp.int32)
        late = jnp.sum((before + filled) * here_f, axis=0, keepdims=True)
        late = late.astype(jnp.int32) - SHARED
        filled = filled + jnp.maximum(jnp.sum(here_f, axis=1, keepdims=True) - SHARED, 0.0)
        fits = place < SHARED
        packs = (late < PACKED - SPARE) & (place >= SHARED)
        base_ref[head] = jnp.where(fits, owner_of[head] * SHARED + place, -1)
        over_ref[head] = jnp.where(packs, owner_of[head] * PACKED + late, -1)
        lane = jnp.where(fits, head * SHARED + place, jnp.where(packs, heads * SHARED + late, -1))
        named = (here_f * (tag_of[head] + 1).astype(F32)).astype(BF16)
        lane_at = jnp.where(iota((lanes, tok_rows), 0) == lane, 1.0, 0.0).astype(BF16)
        header = header + lax.dot_general(
            named, lane_at, CONTRACT_LAST, preferred_element_type=F32
        )
    peak = jnp.max(filled, axis=0, keepdims=True)
    header_ref[...] = jnp.where(iota((owners, lanes), 1) == PEAK_LANE, peak, header).astype(BF16)


def token_rows(refs, at, head_size):
    lanes = slice(at * head_size, (at + 1) * head_size)
    return jnp.concatenate([ref[:, lanes] for ref in refs], axis=1)


def pack_rows_kernel(
    first_head,
    ids_ref,
    slot_ref,
    q_ref,
    k_ref,
    v_ref,
    g_ref,
    send_ref,
    base_ref,
    over_ref,
    header_ref,
    total_ref,
):
    owners, send_rows, width = send_ref.shape
    tok_rows = q_ref.shape[0]
    head_size = width // 4
    step = pl.program_id(0)

    @pl.when(step == 0)
    def _():
        find_rows(first_head, ids_ref, slot_ref, base_ref, over_ref, header_ref)

    rows = [token_rows((q_ref, k_ref, v_ref, g_ref), at, head_size) for at in range(2)]
    halves = []
    for at in range(2):
        place = iota((owners * SHARED, tok_rows), 0) == base_ref[step * 2 + at]
        placed = dot(jnp.where(place, 1.0, 0.0).astype(BF16), rows[at])
        halves.append(placed.reshape(owners, SHARED, width))
    at_row = pl.multiple_of(step * 2 * SHARED, 2 * SHARED)
    shared = jnp.concatenate(halves, axis=1).astype(BF16)
    send_ref[:, pl.ds(at_row, 2 * SHARED), :] = shared

    places = [
        jnp.where(iota((owners * PACKED, tok_rows), 0) == over_ref[step * 2 + at], 1.0, 0.0).astype(BF16)
        for at in range(2)
    ]
    added = dot(jnp.concatenate(places, axis=1), jnp.concatenate(rows, axis=0))

    @pl.when(step == 0)
    def _():
        total_ref[...] = added

    @pl.when(step == pl.num_programs(0) - 1)
    def _():
        total = total_ref[...] + added
        last_row = iota((owners * PACKED, owners), 1) * PACKED + PACKED - 1
        to_last = jnp.where(iota((owners * PACKED, owners), 0) == last_row, 1.0, 0.0)
        tags = dot(to_last.astype(BF16), header_ref[...])
        total = jnp.concatenate([total[:, :head_size] + tags, total[:, head_size:]], axis=1)
        packed = total.astype(BF16).reshape(owners, PACKED, width)
        send_ref[:, send_rows - PACKED :, :] = packed


def own_rows_kernel(
    first_head,
    me_ref,
    shared_ref,
    over_ref,
    back_ref,
    peak_ref,
    turn_ref,
    causal_ref,
    rows_ref,
    grads_ref,
    sums_ref,
):
    sources, pair_rows, width = shared_ref.shape
    head_size = width // 4
    problems = rows_ref.shape[0]
    owned = problems // 2
    slot_count = sources * CAP
    bunch = 16
    groups = sources // bunch
    part = bunch * CAP
    shared_count = bunch * pair_rows
    packed_count = bunch * PACKED
    score_scale = 1.0 / math.sqrt(head_size)
    step = pl.program_id(0)
    steps = pl.num_programs(0)

    @pl.when(step == 0)
    def _():
        at = iota((slot_count, slot_count), 0)
        causal_ref[...] = jnp.where(iota((slot_count, slot_count), 1) <= at, 0.0, MASKED)

    header_of = jnp.where(
        iota((bunch, packed_count), 1) == iota((bunch, packed_count), 0) * PACKED + PACKED - 1,
        1.0,
        0.0,
    ).astype(BF16)

    def turns(header, first_lane, rows_each, used):
        count = bunch * rows_each
        lane = iota((head_size, count), 1) % rows_each
        match = (iota((head_size, count), 0) == lane + first_lane) & (lane < used)
        tags = dot(header, jnp.where(match, 1.0, 0.0).astype(BF16))
        source = iota((1, count), 1) // rows_each
        own = iota((bunch, count), 0) == source
        tag = jnp.sum(jnp.where(own, tags, 0.0), axis=0, keepdims=True).astype(jnp.int32) - 1
        mine = (tag >= 0) & (tag // (problems * CAP) == step)
        problem = (tag // CAP) % problems
        slot = jnp.where(mine, problem * part + source * CAP + tag % CAP, -1)
        hit = iota((problems * part, count), 0) == slot
        return jnp.where(hit, 1.0, 0.0).astype(BF16)

    ones = jnp.ones((shared_count + packed_count, head_size), BF16)
    peak_ref[...] = jnp.zeros(peak_ref.shape, F32)

    @pl.loop(0, groups)
    def _(group):
        from_sources = pl.ds(group * bunch, bunch)
        at_row = pl.multiple_of(group * part, part)
        packed = over_ref[from_sources].reshape(packed_count, width)
        shared = shared_ref[from_sources].reshape(shared_count, width)
        header = dot(header_of, packed[:, :head_size])
        peak_ref[...] = jnp.maximum(peak_ref[...], jnp.max(header, axis=0, keepdims=True))
        header = header.astype(BF16)
        turn = jnp.concatenate(
            [
                turns(header, step * pair_rows, pair_rows, pair_rows),
                turns(header, steps * pair_rows, PACKED, PACKED - SPARE),
            ],
            axis=1,
        )
        turn_ref[group] = turn
        turned = dot(turn, jnp.concatenate([shared, packed], axis=0))
        marked = turned[:, head_size : 2 * head_size] + (1.0 - dot(turn, ones)) * ABSENT
        turned = jnp.concatenate(
            [turned[:, :head_size], marked, turned[:, 2 * head_size :]], axis=1
        )
        rows_ref[:, pl.ds(at_row, part), :] = turned.astype(BF16).reshape(problems, part, width)

    first_lane = jnp.where(iota((8, head_size), 1) == 0, 1.0, 0.0).astype(BF16)

    def attend(problem):
        q = rows_ref[problem, :, 0:head_size]
        k = rows_ref[problem, :, head_size : 2 * head_size]
        v = rows_ref[problem, :, 2 * head_size : 3 * head_size]
        g = rows_ref[problem, :, 3 * head_size : 4 * head_size]
        marks = lax.dot_general(first_lane, k, CONTRACT_LAST, preferred_element_type=F32)
        present = marks < ABSENT / 2
        bias = jnp.where(present, 0.0, MASKED)[0:1]
        scores = lax.dot_general(q, k, CONTRACT_LAST, preferred_element_type=F32) * score_scale
        scores = scores + (causal_ref[...] + bias)
        weights = jnp.exp(scores - jnp.max(scores, axis=-1, keepdims=True))
        probs = weights / jnp.sum(weights, axis=-1, keepdims=True)
        probs_low = probs.astype(BF16)
        out = dot(probs_low, v).astype(BF16)
        grad_prob = lax.dot_general(g, v, CONTRACT_LAST, preferred_element_type=F32)
        delta = jnp.sum(g.astype(F32) * out.astype(F32), axis=-1, keepdims=True)
        grad_score = (probs * (grad_prob - delta) * score_scale).astype(BF16)
        grad_q = dot(grad_score, k)
        grad_k = lax.dot_general(grad_score, q, CONTRACT_FIRST, preferred_element_type=F32)
        grad_v = lax.dot_general(probs_low, g, CONTRACT_FIRST, preferred_element_type=F32)
        grads_ref[problem, :, 0:head_size] = out
        grads_ref[problem, :, head_size : 2 * head_size] = grad_q.astype(BF16)
        grads_ref[problem, :, 2 * head_size : 3 * head_size] = grad_k.astype(BF16)
        grads_ref[problem, :, 3 * head_size : 4 * head_size] = grad_v.astype(BF16)
        sums = dot(jnp.where(present, 1.0, 0.0).astype(BF16), k)[0:1]
        sums_ref[pl.ds(problem, 1), :] = sums

    @pl.loop(0, problems // 2)
    def _(pair):
        attend(pair * 2)
        attend(pair * 2 + 1)

    rest = slice(back_ref.shape[1] - PACKED, back_ref.shape[1])
    at_pair = pl.multiple_of(step * pair_rows, pair_rows)

    @pl.loop(0, groups)
    def _(group):
        from_sources = pl.ds(group * bunch, bunch)
        at_row = pl.multiple_of(group * part, part)
        leaving = grads_ref[:, pl.ds(at_row, part), :].reshape(problems * part, width)
        sent = lax.dot_general(
            turn_ref[group], leaving, CONTRACT_FIRST, preferred_element_type=F32
        ).astype(BF16)
        back_ref[from_sources, pl.ds(at_pair, pair_rows), :] = sent[:shared_count].reshape(
            bunch, pair_rows, width
        )
        packed = sent[shared_count:].reshape(bunch, PACKED, width)

        @pl.when(step == 0)
        def _():
            back_ref[from_sources, rest, :] = packed

        @pl.when(step > 0)
        def _():
            back_ref[from_sources, rest, :] += packed

    for at in range(2):
        sums = jnp.concatenate(
            [sums_ref[at * owned + slot : at * owned + slot + 1, :] for slot in range(owned)],
            axis=1,
        )
        high = sums.astype(BF16).astype(F32)
        low = sums - high
        turned_by = TURN_BY * (first_head + step * 2 + at)
        home = lax.rem(me_ref[0] + sources * TURN_BY - turned_by, sources)
        row = iota((PACKED, width), 0)
        tile = back_ref[home, rest, :].astype(F32)
        tile = jnp.where(row == PACKED - 2, high, jnp.where(row == PACKED - 1, low, tile))
        back_ref[home, rest, :] = tile.astype(BF16)


def unpack_rows_kernel(
    first_head, me_ref, base_ref, over_ref, cent_ref, shared_ref, packed_ref, *refs
):
    new_ref = refs[-1]
    out_refs = refs[-5:-1]
    owners, _, width = shared_ref.shape
    head_size = width // 4
    owned = cent_ref.shape[1]
    tok_rows, heads = base_ref.shape
    step = pl.program_id(0)
    packed = packed_ref[...].reshape(owners * PACKED, width)
    arrived = shared_ref[...].astype(F32)
    for at in range(2):
        here = iota((tok_rows, heads), 1) == step * 2 + at
        base = jnp.sum(jnp.where(here, base_ref[...], 0), axis=1, keepdims=True)
        over = jnp.sum(jnp.where(here, over_ref[...], 0), axis=1, keepdims=True)
        take = iota((tok_rows, owners * SHARED), 1) == base
        take_over = iota((tok_rows, owners * PACKED), 1) == over
        mine = arrived[:, at * SHARED : (at + 1) * SHARED, :].reshape(owners * SHARED, width)
        rows = dot(jnp.where(take, 1.0, 0.0).astype(BF16), mine.astype(BF16))
        rows = rows + dot(jnp.where(take_over, 1.0, 0.0).astype(BF16), packed)
        rows = rows.astype(BF16)
        for which, out_ref in enumerate(out_refs):
            out_ref[:, at * head_size : (at + 1) * head_size] = rows[
                :, which * head_size : (which + 1) * head_size
            ]
        turned_by = TURN_BY * (first_head + step * 2 + at)
        tile = packed_ref[lax.rem(me_ref[0] + turned_by, owners)].astype(F32)
        spare = iota((PACKED, width), 0) >= PACKED - 2
        key_sums = jnp.sum(jnp.where(spare, tile, 0.0), axis=0, keepdims=True)
        for slot in range(owned):
            blend = DECAY_RATE * cent_ref[at, slot : slot + 1, :]
            blend += (1.0 - DECAY_RATE) * key_sums[:, slot * head_size : (slot + 1) * head_size]
            new_ref[at, slot : slot + 1, :] = blend / jnp.sqrt(
                jnp.mean(blend * blend, axis=-1, keepdims=True) + 1e-06
            )


def params():
    return pltpu.CompilerParams(vmem_limit_bytes=VMEM_BYTES)


def dense(queries, keys, values, out_grad, cluster_ids, cluster_slot, centroids):
    seq_count = lax.axis_size("seq")
    local_heads, tok_rows = cluster_ids.shape[:2]
    cluster_count = cluster_slot.shape[0]
    owned = cluster_count // seq_count
    head_size = centroids.shape[2]
    heads = local_heads
    block_rows = owned * CAP
    width = 4 * head_size
    slot_count = seq_count * CAP
    sent = jax.ShapeDtypeStruct((seq_count, heads * block_rows, width), BF16)
    sent_bytes = seq_count * heads * block_rows * width * 2
    ids_rows = cluster_ids.reshape(local_heads, 1, tok_rows)
    slot_row = cluster_slot.reshape(1, cluster_count)
    block = pl.BlockSpec((seq_count, block_rows, width), lambda h: (0, h, 0))

    def exchange(rows):
        return lax.all_to_all(rows, "seq", split_axis=0, concat_axis=0, tiled=True)

    def pack(chunk):
        column = pl.BlockSpec((tok_rows, head_size), lambda h: (0, chunk * heads + h))
        return pl.pallas_call(
            pack_kernel,
            grid=(heads,),
            in_specs=[
                pl.BlockSpec((1, 1, tok_rows), lambda h: (chunk * heads + h, 0, 0)),
                pl.BlockSpec((1, cluster_count), lambda h: (0, 0)),
                column,
                column,
                column,
                column,
            ],
            out_specs=[block, pl.BlockSpec((1, 1, tok_rows), lambda h: (h, 0, 0))],
            out_shape=[sent, jax.ShapeDtypeStruct((heads, 1, tok_rows), jnp.int32)],
            scratch_shapes=[pltpu.VMEM((tok_rows, tok_rows), BF16)],
            compiler_params=params(),
            cost_estimate=pl.CostEstimate(
                flops=heads * 2 * 1024 * 512 * 640, bytes_accessed=2 * sent_bytes, transcendentals=0
            ),
            name="pack",
        )(ids_rows, slot_row, queries, keys, values, out_grad)

    def own(chunk, received):
        return pl.pallas_call(
            owner_kernel,
            grid=(heads,),
            in_specs=[
                block,
                pl.BlockSpec((1, owned, head_size), lambda h: (chunk * heads + h, 0, 0)),
            ],
            out_specs=[block, pl.BlockSpec((1, owned, head_size), lambda h: (h, 0, 0))],
            out_shape=[sent, jax.ShapeDtypeStruct((heads, owned, head_size), F32)],
            scratch_shapes=[
                pltpu.VMEM((16 * block_rows, 16 * block_rows), BF16),
                pltpu.VMEM((slot_count, slot_count), F32),
                pltpu.VMEM((owned, slot_count, width), BF16),
                pltpu.VMEM((owned, slot_count, width), BF16),
            ],
            compiler_params=params(),
            cost_estimate=pl.CostEstimate(
                flops=heads * owned * 7 * 2 * slot_count * slot_count * head_size,
                bytes_accessed=2 * sent_bytes,
                transcendentals=heads * owned * slot_count * slot_count,
            ),
            name="own",
        )(received, centroids)

    def unpack(chunk, flat_cols, returned, previous):
        column = pl.BlockSpec((tok_rows, head_size), lambda h: (0, chunk * heads + h))
        whole = jax.ShapeDtypeStruct((tok_rows, local_heads * head_size), BF16)

        def kernel(*refs):
            unpack_kernel(chunk, *refs)

        return pl.pallas_call(
            kernel,
            grid=(heads,),
            in_specs=[pl.BlockSpec((tok_rows, heads), lambda h: (0, 0)), block]
            + [pl.BlockSpec(memory_space=pl.ANY)] * len(previous),
            out_specs=[column] * 4,
            out_shape=[whole] * 4,
            input_output_aliases={2 + i: i for i in range(len(previous))},
            compiler_params=params(),
            cost_estimate=pl.CostEstimate(
                flops=heads * 2 * 1024 * 512 * 512, bytes_accessed=2 * sent_bytes, transcendentals=0
            ),
            name="unpack",
        )(flat_cols, returned, *previous)

    packed = [pack(chunk) for chunk in range(1)]
    received = [exchange(rows) for rows, _ in packed]
    owned_now = [own(chunk, rows) for chunk, rows in enumerate(received)]
    returned = [exchange(rows) for rows, _ in owned_now]
    outs = ()
    for chunk in range(1):
        flat_cols = packed[chunk][1].reshape(heads, tok_rows).T
        outs = unpack(chunk, flat_cols, returned[chunk], tuple(outs))
    new_centroids = jnp.concatenate([new for _, new in owned_now], axis=0)
    return (*outs, new_centroids)


def body(queries, keys, values, out_grad, cluster_ids, cluster_slot, centroids):
    seq_count = lax.axis_size("seq")
    local_heads, tok_rows = cluster_ids.shape[:2]
    cluster_count = cluster_slot.shape[0]
    owned, head_size = centroids.shape[1:]
    heads = local_heads // CHUNKS
    width = 4 * head_size
    pair_rows = 2 * SHARED
    steps = heads // 2
    send_rows = steps * pair_rows + PACKED
    slot_count = seq_count * CAP
    problems = 2 * owned
    block_bytes = seq_count * pair_rows * width * 2
    sent_shape = jax.ShapeDtypeStruct((seq_count, send_rows, width), BF16)
    ids_rows = cluster_ids.reshape(local_heads, 1, tok_rows)
    slot_row = cluster_slot.reshape(1, cluster_count)
    me = lax.axis_index("seq").reshape(1)

    def cost(flops, exps=0):
        return pl.CostEstimate(
            flops=flops, bytes_accessed=2 * (steps + 1) * block_bytes, transcendentals=exps
        )

    shared_block = pl.BlockSpec((seq_count, pair_rows, width), lambda s: (0, s, 0))
    packed_block = pl.BlockSpec((seq_count, PACKED, width), lambda s: (0, steps, 0))
    whole_block = pl.BlockSpec((seq_count, send_rows, width), lambda s: (0, 0, 0))
    me_spec = pl.BlockSpec(memory_space=pltpu.SMEM)

    def pack(chunk):
        column = pl.BlockSpec((tok_rows, 2 * head_size), lambda s: (0, chunk * steps + s))
        row_shape = jax.ShapeDtypeStruct((heads, 1, tok_rows), jnp.int32)
        rows_block = pl.BlockSpec((heads, 1, tok_rows), lambda s: (0, 0, 0))
        return pl.pallas_call(
            functools.partial(pack_rows_kernel, chunk * heads),
            grid=(steps,),
            in_specs=[
                pl.BlockSpec((heads, 1, tok_rows), lambda s: (chunk, 0, 0)),
                pl.BlockSpec((1, cluster_count), lambda s: (0, 0)),
            ]
            + [column] * 4,
            out_specs=[whole_block, rows_block, rows_block],
            out_shape=[sent_shape, row_shape, row_shape],
            scratch_shapes=[
                pltpu.VMEM((seq_count, head_size), BF16),
                pltpu.VMEM((seq_count * PACKED, width), F32),
            ],
            compiler_params=params(),
            cost_estimate=cost(2 * heads * 1536 * tok_rows * width),
            name="pack_rows",
        )(ids_rows, slot_row, queries, keys, values, out_grad)

    def own(chunk, received):
        return pl.pallas_call(
            functools.partial(own_rows_kernel, chunk * heads),
            grid=(steps,),
            in_specs=[me_spec, shared_block, packed_block],
            out_specs=[whole_block, pl.BlockSpec((8, head_size), lambda s: (0, 0))],
            out_shape=[sent_shape, jax.ShapeDtypeStruct((8, head_size), F32)],
            scratch_shapes=[
                pltpu.VMEM(
                    (seq_count // 16, problems * 16 * CAP, 16 * (pair_rows + PACKED)), BF16
                ),
                pltpu.VMEM((slot_count, slot_count), F32),
                pltpu.VMEM((problems, slot_count, width), BF16),
                pltpu.VMEM((problems, slot_count, width), BF16),
                pltpu.VMEM((problems, head_size), F32),
            ],
            compiler_params=params(),
            cost_estimate=cost(
                steps * problems * 16 * 2 * slot_count * slot_count * head_size,
                steps * problems * slot_count * slot_count,
            ),
            name="own_rows",
        )(me, received, received)

    def unpack(chunk, base_rows, over_rows, returned, previous):
        column = pl.BlockSpec((tok_rows, 2 * head_size), lambda s: (0, chunk * steps + s))
        routes_block = pl.BlockSpec((tok_rows, heads), lambda s: (0, 0))
        centroid_block = pl.BlockSpec(
            (2, owned, head_size), lambda s: (chunk * steps + s, 0, 0)
        )
        return pl.pallas_call(
            functools.partial(unpack_rows_kernel, chunk * heads),
            grid=(steps,),
            in_specs=[
                me_spec,
                routes_block,
                routes_block,
                centroid_block,
                shared_block,
                packed_block,
            ]
            + [pl.BlockSpec(memory_space=pl.ANY)] * len(previous),
            out_specs=[column] * 4 + [centroid_block],
            out_shape=[pltpu.HBM((tok_rows, local_heads * head_size), BF16)] * 4
            + [pltpu.HBM(centroids.shape, F32)],
            input_output_aliases={6 + at: at for at in range(len(previous))},
            compiler_params=params(),
            cost_estimate=cost(2 * heads * 1536 * tok_rows * width),
            name="unpack_rows",
        )(
            me,
            base_rows.reshape(heads, tok_rows).T,
            over_rows.reshape(heads, tok_rows).T,
            centroids,
            returned,
            returned,
            *previous,
        )

    def exchange(rows):
        return lax.all_to_all(rows, "seq", split_axis=0, concat_axis=0, tiled=True)

    packed = [pack(chunk) for chunk in range(CHUNKS)]
    received = [exchange(rows) for rows, _, _ in packed]
    owned_now = [own(chunk, received[chunk]) for chunk in range(CHUNKS)]
    returned = [exchange(back) for back, _ in owned_now]
    outs = ()
    for chunk in range(CHUNKS):
        outs = unpack(chunk, *packed[chunk][1:], returned[chunk], tuple(outs))

    peak = functools.reduce(jnp.maximum, [seen[0:1] for _, seen in owned_now])
    swap = [(at, 1 - at) for at in range(2)]
    peak = jnp.maximum(peak, lax.ppermute(peak, "head", swap))[0, PEAK_LANE]

    def lacking(state):
        return state[0]

    def again(state):
        full = dense(queries, keys, values, out_grad, cluster_ids, cluster_slot, centroids)
        return (jnp.zeros((), jnp.bool_), *full)

    state = lax.while_loop(lacking, again, (peak > PACKED - SPARE, *outs))
    return state[1:]


def solution(mesh):
    return jax.shard_map(
        body,
        mesh=mesh,
        in_specs=(
            P("seq", "head"),
            P("seq", "head"),
            P("seq", "head"),
            P("seq", "head"),
            P("head", "seq", None),
            P(),
            P("head", "seq", None),
        ),
        out_specs=(
            P("seq", "head"),
            P("seq", "head"),
            P("seq", "head"),
            P("seq", "head"),
            P("head", "seq", None),
        ),
        check_vma=False,
    )
```

```python
import functools
import math

import jax
import jax.numpy as jnp
from jax import lax
from jax.experimental import pallas as pl
from jax.experimental.pallas import tpu as pltpu
from jax.sharding import PartitionSpec as P

CAP = 4
DECAY_RATE = 0.9
MASKED = -1e30
ABSENT = 64.0
CHUNKS = 2
SHARED = 8
PACKED = 16
SPARE = 2
PEAK_LANE = 127
TURN_BY = 8
VMEM_BYTES = 63 * 1024 * 1024

F32 = jnp.float32
BF16 = jnp.bfloat16
CONTRACT_LAST = (((1,), (1,)), ((), ()))
CONTRACT_FIRST = (((0,), (0,)), ((), ()))


def iota(shape, dim):
    return lax.broadcasted_iota(jnp.int32, shape, dim)


def dot(left, right):
    return jnp.dot(left, right, preferred_element_type=F32)


def pack_kernel(ids_ref, slot_ref, q_ref, k_ref, v_ref, g_ref, send_ref, flat_ref, earlier_ref):
    tok_rows = ids_ref.shape[2]
    cluster_count = slot_ref.shape[1]
    slot_rows = cluster_count * CAP

    @pl.when(pl.program_id(0) == 0)
    def _():
        earlier_ref[...] = (iota((tok_rows, tok_rows), 0) < iota((tok_rows, tok_rows), 1)).astype(
            F32
        ).astype(BF16)

    ids_row = ids_ref[0]
    member = iota((cluster_count, tok_rows), 0) == ids_row
    member_f = jnp.where(member, 1.0, 0.0)
    member_low = member_f.astype(BF16)
    slots_low = jnp.broadcast_to(slot_ref[...].astype(F32), (8, cluster_count)).astype(BF16)
    slot_row = dot(slots_low, member_low)[0:1]
    rank_row = jnp.sum(dot(member_low, earlier_ref[...]) * member_f, axis=0, keepdims=True)
    flat_row = (slot_row * CAP + rank_row).astype(jnp.int32)
    flat_ref[0] = flat_row
    place = jnp.where(iota((slot_rows, tok_rows), 0) == flat_row, 1.0, 0.0).astype(BF16)
    ones = jnp.ones((tok_rows, 128), BF16)
    head_size = q_ref.shape[1]
    taken = dot(place, ones)
    out_shape = send_ref.shape[:2] + (head_size,)

    def put(at, rows):
        send_ref[:, :, at * head_size : (at + 1) * head_size] = rows.astype(BF16).reshape(out_shape)

    put(0, dot(place, q_ref[...]))
    put(1, dot(place, k_ref[...]) + (1.0 - taken) * ABSENT)
    put(2, dot(place, v_ref[...]))
    put(3, dot(place, g_ref[...]))


def owner_kernel(recv_ref, cent_ref, back_ref, new_ref, turn_ref, causal_ref, rows_ref, grads_ref):
    source_count, block_rows, width = recv_ref.shape
    head_size = width // 4
    owned = block_rows // CAP
    slot_count = source_count * CAP
    group_rows = 16 * block_rows
    groups = source_count // 16
    part = 16 * CAP
    score_scale = 1.0 / math.sqrt(head_size)

    @pl.when(pl.program_id(0) == 0)
    def _():
        row_at = iota((group_rows, group_rows), 0)
        col_at = iota((group_rows, group_rows), 1)
        cluster_of = row_at // part
        source_of = (row_at % part) // CAP
        from_row = source_of * block_rows + cluster_of * CAP + row_at % CAP
        turn_ref[...] = jnp.where(from_row == col_at, 1.0, 0.0).astype(BF16)
        causal_ref[...] = jnp.where(
            iota((slot_count, slot_count), 1) <= iota((slot_count, slot_count), 0), 0.0, MASKED
        )

    turn = turn_ref[...]
    @pl.loop(0, groups)
    def _(group):
        arrived = recv_ref[pl.ds(group * 16, 16)].reshape(group_rows, width)
        turned = dot(turn, arrived).astype(BF16)
        at_row = pl.multiple_of(group * part, part)
        rows_ref[:, pl.ds(at_row, part), :] = turned.reshape(owned, part, width)

    first_lane = jnp.where(iota((8, head_size), 1) == 0, 1.0, 0.0).astype(BF16)
    @pl.loop(0, owned)
    def _(cluster):
        q = rows_ref[cluster, :, 0:head_size]
        k = rows_ref[cluster, :, head_size : 2 * head_size]
        v = rows_ref[cluster, :, 2 * head_size : 3 * head_size]
        g = rows_ref[cluster, :, 3 * head_size : 4 * head_size]
        marks = lax.dot_general(first_lane, k, CONTRACT_LAST, preferred_element_type=F32)
        present = marks < ABSENT / 2
        bias = jnp.where(present, 0.0, MASKED)[0:1]
        scores = lax.dot_general(q, k, CONTRACT_LAST, preferred_element_type=F32) * score_scale
        scores = scores + (causal_ref[...] + bias)
        weights = jnp.exp(scores - jnp.max(scores, axis=-1, keepdims=True))
        probs = weights / jnp.sum(weights, axis=-1, keepdims=True)
        probs_low = probs.astype(BF16)
        out = dot(probs_low, v).astype(BF16)
        grad_prob = lax.dot_general(g, v, CONTRACT_LAST, preferred_element_type=F32)
        delta = jnp.sum(g.astype(F32) * out.astype(F32), axis=-1, keepdims=True)
        grad_score = (probs * (grad_prob - delta) * score_scale).astype(BF16)
        grad_q = dot(grad_score, k)
        grad_k = lax.dot_general(grad_score, q, CONTRACT_FIRST, preferred_element_type=F32)
        grad_v = lax.dot_general(probs_low, g, CONTRACT_FIRST, preferred_element_type=F32)
        grads_ref[cluster, :, 0:head_size] = out
        grads_ref[cluster, :, head_size : 2 * head_size] = grad_q.astype(BF16)
        grads_ref[cluster, :, 2 * head_size : 3 * head_size] = grad_k.astype(BF16)
        grads_ref[cluster, :, 3 * head_size : 4 * head_size] = grad_v.astype(BF16)
        key_sums = dot(jnp.where(present, 1.0, 0.0).astype(BF16), k)[0:1]
        blend = DECAY_RATE * cent_ref[0, pl.ds(cluster, 1), :] + (1.0 - DECAY_RATE) * key_sums
        new_ref[0, pl.ds(cluster, 1), :] = blend / jnp.sqrt(
            jnp.mean(blend * blend, axis=-1, keepdims=True) + 1e-06
        )

    @pl.loop(0, groups)
    def _(group):
        at_row = pl.multiple_of(group * part, part)
        leaving = grads_ref[:, pl.ds(at_row, part), :].reshape(group_rows, width)
        turned = lax.dot_general(turn, leaving, CONTRACT_FIRST, preferred_element_type=F32)
        back_ref[pl.ds(group * 16, 16)] = turned.astype(BF16).reshape(16, block_rows, width)


def unpack_kernel(chunk, flat_ref, ret_ref, *refs):
    out_refs = refs[-4:]
    sources, block_rows, width = ret_ref.shape
    head_size = width // 4
    tok_rows, heads = flat_ref.shape
    slot_rows = sources * block_rows
    here = iota((tok_rows, heads), 1) == pl.program_id(0)
    flat_col = jnp.sum(jnp.where(here, flat_ref[...], 0), axis=1, keepdims=True)
    take = jnp.where(iota((tok_rows, slot_rows), 1) == flat_col, 1.0, 0.0).astype(BF16)
    rows = dot(take, ret_ref[...].reshape(slot_rows, width)).astype(BF16)
    for at, out_ref in enumerate(out_refs):
        out_ref[...] = rows[:, at * head_size : (at + 1) * head_size]


def find_rows(first_head, ids_ref, slot_ref, base_ref, over_ref, header_ref):
    heads, _, tok_rows = ids_ref.shape
    cluster_count = slot_ref.shape[1]
    owners, lanes = header_ref.shape
    earlier = jnp.where(
        iota((tok_rows, tok_rows), 0) < iota((tok_rows, tok_rows), 1), 1.0, 0.0
    ).astype(BF16)
    slots_low = jnp.broadcast_to(slot_ref[...].astype(F32), (8, cluster_count)).astype(BF16)
    members = [
        jnp.where(iota((cluster_count, tok_rows), 0) == ids_ref[head], 1.0, 0.0)
        for head in range(heads)
    ]
    member_low = jnp.concatenate(members, axis=0).astype(BF16)
    earlier_members = dot(member_low, earlier)
    owner_of, tag_of, here_of = [], [], []
    for head in range(heads):
        own = slice(head * cluster_count, (head + 1) * cluster_count)
        slot = dot(slots_low, member_low[own])[0:1].astype(jnp.int32)
        rank = jnp.sum(earlier_members[own] * members[head], axis=0, keepdims=True)
        owner = (slot // CAP + TURN_BY * (first_head + head)) % owners
        owner_of.append(owner)
        tag_of.append((head * CAP + slot % CAP) * CAP + rank.astype(jnp.int32))
        here_of.append(jnp.where(iota((owners, tok_rows), 0) == owner, 1.0, 0.0))
    before_all = dot(jnp.concatenate(here_of, axis=0).astype(BF16), earlier)
    filled = jnp.zeros((owners, 1), F32)
    header = jnp.zeros((owners, lanes), F32)
    for head in range(heads):
        here_f = here_of[head]
        before = before_all[head * owners : (head + 1) * owners]
        place = jnp.sum(before * here_f, axis=0, keepdims=True).astype(jnp.int32)
        late = jnp.sum((before + filled) * here_f, axis=0, keepdims=True)
        late = late.astype(jnp.int32) - SHARED
        filled = filled + jnp.maximum(jnp.sum(here_f, axis=1, keepdims=True) - SHARED, 0.0)
        fits = place < SHARED
        packs = (late < PACKED - SPARE) & (place >= SHARED)
        base_ref[head] = jnp.where(fits, owner_of[head] * SHARED + place, -1)
        over_ref[head] = jnp.where(packs, owner_of[head] * PACKED + late, -1)
        lane = jnp.where(fits, head * SHARED + place, jnp.where(packs, heads * SHARED + late, -1))
        named = (here_f * (tag_of[head] + 1).astype(F32)).astype(BF16)
        lane_at = jnp.where(iota((lanes, tok_rows), 0) == lane, 1.0, 0.0).astype(BF16)
        header = header + lax.dot_general(
            named, lane_at, CONTRACT_LAST, preferred_element_type=F32
        )
    peak = jnp.max(filled, axis=0, keepdims=True)
    header_ref[...] = jnp.where(iota((owners, lanes), 1) == PEAK_LANE, peak, header).astype(BF16)


def token_rows(refs, at, head_size):
    lanes = slice(at * head_size, (at + 1) * head_size)
    return jnp.concatenate([ref[:, lanes] for ref in refs], axis=1)


def pack_rows_kernel(
    first_head,
    ids_ref,
    slot_ref,
    q_ref,
    k_ref,
    v_ref,
    g_ref,
    send_ref,
    base_ref,
    over_ref,
    header_ref,
    total_ref,
):
    owners, send_rows, width = send_ref.shape
    tok_rows = q_ref.shape[0]
    head_size = width // 4
    step = pl.program_id(0)

    @pl.when(step == 0)
    def _():
        find_rows(first_head, ids_ref, slot_ref, base_ref, over_ref, header_ref)

    rows = [token_rows((q_ref, k_ref, v_ref, g_ref), at, head_size) for at in range(2)]
    halves = []
    for at in range(2):
        place = iota((owners * SHARED, tok_rows), 0) == base_ref[step * 2 + at]
        placed = dot(jnp.where(place, 1.0, 0.0).astype(BF16), rows[at])
        halves.append(placed.reshape(owners, SHARED, width))
    at_row = pl.multiple_of(step * 2 * SHARED, 2 * SHARED)
    shared = jnp.concatenate(halves, axis=1).astype(BF16)
    send_ref[:, pl.ds(at_row, 2 * SHARED), :] = shared

    places = [
        jnp.where(iota((owners * PACKED, tok_rows), 0) == over_ref[step * 2 + at], 1.0, 0.0).astype(BF16)
        for at in range(2)
    ]
    added = dot(jnp.concatenate(places, axis=1), jnp.concatenate(rows, axis=0))

    @pl.when(step == 0)
    def _():
        total_ref[...] = added

    @pl.when(step == pl.num_programs(0) - 1)
    def _():
        total = total_ref[...] + added
        last_row = iota((owners * PACKED, owners), 1) * PACKED + PACKED - 1
        to_last = jnp.where(iota((owners * PACKED, owners), 0) == last_row, 1.0, 0.0)
        tags = dot(to_last.astype(BF16), header_ref[...])
        total = jnp.concatenate([total[:, :head_size] + tags, total[:, head_size:]], axis=1)
        packed = total.astype(BF16).reshape(owners, PACKED, width)
        send_ref[:, send_rows - PACKED :, :] = packed


def own_rows_kernel(
    first_head,
    me_ref,
    shared_ref,
    over_ref,
    back_ref,
    peak_ref,
    turn_ref,
    causal_ref,
    rows_ref,
    grads_ref,
    sums_ref,
):
    sources, pair_rows, width = shared_ref.shape
    head_size = width // 4
    problems = rows_ref.shape[0]
    owned = problems // 2
    slot_count = sources * CAP
    bunch = 16
    groups = sources // bunch
    part = bunch * CAP
    shared_count = bunch * pair_rows
    packed_count = bunch * PACKED
    score_scale = 1.0 / math.sqrt(head_size)
    step = pl.program_id(0)
    steps = pl.num_programs(0)

    @pl.when(step == 0)
    def _():
        at = iota((slot_count, slot_count), 0)
        causal_ref[...] = jnp.where(iota((slot_count, slot_count), 1) <= at, 0.0, MASKED)

    header_of = jnp.where(
        iota((bunch, packed_count), 1) == iota((bunch, packed_count), 0) * PACKED + PACKED - 1,
        1.0,
        0.0,
    ).astype(BF16)

    def turns(header, first_lane, rows_each, used):
        count = bunch * rows_each
        lane = iota((head_size, count), 1) % rows_each
        match = (iota((head_size, count), 0) == lane + first_lane) & (lane < used)
        tags = dot(header, jnp.where(match, 1.0, 0.0).astype(BF16))
        source = iota((1, count), 1) // rows_each
        own = iota((bunch, count), 0) == source
        tag = jnp.sum(jnp.where(own, tags, 0.0), axis=0, keepdims=True).astype(jnp.int32) - 1
        mine = (tag >= 0) & (tag // (problems * CAP) == step)
        problem = (tag // CAP) % problems
        slot = jnp.where(mine, problem * part + source * CAP + tag % CAP, -1)
        hit = iota((problems * part, count), 0) == slot
        return jnp.where(hit, 1.0, 0.0).astype(BF16)

    ones = jnp.ones((shared_count + packed_count, head_size), BF16)
    peak_ref[...] = jnp.zeros(peak_ref.shape, F32)

    @pl.loop(0, groups)
    def _(group):
        from_sources = pl.ds(group * bunch, bunch)
        at_row = pl.multiple_of(group * part, part)
        packed = over_ref[from_sources].reshape(packed_count, width)
        shared = shared_ref[from_sources].reshape(shared_count, width)
        header = dot(header_of, packed[:, :head_size])
        peak_ref[...] = jnp.maximum(peak_ref[...], jnp.max(header, axis=0, keepdims=True))
        header = header.astype(BF16)
        turn = jnp.concatenate(
            [
                turns(header, step * pair_rows, pair_rows, pair_rows),
                turns(header, steps * pair_rows, PACKED, PACKED - SPARE),
            ],
            axis=1,
        )
        turn_ref[group] = turn
        turned = dot(turn, jnp.concatenate([shared, packed], axis=0))
        marked = turned[:, head_size : 2 * head_size] + (1.0 - dot(turn, ones)) * ABSENT
        turned = jnp.concatenate(
            [turned[:, :head_size], marked, turned[:, 2 * head_size :]], axis=1
        )
        rows_ref[:, pl.ds(at_row, part), :] = turned.astype(BF16).reshape(problems, part, width)

    first_lane = jnp.where(iota((8, head_size), 1) == 0, 1.0, 0.0).astype(BF16)

    def attend(problem):
        q = rows_ref[problem, :, 0:head_size]
        k = rows_ref[problem, :, head_size : 2 * head_size]
        v = rows_ref[problem, :, 2 * head_size : 3 * head_size]
        g = rows_ref[problem, :, 3 * head_size : 4 * head_size]
        marks = lax.dot_general(first_lane, k, CONTRACT_LAST, preferred_element_type=F32)
        present = marks < ABSENT / 2
        bias = jnp.where(present, 0.0, MASKED)[0:1]
        scores = lax.dot_general(q, k, CONTRACT_LAST, preferred_element_type=F32) * score_scale
        scores = scores + (causal_ref[...] + bias)
        weights = jnp.exp(scores - jnp.max(scores, axis=-1, keepdims=True))
        probs = weights / jnp.sum(weights, axis=-1, keepdims=True)
        probs_low = probs.astype(BF16)
        out = dot(probs_low, v).astype(BF16)
        grad_prob = lax.dot_general(g, v, CONTRACT_LAST, preferred_element_type=F32)
        delta = jnp.sum(g.astype(F32) * out.astype(F32), axis=-1, keepdims=True)
        grad_score = (probs * (grad_prob - delta) * score_scale).astype(BF16)
        grad_q = dot(grad_score, k)
        grad_k = lax.dot_general(grad_score, q, CONTRACT_FIRST, preferred_element_type=F32)
        grad_v = lax.dot_general(probs_low, g, CONTRACT_FIRST, preferred_element_type=F32)
        grads_ref[problem, :, 0:head_size] = out
        grads_ref[problem, :, head_size : 2 * head_size] = grad_q.astype(BF16)
        grads_ref[problem, :, 2 * head_size : 3 * head_size] = grad_k.astype(BF16)
        grads_ref[problem, :, 3 * head_size : 4 * head_size] = grad_v.astype(BF16)
        sums = dot(jnp.where(present, 1.0, 0.0).astype(BF16), k)[0:1]
        sums_ref[pl.ds(problem, 1), :] = sums

    @pl.loop(0, problems // 2)
    def _(pair):
        attend(pair * 2)
        attend(pair * 2 + 1)

    rest = slice(back_ref.shape[1] - PACKED, back_ref.shape[1])
    at_pair = pl.multiple_of(step * pair_rows, pair_rows)

    @pl.loop(0, groups)
    def _(group):
        from_sources = pl.ds(group * bunch, bunch)
        at_row = pl.multiple_of(group * part, part)
        leaving = grads_ref[:, pl.ds(at_row, part), :].reshape(problems * part, width)
        sent = lax.dot_general(
            turn_ref[group], leaving, CONTRACT_FIRST, preferred_element_type=F32
        ).astype(BF16)
        back_ref[from_sources, pl.ds(at_pair, pair_rows), :] = sent[:shared_count].reshape(
            bunch, pair_rows, width
        )
        packed = sent[shared_count:].reshape(bunch, PACKED, width)

        @pl.when(step == 0)
        def _():
            back_ref[from_sources, rest, :] = packed

        @pl.when(step > 0)
        def _():
            back_ref[from_sources, rest, :] += packed

    for at in range(2):
        sums = jnp.concatenate(
            [sums_ref[at * owned + slot : at * owned + slot + 1, :] for slot in range(owned)],
            axis=1,
        )
        high = sums.astype(BF16).astype(F32)
        low = sums - high
        turned_by = TURN_BY * (first_head + step * 2 + at)
        home = lax.rem(me_ref[0] + sources * TURN_BY - turned_by, sources)
        row = iota((PACKED, width), 0)
        tile = back_ref[home, rest, :].astype(F32)
        tile = jnp.where(row == PACKED - 2, high, jnp.where(row == PACKED - 1, low, tile))
        back_ref[home, rest, :] = tile.astype(BF16)


def unpack_rows_kernel(
    first_head, me_ref, base_ref, over_ref, cent_ref, shared_ref, packed_ref, *refs
):
    new_ref = refs[-1]
    out_refs = refs[-5:-1]
    owners, _, width = shared_ref.shape
    head_size = width // 4
    owned = cent_ref.shape[1]
    tok_rows, heads = base_ref.shape
    step = pl.program_id(0)
    packed = packed_ref[...].reshape(owners * PACKED, width)
    arrived = shared_ref[...].astype(F32)
    for at in range(2):
        here = iota((tok_rows, heads), 1) == step * 2 + at
        base = jnp.sum(jnp.where(here, base_ref[...], 0), axis=1, keepdims=True)
        over = jnp.sum(jnp.where(here, over_ref[...], 0), axis=1, keepdims=True)
        take = iota((tok_rows, owners * SHARED), 1) == base
        take_over = iota((tok_rows, owners * PACKED), 1) == over
        mine = arrived[:, at * SHARED : (at + 1) * SHARED, :].reshape(owners * SHARED, width)
        rows = dot(jnp.where(take, 1.0, 0.0).astype(BF16), mine.astype(BF16))
        rows = rows + dot(jnp.where(take_over, 1.0, 0.0).astype(BF16), packed)
        rows = rows.astype(BF16)
        for which, out_ref in enumerate(out_refs):
            out_ref[:, at * head_size : (at + 1) * head_size] = rows[
                :, which * head_size : (which + 1) * head_size
            ]
        turned_by = TURN_BY * (first_head + step * 2 + at)
        tile = packed_ref[lax.rem(me_ref[0] + turned_by, owners)].astype(F32)
        spare = iota((PACKED, width), 0) >= PACKED - 2
        key_sums = jnp.sum(jnp.where(spare, tile, 0.0), axis=0, keepdims=True)
        for slot in range(owned):
            blend = DECAY_RATE * cent_ref[at, slot : slot + 1, :]
            blend += (1.0 - DECAY_RATE) * key_sums[:, slot * head_size : (slot + 1) * head_size]
            new_ref[at, slot : slot + 1, :] = blend / jnp.sqrt(
                jnp.mean(blend * blend, axis=-1, keepdims=True) + 1e-06
            )


def params():
    return pltpu.CompilerParams(vmem_limit_bytes=VMEM_BYTES)


def dense(queries, keys, values, out_grad, cluster_ids, cluster_slot, centroids):
    seq_count = lax.axis_size("seq")
    local_heads, tok_rows = cluster_ids.shape[:2]
    cluster_count = cluster_slot.shape[0]
    owned = cluster_count // seq_count
    head_size = centroids.shape[2]
    heads = local_heads
    block_rows = owned * CAP
    width = 4 * head_size
    slot_count = seq_count * CAP
    sent = jax.ShapeDtypeStruct((seq_count, heads * block_rows, width), BF16)
    sent_bytes = seq_count * heads * block_rows * width * 2
    ids_rows = cluster_ids.reshape(local_heads, 1, tok_rows)
    slot_row = cluster_slot.reshape(1, cluster_count)
    block = pl.BlockSpec((seq_count, block_rows, width), lambda h: (0, h, 0))

    def exchange(rows):
        return lax.all_to_all(rows, "seq", split_axis=0, concat_axis=0, tiled=True)

    def pack(chunk):
        column = pl.BlockSpec((tok_rows, head_size), lambda h: (0, chunk * heads + h))
        return pl.pallas_call(
            pack_kernel,
            grid=(heads,),
            in_specs=[
                pl.BlockSpec((1, 1, tok_rows), lambda h: (chunk * heads + h, 0, 0)),
                pl.BlockSpec((1, cluster_count), lambda h: (0, 0)),
                column,
                column,
                column,
                column,
            ],
            out_specs=[block, pl.BlockSpec((1, 1, tok_rows), lambda h: (h, 0, 0))],
            out_shape=[sent, jax.ShapeDtypeStruct((heads, 1, tok_rows), jnp.int32)],
            scratch_shapes=[pltpu.VMEM((tok_rows, tok_rows), BF16)],
            compiler_params=params(),
            cost_estimate=pl.CostEstimate(
                flops=heads * 2 * 1024 * 512 * 640, bytes_accessed=2 * sent_bytes, transcendentals=0
            ),
            name="pack",
        )(ids_rows, slot_row, queries, keys, values, out_grad)

    def own(chunk, received):
        return pl.pallas_call(
            owner_kernel,
            grid=(heads,),
            in_specs=[
                block,
                pl.BlockSpec((1, owned, head_size), lambda h: (chunk * heads + h, 0, 0)),
            ],
            out_specs=[block, pl.BlockSpec((1, owned, head_size), lambda h: (h, 0, 0))],
            out_shape=[sent, jax.ShapeDtypeStruct((heads, owned, head_size), F32)],
            scratch_shapes=[
                pltpu.VMEM((16 * block_rows, 16 * block_rows), BF16),
                pltpu.VMEM((slot_count, slot_count), F32),
                pltpu.VMEM((owned, slot_count, width), BF16),
                pltpu.VMEM((owned, slot_count, width), BF16),
            ],
            compiler_params=params(),
            cost_estimate=pl.CostEstimate(
                flops=heads * owned * 7 * 2 * slot_count * slot_count * head_size,
                bytes_accessed=2 * sent_bytes,
                transcendentals=heads * owned * slot_count * slot_count,
            ),
            name="own",
        )(received, centroids)

    def unpack(chunk, flat_cols, returned, previous):
        column = pl.BlockSpec((tok_rows, head_size), lambda h: (0, chunk * heads + h))
        whole = jax.ShapeDtypeStruct((tok_rows, local_heads * head_size), BF16)

        def kernel(*refs):
            unpack_kernel(chunk, *refs)

        return pl.pallas_call(
            kernel,
            grid=(heads,),
            in_specs=[pl.BlockSpec((tok_rows, heads), lambda h: (0, 0)), block]
            + [pl.BlockSpec(memory_space=pl.ANY)] * len(previous),
            out_specs=[column] * 4,
            out_shape=[whole] * 4,
            input_output_aliases={2 + i: i for i in range(len(previous))},
            compiler_params=params(),
            cost_estimate=pl.CostEstimate(
                flops=heads * 2 * 1024 * 512 * 512, bytes_accessed=2 * sent_bytes, transcendentals=0
            ),
            name="unpack",
        )(flat_cols, returned, *previous)

    packed = [pack(chunk) for chunk in range(1)]
    received = [exchange(rows) for rows, _ in packed]
    owned_now = [own(chunk, rows) for chunk, rows in enumerate(received)]
    returned = [exchange(rows) for rows, _ in owned_now]
    outs = ()
    for chunk in range(1):
        flat_cols = packed[chunk][1].reshape(heads, tok_rows).T
        outs = unpack(chunk, flat_cols, returned[chunk], tuple(outs))
    new_centroids = jnp.concatenate([new for _, new in owned_now], axis=0)
    return (*outs, new_centroids)


def body(queries, keys, values, out_grad, cluster_ids, cluster_slot, centroids):
    seq_count = lax.axis_size("seq")
    local_heads, tok_rows = cluster_ids.shape[:2]
    cluster_count = cluster_slot.shape[0]
    owned, head_size = centroids.shape[1:]
    heads = local_heads // CHUNKS
    width = 4 * head_size
    pair_rows = 2 * SHARED
    steps = heads // 2
    send_rows = steps * pair_rows + PACKED
    slot_count = seq_count * CAP
    problems = 2 * owned
    block_bytes = seq_count * pair_rows * width * 2
    sent_shape = jax.ShapeDtypeStruct((seq_count, send_rows, width), BF16)
    ids_rows = cluster_ids.reshape(local_heads, 1, tok_rows)
    slot_row = cluster_slot.reshape(1, cluster_count)
    me = lax.axis_index("seq").reshape(1)

    def cost(flops, exps=0):
        return pl.CostEstimate(
            flops=flops, bytes_accessed=2 * (steps + 1) * block_bytes, transcendentals=exps
        )

    shared_block = pl.BlockSpec((seq_count, pair_rows, width), lambda s: (0, s, 0))
    packed_block = pl.BlockSpec((seq_count, PACKED, width), lambda s: (0, steps, 0))
    whole_block = pl.BlockSpec((seq_count, send_rows, width), lambda s: (0, 0, 0))
    me_spec = pl.BlockSpec(memory_space=pltpu.SMEM)

    def pack(chunk):
        column = pl.BlockSpec((tok_rows, 2 * head_size), lambda s: (0, chunk * steps + s))
        row_shape = jax.ShapeDtypeStruct((heads, 1, tok_rows), jnp.int32)
        rows_block = pl.BlockSpec((heads, 1, tok_rows), lambda s: (0, 0, 0))
        return pl.pallas_call(
            functools.partial(pack_rows_kernel, chunk * heads),
            grid=(steps,),
            in_specs=[
                pl.BlockSpec((heads, 1, tok_rows), lambda s: (chunk, 0, 0)),
                pl.BlockSpec((1, cluster_count), lambda s: (0, 0)),
            ]
            + [column] * 4,
            out_specs=[whole_block, rows_block, rows_block],
            out_shape=[sent_shape, row_shape, row_shape],
            scratch_shapes=[
                pltpu.VMEM((seq_count, head_size), BF16),
                pltpu.VMEM((seq_count * PACKED, width), F32),
            ],
            compiler_params=params(),
            cost_estimate=cost(2 * heads * 1536 * tok_rows * width),
            name="pack_rows",
        )(ids_rows, slot_row, queries, keys, values, out_grad)

    def own(chunk, received):
        return pl.pallas_call(
            functools.partial(own_rows_kernel, chunk * heads),
            grid=(steps,),
            in_specs=[me_spec, shared_block, packed_block],
            out_specs=[whole_block, pl.BlockSpec((8, head_size), lambda s: (0, 0))],
            out_shape=[sent_shape, jax.ShapeDtypeStruct((8, head_size), F32)],
            scratch_shapes=[
                pltpu.VMEM(
                    (seq_count // 16, problems * 16 * CAP, 16 * (pair_rows + PACKED)), BF16
                ),
                pltpu.VMEM((slot_count, slot_count), F32),
                pltpu.VMEM((problems, slot_count, width), BF16),
                pltpu.VMEM((problems, slot_count, width), BF16),
                pltpu.VMEM((problems, head_size), F32),
            ],
            compiler_params=params(),
            cost_estimate=cost(
                steps * problems * 16 * 2 * slot_count * slot_count * head_size,
                steps * problems * slot_count * slot_count,
            ),
            name="own_rows",
        )(me, received, received)

    def unpack(chunk, base_rows, over_rows, returned, previous):
        column = pl.BlockSpec((tok_rows, 2 * head_size), lambda s: (0, chunk * steps + s))
        routes_block = pl.BlockSpec((tok_rows, heads), lambda s: (0, 0))
        centroid_block = pl.BlockSpec(
            (2, owned, head_size), lambda s: (chunk * steps + s, 0, 0)
        )
        return pl.pallas_call(
            functools.partial(unpack_rows_kernel, chunk * heads),
            grid=(steps,),
            in_specs=[
                me_spec,
                routes_block,
                routes_block,
                centroid_block,
                shared_block,
                packed_block,
            ]
            + [pl.BlockSpec(memory_space=pl.ANY)] * len(previous),
            out_specs=[column] * 4 + [centroid_block],
            out_shape=[pltpu.HBM((tok_rows, local_heads * head_size), BF16)] * 4
            + [pltpu.HBM(centroids.shape, F32)],
            input_output_aliases={6 + at: at for at in range(len(previous))},
            compiler_params=params(),
            cost_estimate=cost(2 * heads * 1536 * tok_rows * width),
            name="unpack_rows",
        )(
            me,
            base_rows.reshape(heads, tok_rows).T,
            over_rows.reshape(heads, tok_rows).T,
            centroids,
            returned,
            returned,
            *previous,
        )

    def exchange(rows):
        return lax.all_to_all(rows, "seq", split_axis=0, concat_axis=0, tiled=True)

    ahead = lax.axis_index("head") == 1

    def unwritten():
        shapes = jax.eval_shape(lambda: tuple(pack(1)))
        return tuple(
            pl.pallas_call(
                lambda *refs: None,
                out_specs=[pl.BlockSpec(memory_space=pl.ANY)] * len(shapes),
                out_shape=[jax.ShapeDtypeStruct(each.shape, each.dtype) for each in shapes],
                name="unwritten",
            )()
        )

    first = tuple(pack(0))
    early = lax.cond(ahead, lambda: tuple(pack(1)), unwritten)
    first, early = lax.optimization_barrier((first, early))
    second = lax.cond(ahead, lambda: early, lambda: tuple(pack(1)))
    packed = [first, second]
    received = [exchange(rows) for rows, _, _ in packed]
    owned_now = [own(chunk, received[chunk]) for chunk in range(CHUNKS)]
    returned = [exchange(back) for back, _ in owned_now]
    outs = ()
    for chunk in range(CHUNKS):
        outs = unpack(chunk, *packed[chunk][1:], returned[chunk], tuple(outs))

    peak = functools.reduce(jnp.maximum, [seen[0:1] for _, seen in owned_now])
    swap = [(at, 1 - at) for at in range(2)]
    peak = jnp.maximum(peak, lax.ppermute(peak, "head", swap))[0, PEAK_LANE]

    def lacking(state):
        return state[0]

    def again(state):
        full = dense(queries, keys, values, out_grad, cluster_ids, cluster_slot, centroids)
        return (jnp.zeros((), jnp.bool_), *full)

    state = lax.while_loop(lacking, again, (peak > PACKED - SPARE, *outs))
    return state[1:]


def solution(mesh):
    return jax.shard_map(
        body,
        mesh=mesh,
        in_specs=(
            P("seq", "head"),
            P("seq", "head"),
            P("seq", "head"),
            P("seq", "head"),
            P("head", "seq", None),
            P(),
            P("head", "seq", None),
        ),
        out_specs=(
            P("seq", "head"),
            P("seq", "head"),
            P("seq", "head"),
            P("seq", "head"),
            P("head", "seq", None),
        ),
        check_vma=False,
    )
```

```python
import functools
import math

import jax
import jax.numpy as jnp
from jax import lax
from jax.experimental import pallas as pl
from jax.experimental.pallas import tpu as pltpu
from jax.sharding import PartitionSpec as P

CAP = 4
DECAY_RATE = 0.9
MASKED = -1e30
ABSENT = 64.0
CHUNKS = 2
SHARED = 8
PACKED = 16
SPARE = 2
PEAK_LANE = 127
TURN_BY = 8
VMEM_BYTES = 63 * 1024 * 1024
LESS_VMEM_BYTES = 40 * 1024 * 1024

F32 = jnp.float32
BF16 = jnp.bfloat16
CONTRACT_LAST = (((1,), (1,)), ((), ()))
CONTRACT_FIRST = (((0,), (0,)), ((), ()))


def iota(shape, dim):
    return lax.broadcasted_iota(jnp.int32, shape, dim)


def dot(left, right):
    return jnp.dot(left, right, preferred_element_type=F32)


def pack_kernel(ids_ref, slot_ref, q_ref, k_ref, v_ref, g_ref, send_ref, flat_ref, earlier_ref):
    tok_rows = ids_ref.shape[2]
    cluster_count = slot_ref.shape[1]
    slot_rows = cluster_count * CAP

    @pl.when(pl.program_id(0) == 0)
    def _():
        earlier_ref[...] = (iota((tok_rows, tok_rows), 0) < iota((tok_rows, tok_rows), 1)).astype(
            F32
        ).astype(BF16)

    ids_row = ids_ref[0]
    member = iota((cluster_count, tok_rows), 0) == ids_row
    member_f = jnp.where(member, 1.0, 0.0)
    member_low = member_f.astype(BF16)
    slots_low = jnp.broadcast_to(slot_ref[...].astype(F32), (8, cluster_count)).astype(BF16)
    slot_row = dot(slots_low, member_low)[0:1]
    rank_row = jnp.sum(dot(member_low, earlier_ref[...]) * member_f, axis=0, keepdims=True)
    flat_row = (slot_row * CAP + rank_row).astype(jnp.int32)
    flat_ref[0] = flat_row
    place = jnp.where(iota((slot_rows, tok_rows), 0) == flat_row, 1.0, 0.0).astype(BF16)
    ones = jnp.ones((tok_rows, 128), BF16)
    head_size = q_ref.shape[1]
    taken = dot(place, ones)
    out_shape = send_ref.shape[:2] + (head_size,)

    def put(at, rows):
        send_ref[:, :, at * head_size : (at + 1) * head_size] = rows.astype(BF16).reshape(out_shape)

    put(0, dot(place, q_ref[...]))
    put(1, dot(place, k_ref[...]) + (1.0 - taken) * ABSENT)
    put(2, dot(place, v_ref[...]))
    put(3, dot(place, g_ref[...]))


def owner_kernel(recv_ref, cent_ref, back_ref, new_ref, turn_ref, causal_ref, rows_ref, grads_ref):
    source_count, block_rows, width = recv_ref.shape
    head_size = width // 4
    owned = block_rows // CAP
    slot_count = source_count * CAP
    group_rows = 16 * block_rows
    groups = source_count // 16
    part = 16 * CAP
    score_scale = 1.0 / math.sqrt(head_size)

    @pl.when(pl.program_id(0) == 0)
    def _():
        row_at = iota((group_rows, group_rows), 0)
        col_at = iota((group_rows, group_rows), 1)
        cluster_of = row_at // part
        source_of = (row_at % part) // CAP
        from_row = source_of * block_rows + cluster_of * CAP + row_at % CAP
        turn_ref[...] = jnp.where(from_row == col_at, 1.0, 0.0).astype(BF16)
        causal_ref[...] = jnp.where(
            iota((slot_count, slot_count), 1) <= iota((slot_count, slot_count), 0), 0.0, MASKED
        )

    turn = turn_ref[...]
    @pl.loop(0, groups)
    def _(group):
        arrived = recv_ref[pl.ds(group * 16, 16)].reshape(group_rows, width)
        turned = dot(turn, arrived).astype(BF16)
        at_row = pl.multiple_of(group * part, part)
        rows_ref[:, pl.ds(at_row, part), :] = turned.reshape(owned, part, width)

    first_lane = jnp.where(iota((8, head_size), 1) == 0, 1.0, 0.0).astype(BF16)
    @pl.loop(0, owned)
    def _(cluster):
        q = rows_ref[cluster, :, 0:head_size]
        k = rows_ref[cluster, :, head_size : 2 * head_size]
        v = rows_ref[cluster, :, 2 * head_size : 3 * head_size]
        g = rows_ref[cluster, :, 3 * head_size : 4 * head_size]
        marks = lax.dot_general(first_lane, k, CONTRACT_LAST, preferred_element_type=F32)
        present = marks < ABSENT / 2
        bias = jnp.where(present, 0.0, MASKED)[0:1]
        scores = lax.dot_general(q, k, CONTRACT_LAST, preferred_element_type=F32) * score_scale
        scores = scores + (causal_ref[...] + bias)
        weights = jnp.exp(scores - jnp.max(scores, axis=-1, keepdims=True))
        probs = weights / jnp.sum(weights, axis=-1, keepdims=True)
        probs_low = probs.astype(BF16)
        out = dot(probs_low, v).astype(BF16)
        grad_prob = lax.dot_general(g, v, CONTRACT_LAST, preferred_element_type=F32)
        delta = jnp.sum(g.astype(F32) * out.astype(F32), axis=-1, keepdims=True)
        grad_score = (probs * (grad_prob - delta) * score_scale).astype(BF16)
        grad_q = dot(grad_score, k)
        grad_k = lax.dot_general(grad_score, q, CONTRACT_FIRST, preferred_element_type=F32)
        grad_v = lax.dot_general(probs_low, g, CONTRACT_FIRST, preferred_element_type=F32)
        grads_ref[cluster, :, 0:head_size] = out
        grads_ref[cluster, :, head_size : 2 * head_size] = grad_q.astype(BF16)
        grads_ref[cluster, :, 2 * head_size : 3 * head_size] = grad_k.astype(BF16)
        grads_ref[cluster, :, 3 * head_size : 4 * head_size] = grad_v.astype(BF16)
        key_sums = dot(jnp.where(present, 1.0, 0.0).astype(BF16), k)[0:1]
        blend = DECAY_RATE * cent_ref[0, pl.ds(cluster, 1), :] + (1.0 - DECAY_RATE) * key_sums
        new_ref[0, pl.ds(cluster, 1), :] = blend / jnp.sqrt(
            jnp.mean(blend * blend, axis=-1, keepdims=True) + 1e-06
        )

    @pl.loop(0, groups)
    def _(group):
        at_row = pl.multiple_of(group * part, part)
        leaving = grads_ref[:, pl.ds(at_row, part), :].reshape(group_rows, width)
        turned = lax.dot_general(turn, leaving, CONTRACT_FIRST, preferred_element_type=F32)
        back_ref[pl.ds(group * 16, 16)] = turned.astype(BF16).reshape(16, block_rows, width)


def unpack_kernel(chunk, flat_ref, ret_ref, *refs):
    out_refs = refs[-4:]
    sources, block_rows, width = ret_ref.shape
    head_size = width // 4
    tok_rows, heads = flat_ref.shape
    slot_rows = sources * block_rows
    here = iota((tok_rows, heads), 1) == pl.program_id(0)
    flat_col = jnp.sum(jnp.where(here, flat_ref[...], 0), axis=1, keepdims=True)
    take = jnp.where(iota((tok_rows, slot_rows), 1) == flat_col, 1.0, 0.0).astype(BF16)
    rows = dot(take, ret_ref[...].reshape(slot_rows, width)).astype(BF16)
    for at, out_ref in enumerate(out_refs):
        out_ref[...] = rows[:, at * head_size : (at + 1) * head_size]


def find_rows(first_head, ids_ref, slot_ref, base_ref, over_ref, header_ref):
    heads, _, tok_rows = ids_ref.shape
    cluster_count = slot_ref.shape[1]
    owners, lanes = header_ref.shape
    earlier = jnp.where(
        iota((tok_rows, tok_rows), 0) < iota((tok_rows, tok_rows), 1), 1.0, 0.0
    ).astype(BF16)
    slots_low = jnp.broadcast_to(slot_ref[...].astype(F32), (8, cluster_count)).astype(BF16)
    members = [
        jnp.where(iota((cluster_count, tok_rows), 0) == ids_ref[head], 1.0, 0.0)
        for head in range(heads)
    ]
    member_low = jnp.concatenate(members, axis=0).astype(BF16)
    earlier_members = dot(member_low, earlier)
    owner_of, tag_of, here_of = [], [], []
    for head in range(heads):
        own = slice(head * cluster_count, (head + 1) * cluster_count)
        slot = dot(slots_low, member_low[own])[0:1].astype(jnp.int32)
        rank = jnp.sum(earlier_members[own] * members[head], axis=0, keepdims=True)
        owner = (slot // CAP + TURN_BY * (first_head + head)) % owners
        owner_of.append(owner)
        tag_of.append((head * CAP + slot % CAP) * CAP + rank.astype(jnp.int32))
        here_of.append(jnp.where(iota((owners, tok_rows), 0) == owner, 1.0, 0.0))
    before_all = dot(jnp.concatenate(here_of, axis=0).astype(BF16), earlier)
    filled = jnp.zeros((owners, 1), F32)
    header = jnp.zeros((owners, lanes), F32)
    for head in range(heads):
        here_f = here_of[head]
        before = before_all[head * owners : (head + 1) * owners]
        place = jnp.sum(before * here_f, axis=0, keepdims=True).astype(jnp.int32)
        late = jnp.sum((before + filled) * here_f, axis=0, keepdims=True)
        late = late.astype(jnp.int32) - SHARED
        filled = filled + jnp.maximum(jnp.sum(here_f, axis=1, keepdims=True) - SHARED, 0.0)
        fits = place < SHARED
        packs = (late < PACKED - SPARE) & (place >= SHARED)
        base_ref[head] = jnp.where(fits, owner_of[head] * SHARED + place, -1)
        over_ref[head] = jnp.where(packs, owner_of[head] * PACKED + late, -1)
        lane = jnp.where(fits, head * SHARED + place, jnp.where(packs, heads * SHARED + late, -1))
        named = (here_f * (tag_of[head] + 1).astype(F32)).astype(BF16)
        lane_at = jnp.where(iota((lanes, tok_rows), 0) == lane, 1.0, 0.0).astype(BF16)
        header = header + lax.dot_general(
            named, lane_at, CONTRACT_LAST, preferred_element_type=F32
        )
    peak = jnp.max(filled, axis=0, keepdims=True)
    header_ref[...] = jnp.where(iota((owners, lanes), 1) == PEAK_LANE, peak, header).astype(BF16)


def token_rows(columns_ref, step, at, head_size):
    lanes = slice(at * head_size, (at + 1) * head_size)
    parts = [columns_ref[step, which, :, lanes] for which in range(columns_ref.shape[1])]
    return jnp.concatenate(parts, axis=1)


def pack_rows_kernel(
    first_head,
    ids_ref,
    slot_ref,
    q_ref,
    k_ref,
    v_ref,
    g_ref,
    send_ref,
    base_ref,
    over_ref,
    header_ref,
    total_ref,
    columns_ref,
    arrived_ref,
):
    owners, send_rows, width = send_ref.shape
    tok_rows = q_ref.shape[0]
    head_size = width // 4
    step = pl.program_id(0)

    steps = columns_ref.shape[0]

    def column_copy(at_step, which):
        lanes = pl.ds((first_head + 2 * at_step) * head_size, 2 * head_size)
        return pltpu.make_async_copy(
            (q_ref, k_ref, v_ref, g_ref)[which].at[:, lanes],
            columns_ref.at[at_step, which],
            arrived_ref.at[at_step, which],
        )

    @pl.when(step == 0)
    def _():
        for at_step in range(steps):
            for which in range(4):
                column_copy(at_step, which).start()
        find_rows(first_head, ids_ref, slot_ref, base_ref, over_ref, header_ref)

    for at_step in range(steps):

        @pl.when(step == at_step)
        def _():
            for which in range(4):
                column_copy(at_step, which).wait()

    rows = [token_rows(columns_ref, step, at, head_size) for at in range(2)]
    halves = []
    for at in range(2):
        place = iota((owners * SHARED, tok_rows), 0) == base_ref[step * 2 + at]
        placed = dot(jnp.where(place, 1.0, 0.0).astype(BF16), rows[at])
        halves.append(placed.reshape(owners, SHARED, width))
    at_row = pl.multiple_of(step * 2 * SHARED, 2 * SHARED)
    shared = jnp.concatenate(halves, axis=1).astype(BF16)
    send_ref[:, pl.ds(at_row, 2 * SHARED), :] = shared

    places = [
        jnp.where(iota((owners * PACKED, tok_rows), 0) == over_ref[step * 2 + at], 1.0, 0.0).astype(BF16)
        for at in range(2)
    ]
    added = dot(jnp.concatenate(places, axis=1), jnp.concatenate(rows, axis=0))

    @pl.when(step == 0)
    def _():
        total_ref[...] = added

    @pl.when(step == pl.num_programs(0) - 1)
    def _():
        total = total_ref[...] + added
        last_row = iota((owners * PACKED, owners), 1) * PACKED + PACKED - 1
        to_last = jnp.where(iota((owners * PACKED, owners), 0) == last_row, 1.0, 0.0)
        tags = dot(to_last.astype(BF16), header_ref[...])
        total = jnp.concatenate([total[:, :head_size] + tags, total[:, head_size:]], axis=1)
        packed = total.astype(BF16).reshape(owners, PACKED, width)
        send_ref[:, send_rows - PACKED :, :] = packed


def own_rows_kernel(
    first_head,
    me_ref,
    shared_ref,
    over_ref,
    back_ref,
    peak_ref,
    turn_ref,
    causal_ref,
    rows_ref,
    grads_ref,
    sums_ref,
):
    sources, pair_rows, width = shared_ref.shape
    head_size = width // 4
    problems = rows_ref.shape[0]
    owned = problems // 2
    slot_count = sources * CAP
    bunch = 16
    groups = sources // bunch
    part = bunch * CAP
    shared_count = bunch * pair_rows
    packed_count = bunch * PACKED
    score_scale = 1.0 / math.sqrt(head_size)
    step = pl.program_id(0)
    steps = pl.num_programs(0)

    @pl.when(step == 0)
    def _():
        at = iota((slot_count, slot_count), 0)
        causal_ref[...] = jnp.where(iota((slot_count, slot_count), 1) <= at, 0.0, MASKED)

    header_of = jnp.where(
        iota((bunch, packed_count), 1) == iota((bunch, packed_count), 0) * PACKED + PACKED - 1,
        1.0,
        0.0,
    ).astype(BF16)

    def turns(header, first_lane, rows_each, used):
        count = bunch * rows_each
        lane = iota((head_size, count), 1) % rows_each
        match = (iota((head_size, count), 0) == lane + first_lane) & (lane < used)
        tags = dot(header, jnp.where(match, 1.0, 0.0).astype(BF16))
        source = iota((1, count), 1) // rows_each
        own = iota((bunch, count), 0) == source
        tag = jnp.sum(jnp.where(own, tags, 0.0), axis=0, keepdims=True).astype(jnp.int32) - 1
        mine = (tag >= 0) & (tag // (problems * CAP) == step)
        problem = (tag // CAP) % problems
        slot = jnp.where(mine, problem * part + source * CAP + tag % CAP, -1)
        hit = iota((problems * part, count), 0) == slot
        return jnp.where(hit, 1.0, 0.0).astype(BF16)

    ones = jnp.ones((shared_count + packed_count, head_size), BF16)
    peak_ref[...] = jnp.zeros(peak_ref.shape, F32)

    @pl.loop(0, groups)
    def _(group):
        from_sources = pl.ds(group * bunch, bunch)
        at_row = pl.multiple_of(group * part, part)
        packed = over_ref[from_sources].reshape(packed_count, width)
        shared = shared_ref[from_sources].reshape(shared_count, width)
        header = dot(header_of, packed[:, :head_size])
        peak_ref[...] = jnp.maximum(peak_ref[...], jnp.max(header, axis=0, keepdims=True))
        header = header.astype(BF16)
        turn = jnp.concatenate(
            [
                turns(header, step * pair_rows, pair_rows, pair_rows),
                turns(header, steps * pair_rows, PACKED, PACKED - SPARE),
            ],
            axis=1,
        )
        turn_ref[group] = turn
        turned = dot(turn, jnp.concatenate([shared, packed], axis=0))
        marked = turned[:, head_size : 2 * head_size] + (1.0 - dot(turn, ones)) * ABSENT
        turned = jnp.concatenate(
            [turned[:, :head_size], marked, turned[:, 2 * head_size :]], axis=1
        )
        rows_ref[:, pl.ds(at_row, part), :] = turned.astype(BF16).reshape(problems, part, width)

    first_lane = jnp.where(iota((8, head_size), 1) == 0, 1.0, 0.0).astype(BF16)

    def attend(problem):
        q = rows_ref[problem, :, 0:head_size]
        k = rows_ref[problem, :, head_size : 2 * head_size]
        v = rows_ref[problem, :, 2 * head_size : 3 * head_size]
        g = rows_ref[problem, :, 3 * head_size : 4 * head_size]
        marks = lax.dot_general(first_lane, k, CONTRACT_LAST, preferred_element_type=F32)
        present = marks < ABSENT / 2
        bias = jnp.where(present, 0.0, MASKED)[0:1]
        scores = lax.dot_general(q, k, CONTRACT_LAST, preferred_element_type=F32) * score_scale
        scores = scores + (causal_ref[...] + bias)
        weights = jnp.exp(scores - jnp.max(scores, axis=-1, keepdims=True))
        probs = weights / jnp.sum(weights, axis=-1, keepdims=True)
        probs_low = probs.astype(BF16)
        out = dot(probs_low, v).astype(BF16)
        grad_prob = lax.dot_general(g, v, CONTRACT_LAST, preferred_element_type=F32)
        delta = jnp.sum(g.astype(F32) * out.astype(F32), axis=-1, keepdims=True)
        grad_score = (probs * (grad_prob - delta) * score_scale).astype(BF16)
        grad_q = dot(grad_score, k)
        grad_k = lax.dot_general(grad_score, q, CONTRACT_FIRST, preferred_element_type=F32)
        grad_v = lax.dot_general(probs_low, g, CONTRACT_FIRST, preferred_element_type=F32)
        grads_ref[problem, :, 0:head_size] = out
        grads_ref[problem, :, head_size : 2 * head_size] = grad_q.astype(BF16)
        grads_ref[problem, :, 2 * head_size : 3 * head_size] = grad_k.astype(BF16)
        grads_ref[problem, :, 3 * head_size : 4 * head_size] = grad_v.astype(BF16)
        sums = dot(jnp.where(present, 1.0, 0.0).astype(BF16), k)[0:1]
        sums_ref[pl.ds(problem, 1), :] = sums

    @pl.loop(0, problems // 2)
    def _(pair):
        attend(pair * 2)
        attend(pair * 2 + 1)

    rest = slice(back_ref.shape[1] - PACKED, back_ref.shape[1])
    at_pair = pl.multiple_of(step * pair_rows, pair_rows)

    @pl.loop(0, groups)
    def _(group):
        from_sources = pl.ds(group * bunch, bunch)
        at_row = pl.multiple_of(group * part, part)
        leaving = grads_ref[:, pl.ds(at_row, part), :].reshape(problems * part, width)
        sent = lax.dot_general(
            turn_ref[group], leaving, CONTRACT_FIRST, preferred_element_type=F32
        ).astype(BF16)
        back_ref[from_sources, pl.ds(at_pair, pair_rows), :] = sent[:shared_count].reshape(
            bunch, pair_rows, width
        )
        packed = sent[shared_count:].reshape(bunch, PACKED, width)

        @pl.when(step == 0)
        def _():
            back_ref[from_sources, rest, :] = packed

        @pl.when(step > 0)
        def _():
            back_ref[from_sources, rest, :] += packed

    for at in range(2):
        sums = jnp.concatenate(
            [sums_ref[at * owned + slot : at * owned + slot + 1, :] for slot in range(owned)],
            axis=1,
        )
        high = sums.astype(BF16).astype(F32)
        low = sums - high
        turned_by = TURN_BY * (first_head + step * 2 + at)
        home = lax.rem(me_ref[0] + sources * TURN_BY - turned_by, sources)
        row = iota((PACKED, width), 0)
        tile = back_ref[home, rest, :].astype(F32)
        tile = jnp.where(row == PACKED - 2, high, jnp.where(row == PACKED - 1, low, tile))
        back_ref[home, rest, :] = tile.astype(BF16)


def unpack_rows_kernel(
    first_head, me_ref, base_ref, over_ref, cent_ref, shared_ref, packed_ref, *refs
):
    new_ref = refs[-1]
    out_refs = refs[-5:-1]
    owners, _, width = shared_ref.shape
    head_size = width // 4
    owned = cent_ref.shape[1]
    tok_rows, heads = base_ref.shape
    step = pl.program_id(0)
    packed = packed_ref[...].reshape(owners * PACKED, width)
    arrived = shared_ref[...].astype(F32)
    for at in range(2):
        here = iota((tok_rows, heads), 1) == step * 2 + at
        base = jnp.sum(jnp.where(here, base_ref[...], 0), axis=1, keepdims=True)
        over = jnp.sum(jnp.where(here, over_ref[...], 0), axis=1, keepdims=True)
        take = iota((tok_rows, owners * SHARED), 1) == base
        take_over = iota((tok_rows, owners * PACKED), 1) == over
        mine = arrived[:, at * SHARED : (at + 1) * SHARED, :].reshape(owners * SHARED, width)
        rows = dot(jnp.where(take, 1.0, 0.0).astype(BF16), mine.astype(BF16))
        rows = rows + dot(jnp.where(take_over, 1.0, 0.0).astype(BF16), packed)
        rows = rows.astype(BF16)
        for which, out_ref in enumerate(out_refs):
            out_ref[:, at * head_size : (at + 1) * head_size] = rows[
                :, which * head_size : (which + 1) * head_size
            ]
        turned_by = TURN_BY * (first_head + step * 2 + at)
        tile = packed_ref[lax.rem(me_ref[0] + turned_by, owners)].astype(F32)
        spare = iota((PACKED, width), 0) >= PACKED - 2
        key_sums = jnp.sum(jnp.where(spare, tile, 0.0), axis=0, keepdims=True)
        for slot in range(owned):
            blend = DECAY_RATE * cent_ref[at, slot : slot + 1, :]
            blend += (1.0 - DECAY_RATE) * key_sums[:, slot * head_size : (slot + 1) * head_size]
            new_ref[at, slot : slot + 1, :] = blend / jnp.sqrt(
                jnp.mean(blend * blend, axis=-1, keepdims=True) + 1e-06
            )


def params(limit=VMEM_BYTES):
    return pltpu.CompilerParams(vmem_limit_bytes=limit)


def dense(queries, keys, values, out_grad, cluster_ids, cluster_slot, centroids):
    seq_count = lax.axis_size("seq")
    local_heads, tok_rows = cluster_ids.shape[:2]
    cluster_count = cluster_slot.shape[0]
    owned = cluster_count // seq_count
    head_size = centroids.shape[2]
    heads = local_heads
    block_rows = owned * CAP
    width = 4 * head_size
    slot_count = seq_count * CAP
    sent = jax.ShapeDtypeStruct((seq_count, heads * block_rows, width), BF16)
    sent_bytes = seq_count * heads * block_rows * width * 2
    ids_rows = cluster_ids.reshape(local_heads, 1, tok_rows)
    slot_row = cluster_slot.reshape(1, cluster_count)
    block = pl.BlockSpec((seq_count, block_rows, width), lambda h: (0, h, 0))

    def exchange(rows):
        return lax.all_to_all(rows, "seq", split_axis=0, concat_axis=0, tiled=True)

    def pack(chunk):
        column = pl.BlockSpec((tok_rows, head_size), lambda h: (0, chunk * heads + h))
        return pl.pallas_call(
            pack_kernel,
            grid=(heads,),
            in_specs=[
                pl.BlockSpec((1, 1, tok_rows), lambda h: (chunk * heads + h, 0, 0)),
                pl.BlockSpec((1, cluster_count), lambda h: (0, 0)),
                column,
                column,
                column,
                column,
            ],
            out_specs=[block, pl.BlockSpec((1, 1, tok_rows), lambda h: (h, 0, 0))],
            out_shape=[sent, jax.ShapeDtypeStruct((heads, 1, tok_rows), jnp.int32)],
            scratch_shapes=[pltpu.VMEM((tok_rows, tok_rows), BF16)],
            compiler_params=params(),
            cost_estimate=pl.CostEstimate(
                flops=heads * 2 * 1024 * 512 * 640, bytes_accessed=2 * sent_bytes, transcendentals=0
            ),
            name="pack",
        )(ids_rows, slot_row, queries, keys, values, out_grad)

    def own(chunk, received):
        return pl.pallas_call(
            owner_kernel,
            grid=(heads,),
            in_specs=[
                block,
                pl.BlockSpec((1, owned, head_size), lambda h: (chunk * heads + h, 0, 0)),
            ],
            out_specs=[block, pl.BlockSpec((1, owned, head_size), lambda h: (h, 0, 0))],
            out_shape=[sent, jax.ShapeDtypeStruct((heads, owned, head_size), F32)],
            scratch_shapes=[
                pltpu.VMEM((16 * block_rows, 16 * block_rows), BF16),
                pltpu.VMEM((slot_count, slot_count), F32),
                pltpu.VMEM((owned, slot_count, width), BF16),
                pltpu.VMEM((owned, slot_count, width), BF16),
            ],
            compiler_params=params(),
            cost_estimate=pl.CostEstimate(
                flops=heads * owned * 7 * 2 * slot_count * slot_count * head_size,
                bytes_accessed=2 * sent_bytes,
                transcendentals=heads * owned * slot_count * slot_count,
            ),
            name="own",
        )(received, centroids)

    def unpack(chunk, flat_cols, returned, previous):
        column = pl.BlockSpec((tok_rows, head_size), lambda h: (0, chunk * heads + h))
        whole = jax.ShapeDtypeStruct((tok_rows, local_heads * head_size), BF16)

        def kernel(*refs):
            unpack_kernel(chunk, *refs)

        return pl.pallas_call(
            kernel,
            grid=(heads,),
            in_specs=[pl.BlockSpec((tok_rows, heads), lambda h: (0, 0)), block]
            + [pl.BlockSpec(memory_space=pl.ANY)] * len(previous),
            out_specs=[column] * 4,
            out_shape=[whole] * 4,
            input_output_aliases={2 + i: i for i in range(len(previous))},
            compiler_params=params(),
            cost_estimate=pl.CostEstimate(
                flops=heads * 2 * 1024 * 512 * 512, bytes_accessed=2 * sent_bytes, transcendentals=0
            ),
            name="unpack",
        )(flat_cols, returned, *previous)

    packed = [pack(chunk) for chunk in range(1)]
    received = [exchange(rows) for rows, _ in packed]
    owned_now = [own(chunk, rows) for chunk, rows in enumerate(received)]
    returned = [exchange(rows) for rows, _ in owned_now]
    outs = ()
    for chunk in range(1):
        flat_cols = packed[chunk][1].reshape(heads, tok_rows).T
        outs = unpack(chunk, flat_cols, returned[chunk], tuple(outs))
    new_centroids = jnp.concatenate([new for _, new in owned_now], axis=0)
    return (*outs, new_centroids)


def body(queries, keys, values, out_grad, cluster_ids, cluster_slot, centroids):
    seq_count = lax.axis_size("seq")
    local_heads, tok_rows = cluster_ids.shape[:2]
    cluster_count = cluster_slot.shape[0]
    owned, head_size = centroids.shape[1:]
    heads = local_heads // CHUNKS
    width = 4 * head_size
    pair_rows = 2 * SHARED
    steps = heads // 2
    send_rows = steps * pair_rows + PACKED
    slot_count = seq_count * CAP
    problems = 2 * owned
    block_bytes = seq_count * pair_rows * width * 2
    sent_shape = jax.ShapeDtypeStruct((seq_count, send_rows, width), BF16)
    ids_rows = cluster_ids.reshape(local_heads, 1, tok_rows)
    slot_row = cluster_slot.reshape(1, cluster_count)
    me = lax.axis_index("seq").reshape(1)

    def cost(flops, exps=0):
        return pl.CostEstimate(
            flops=flops, bytes_accessed=2 * (steps + 1) * block_bytes, transcendentals=exps
        )

    shared_block = pl.BlockSpec((seq_count, pair_rows, width), lambda s: (0, s, 0))
    packed_block = pl.BlockSpec((seq_count, PACKED, width), lambda s: (0, steps, 0))
    whole_block = pl.BlockSpec((seq_count, send_rows, width), lambda s: (0, 0, 0))
    me_spec = pl.BlockSpec(memory_space=pltpu.SMEM)

    def pack(chunk):
        row_shape = jax.ShapeDtypeStruct((heads, 1, tok_rows), jnp.int32)
        rows_block = pl.BlockSpec((heads, 1, tok_rows), lambda s: (0, 0, 0))
        return pl.pallas_call(
            functools.partial(pack_rows_kernel, chunk * heads),
            grid=(steps,),
            in_specs=[
                pl.BlockSpec((heads, 1, tok_rows), lambda s: (chunk, 0, 0)),
                pl.BlockSpec((1, cluster_count), lambda s: (0, 0)),
            ]
            + [pl.BlockSpec(memory_space=pl.ANY)] * 4,
            out_specs=[whole_block, rows_block, rows_block],
            out_shape=[sent_shape, row_shape, row_shape],
            scratch_shapes=[
                pltpu.VMEM((seq_count, head_size), BF16),
                pltpu.VMEM((seq_count * PACKED, width), F32),
                pltpu.VMEM((steps, 4, tok_rows, 2 * head_size), BF16),
                pltpu.SemaphoreType.DMA((steps, 4)),
            ],
            compiler_params=params(),
            cost_estimate=cost(2 * heads * 1536 * tok_rows * width),
            name="pack_rows",
        )(ids_rows, slot_row, queries, keys, values, out_grad)

    def own(chunk, received):
        return pl.pallas_call(
            functools.partial(own_rows_kernel, chunk * heads),
            grid=(steps,),
            in_specs=[me_spec, shared_block, packed_block],
            out_specs=[whole_block, pl.BlockSpec((8, head_size), lambda s: (0, 0))],
            out_shape=[sent_shape, jax.ShapeDtypeStruct((8, head_size), F32)],
            scratch_shapes=[
                pltpu.VMEM(
                    (seq_count // 16, problems * 16 * CAP, 16 * (pair_rows + PACKED)), BF16
                ),
                pltpu.VMEM((slot_count, slot_count), F32),
                pltpu.VMEM((problems, slot_count, width), BF16),
                pltpu.VMEM((problems, slot_count, width), BF16),
                pltpu.VMEM((problems, head_size), F32),
            ],
            compiler_params=params(),
            cost_estimate=cost(
                steps * problems * 16 * 2 * slot_count * slot_count * head_size,
                steps * problems * slot_count * slot_count,
            ),
            name="own_rows",
        )(me, received, received)

    def unpack(chunk, base_rows, over_rows, returned, previous):
        column = pl.BlockSpec((tok_rows, 2 * head_size), lambda s: (0, chunk * steps + s))
        routes_block = pl.BlockSpec((tok_rows, heads), lambda s: (0, 0))
        centroid_block = pl.BlockSpec(
            (2, owned, head_size), lambda s: (chunk * steps + s, 0, 0)
        )
        return pl.pallas_call(
            functools.partial(unpack_rows_kernel, chunk * heads),
            grid=(steps,),
            in_specs=[
                me_spec,
                routes_block,
                routes_block,
                centroid_block,
                shared_block,
                packed_block,
            ]
            + [pl.BlockSpec(memory_space=pl.ANY)] * len(previous),
            out_specs=[column] * 4 + [centroid_block],
            out_shape=[pltpu.HBM((tok_rows, local_heads * head_size), BF16)] * 4
            + [pltpu.HBM(centroids.shape, F32)],
            input_output_aliases={6 + at: at for at in range(len(previous))},
            compiler_params=params(LESS_VMEM_BYTES),
            cost_estimate=cost(2 * heads * 1536 * tok_rows * width),
            name="unpack_rows",
        )(
            me,
            base_rows.reshape(heads, tok_rows).T,
            over_rows.reshape(heads, tok_rows).T,
            centroids,
            returned,
            returned,
            *previous,
        )

    def exchange(rows):
        return lax.all_to_all(rows, "seq", split_axis=0, concat_axis=0, tiled=True)

    packed = [pack(chunk) for chunk in range(CHUNKS)]
    received = [exchange(rows) for rows, _, _ in packed]
    owned_now = [own(chunk, received[chunk]) for chunk in range(CHUNKS)]
    returned = [exchange(back) for back, _ in owned_now]
    outs = ()
    for chunk in range(CHUNKS):
        outs = unpack(chunk, *packed[chunk][1:], returned[chunk], tuple(outs))

    peak = functools.reduce(jnp.maximum, [seen[0:1] for _, seen in owned_now])
    swap = [(at, 1 - at) for at in range(2)]
    peak = jnp.maximum(peak, lax.ppermute(peak, "head", swap))[0, PEAK_LANE]

    def lacking(state):
        return state[0]

    def again(state):
        full = dense(queries, keys, values, out_grad, cluster_ids, cluster_slot, centroids)
        return (jnp.zeros((), jnp.bool_), *full)

    state = lax.while_loop(lacking, again, (peak > PACKED - SPARE, *outs))
    return state[1:]


def solution(mesh):
    return jax.shard_map(
        body,
        mesh=mesh,
        in_specs=(
            P("seq", "head"),
            P("seq", "head"),
            P("seq", "head"),
            P("seq", "head"),
            P("head", "seq", None),
            P(),
            P("head", "seq", None),
        ),
        out_specs=(
            P("seq", "head"),
            P("seq", "head"),
            P("seq", "head"),
            P("seq", "head"),
            P("head", "seq", None),
        ),
        check_vma=False,
    )
```

```python
import functools
import math

import jax
import jax.numpy as jnp
from jax import lax
from jax.experimental import pallas as pl
from jax.experimental.pallas import tpu as pltpu
from jax.sharding import PartitionSpec as P

CAP = 4
DECAY_RATE = 0.9
MASKED = -1e30
ABSENT = 64.0
CHUNKS = 2
SHARED = 8
PACKED = 16
SPARE = 2
PEAK_LANE = 127
TURN_BY = 8
VMEM_BYTES = 63 * 1024 * 1024
LESS_VMEM_BYTES = 40 * 1024 * 1024

F32 = jnp.float32
BF16 = jnp.bfloat16
CONTRACT_LAST = (((1,), (1,)), ((), ()))
CONTRACT_FIRST = (((0,), (0,)), ((), ()))


def iota(shape, dim):
    return lax.broadcasted_iota(jnp.int32, shape, dim)


def dot(left, right):
    return jnp.dot(left, right, preferred_element_type=F32)


def pack_kernel(ids_ref, slot_ref, q_ref, k_ref, v_ref, g_ref, send_ref, flat_ref, earlier_ref):
    tok_rows = ids_ref.shape[2]
    cluster_count = slot_ref.shape[1]
    slot_rows = cluster_count * CAP

    @pl.when(pl.program_id(0) == 0)
    def _():
        earlier_ref[...] = (iota((tok_rows, tok_rows), 0) < iota((tok_rows, tok_rows), 1)).astype(
            F32
        ).astype(BF16)

    ids_row = ids_ref[0]
    member = iota((cluster_count, tok_rows), 0) == ids_row
    member_f = jnp.where(member, 1.0, 0.0)
    member_low = member_f.astype(BF16)
    slots_low = jnp.broadcast_to(slot_ref[...].astype(F32), (8, cluster_count)).astype(BF16)
    slot_row = dot(slots_low, member_low)[0:1]
    rank_row = jnp.sum(dot(member_low, earlier_ref[...]) * member_f, axis=0, keepdims=True)
    flat_row = (slot_row * CAP + rank_row).astype(jnp.int32)
    flat_ref[0] = flat_row
    place = jnp.where(iota((slot_rows, tok_rows), 0) == flat_row, 1.0, 0.0).astype(BF16)
    ones = jnp.ones((tok_rows, 128), BF16)
    head_size = q_ref.shape[1]
    taken = dot(place, ones)
    out_shape = send_ref.shape[:2] + (head_size,)

    def put(at, rows):
        send_ref[:, :, at * head_size : (at + 1) * head_size] = rows.astype(BF16).reshape(out_shape)

    put(0, dot(place, q_ref[...]))
    put(1, dot(place, k_ref[...]) + (1.0 - taken) * ABSENT)
    put(2, dot(place, v_ref[...]))
    put(3, dot(place, g_ref[...]))


def owner_kernel(recv_ref, cent_ref, back_ref, new_ref, turn_ref, causal_ref, rows_ref, grads_ref):
    source_count, block_rows, width = recv_ref.shape
    head_size = width // 4
    owned = block_rows // CAP
    slot_count = source_count * CAP
    group_rows = 16 * block_rows
    groups = source_count // 16
    part = 16 * CAP
    score_scale = 1.0 / math.sqrt(head_size)

    @pl.when(pl.program_id(0) == 0)
    def _():
        row_at = iota((group_rows, group_rows), 0)
        col_at = iota((group_rows, group_rows), 1)
        cluster_of = row_at // part
        source_of = (row_at % part) // CAP
        from_row = source_of * block_rows + cluster_of * CAP + row_at % CAP
        turn_ref[...] = jnp.where(from_row == col_at, 1.0, 0.0).astype(BF16)
        causal_ref[...] = jnp.where(
            iota((slot_count, slot_count), 1) <= iota((slot_count, slot_count), 0), 0.0, MASKED
        )

    turn = turn_ref[...]
    @pl.loop(0, groups)
    def _(group):
        arrived = recv_ref[pl.ds(group * 16, 16)].reshape(group_rows, width)
        turned = dot(turn, arrived).astype(BF16)
        at_row = pl.multiple_of(group * part, part)
        rows_ref[:, pl.ds(at_row, part), :] = turned.reshape(owned, part, width)

    first_lane = jnp.where(iota((8, head_size), 1) == 0, 1.0, 0.0).astype(BF16)
    @pl.loop(0, owned)
    def _(cluster):
        q = rows_ref[cluster, :, 0:head_size]
        k = rows_ref[cluster, :, head_size : 2 * head_size]
        v = rows_ref[cluster, :, 2 * head_size : 3 * head_size]
        g = rows_ref[cluster, :, 3 * head_size : 4 * head_size]
        marks = lax.dot_general(first_lane, k, CONTRACT_LAST, preferred_element_type=F32)
        present = marks < ABSENT / 2
        bias = jnp.where(present, 0.0, MASKED)[0:1]
        scores = lax.dot_general(q, k, CONTRACT_LAST, preferred_element_type=F32) * score_scale
        scores = scores + (causal_ref[...] + bias)
        weights = jnp.exp(scores - jnp.max(scores, axis=-1, keepdims=True))
        probs = weights / jnp.sum(weights, axis=-1, keepdims=True)
        probs_low = probs.astype(BF16)
        out = dot(probs_low, v).astype(BF16)
        grad_prob = lax.dot_general(g, v, CONTRACT_LAST, preferred_element_type=F32)
        delta = jnp.sum(g.astype(F32) * out.astype(F32), axis=-1, keepdims=True)
        grad_score = (probs * (grad_prob - delta) * score_scale).astype(BF16)
        grad_q = dot(grad_score, k)
        grad_k = lax.dot_general(grad_score, q, CONTRACT_FIRST, preferred_element_type=F32)
        grad_v = lax.dot_general(probs_low, g, CONTRACT_FIRST, preferred_element_type=F32)
        grads_ref[cluster, :, 0:head_size] = out
        grads_ref[cluster, :, head_size : 2 * head_size] = grad_q.astype(BF16)
        grads_ref[cluster, :, 2 * head_size : 3 * head_size] = grad_k.astype(BF16)
        grads_ref[cluster, :, 3 * head_size : 4 * head_size] = grad_v.astype(BF16)
        key_sums = dot(jnp.where(present, 1.0, 0.0).astype(BF16), k)[0:1]
        blend = DECAY_RATE * cent_ref[0, pl.ds(cluster, 1), :] + (1.0 - DECAY_RATE) * key_sums
        new_ref[0, pl.ds(cluster, 1), :] = blend / jnp.sqrt(
            jnp.mean(blend * blend, axis=-1, keepdims=True) + 1e-06
        )

    @pl.loop(0, groups)
    def _(group):
        at_row = pl.multiple_of(group * part, part)
        leaving = grads_ref[:, pl.ds(at_row, part), :].reshape(group_rows, width)
        turned = lax.dot_general(turn, leaving, CONTRACT_FIRST, preferred_element_type=F32)
        back_ref[pl.ds(group * 16, 16)] = turned.astype(BF16).reshape(16, block_rows, width)


def unpack_kernel(chunk, flat_ref, ret_ref, *refs):
    out_refs = refs[-4:]
    sources, block_rows, width = ret_ref.shape
    head_size = width // 4
    tok_rows, heads = flat_ref.shape
    slot_rows = sources * block_rows
    here = iota((tok_rows, heads), 1) == pl.program_id(0)
    flat_col = jnp.sum(jnp.where(here, flat_ref[...], 0), axis=1, keepdims=True)
    take = jnp.where(iota((tok_rows, slot_rows), 1) == flat_col, 1.0, 0.0).astype(BF16)
    rows = dot(take, ret_ref[...].reshape(slot_rows, width)).astype(BF16)
    for at, out_ref in enumerate(out_refs):
        out_ref[...] = rows[:, at * head_size : (at + 1) * head_size]


def find_rows(first_head, ids_ref, slot_ref, base_ref, over_ref, header_ref):
    heads, _, tok_rows = ids_ref.shape
    cluster_count = slot_ref.shape[1]
    owners, lanes = header_ref.shape
    earlier = jnp.where(
        iota((tok_rows, tok_rows), 0) < iota((tok_rows, tok_rows), 1), 1.0, 0.0
    ).astype(BF16)
    slots_low = jnp.broadcast_to(slot_ref[...].astype(F32), (8, cluster_count)).astype(BF16)
    members = [
        jnp.where(iota((cluster_count, tok_rows), 0) == ids_ref[head], 1.0, 0.0)
        for head in range(heads)
    ]
    member_low = jnp.concatenate(members, axis=0).astype(BF16)
    earlier_members = dot(member_low, earlier)
    owner_of, tag_of, here_of = [], [], []
    for head in range(heads):
        own = slice(head * cluster_count, (head + 1) * cluster_count)
        slot = dot(slots_low, member_low[own])[0:1].astype(jnp.int32)
        rank = jnp.sum(earlier_members[own] * members[head], axis=0, keepdims=True)
        owner = (slot // CAP + TURN_BY * (first_head + head)) % owners
        owner_of.append(owner)
        tag_of.append((head * CAP + slot % CAP) * CAP + rank.astype(jnp.int32))
        here_of.append(jnp.where(iota((owners, tok_rows), 0) == owner, 1.0, 0.0))
    before_all = dot(jnp.concatenate(here_of, axis=0).astype(BF16), earlier)
    filled = jnp.zeros((owners, 1), F32)
    header = jnp.zeros((owners, lanes), F32)
    for head in range(heads):
        here_f = here_of[head]
        before = before_all[head * owners : (head + 1) * owners]
        place = jnp.sum(before * here_f, axis=0, keepdims=True).astype(jnp.int32)
        late = jnp.sum((before + filled) * here_f, axis=0, keepdims=True)
        late = late.astype(jnp.int32) - SHARED
        filled = filled + jnp.maximum(jnp.sum(here_f, axis=1, keepdims=True) - SHARED, 0.0)
        fits = place < SHARED
        packs = (late < PACKED - SPARE) & (place >= SHARED)
        base_ref[head] = jnp.where(fits, owner_of[head] * SHARED + place, -1)
        over_ref[head] = jnp.where(packs, owner_of[head] * PACKED + late, -1)
        lane = jnp.where(fits, head * SHARED + place, jnp.where(packs, heads * SHARED + late, -1))
        named = (here_f * (tag_of[head] + 1).astype(F32)).astype(BF16)
        lane_at = jnp.where(iota((lanes, tok_rows), 0) == lane, 1.0, 0.0).astype(BF16)
        header = header + lax.dot_general(
            named, lane_at, CONTRACT_LAST, preferred_element_type=F32
        )
    peak = jnp.max(filled, axis=0, keepdims=True)
    header_ref[...] = jnp.where(iota((owners, lanes), 1) == PEAK_LANE, peak, header).astype(BF16)


def token_rows(columns_ref, step, at, head_size):
    lanes = slice(at * head_size, (at + 1) * head_size)
    parts = [columns_ref[step, which, :, lanes] for which in range(columns_ref.shape[1])]
    return jnp.concatenate(parts, axis=1)


def pack_rows_kernel(
    first_head,
    ids_ref,
    slot_ref,
    q_ref,
    k_ref,
    v_ref,
    g_ref,
    send_ref,
    base_ref,
    over_ref,
    header_ref,
    total_ref,
    columns_ref,
    arrived_ref,
):
    owners, send_rows, width = send_ref.shape
    tok_rows = q_ref.shape[0]
    head_size = width // 4
    step = pl.program_id(0)

    steps = columns_ref.shape[0]

    def column_copy(at_step, which):
        lanes = pl.ds((first_head + 2 * at_step) * head_size, 2 * head_size)
        return pltpu.make_async_copy(
            (q_ref, k_ref, v_ref, g_ref)[which].at[:, lanes],
            columns_ref.at[at_step, which],
            arrived_ref.at[at_step, which],
        )

    @pl.when(step == 0)
    def _():
        for at_step in range(steps):
            for which in range(4):
                column_copy(at_step, which).start()
        find_rows(first_head, ids_ref, slot_ref, base_ref, over_ref, header_ref)

    for at_step in range(steps):

        @pl.when(step == at_step)
        def _():
            for which in range(4):
                column_copy(at_step, which).wait()

    rows = [token_rows(columns_ref, step, at, head_size) for at in range(2)]
    halves = []
    for at in range(2):
        place = iota((owners * SHARED, tok_rows), 0) == base_ref[step * 2 + at]
        placed = dot(jnp.where(place, 1.0, 0.0).astype(BF16), rows[at])
        halves.append(placed.reshape(owners, SHARED, width))
    at_row = pl.multiple_of(step * 2 * SHARED, 2 * SHARED)
    shared = jnp.concatenate(halves, axis=1).astype(BF16)
    send_ref[:, pl.ds(at_row, 2 * SHARED), :] = shared

    places = [
        jnp.where(iota((owners * PACKED, tok_rows), 0) == over_ref[step * 2 + at], 1.0, 0.0).astype(BF16)
        for at in range(2)
    ]
    added = dot(jnp.concatenate(places, axis=1), jnp.concatenate(rows, axis=0))

    @pl.when(step == 0)
    def _():
        total_ref[...] = added

    @pl.when(step == pl.num_programs(0) - 1)
    def _():
        total = total_ref[...] + added
        last_row = iota((owners * PACKED, owners), 1) * PACKED + PACKED - 1
        to_last = jnp.where(iota((owners * PACKED, owners), 0) == last_row, 1.0, 0.0)
        tags = dot(to_last.astype(BF16), header_ref[...])
        total = jnp.concatenate([total[:, :head_size] + tags, total[:, head_size:]], axis=1)
        packed = total.astype(BF16).reshape(owners, PACKED, width)
        send_ref[:, send_rows - PACKED :, :] = packed


def own_rows_kernel(
    first_head,
    me_ref,
    shared_ref,
    over_ref,
    back_ref,
    peak_ref,
    turn_ref,
    causal_ref,
    rows_ref,
    grads_ref,
    sums_ref,
):
    sources, pair_rows, width = shared_ref.shape
    head_size = width // 4
    problems = rows_ref.shape[0]
    owned = problems // 2
    slot_count = sources * CAP
    bunch = 16
    groups = sources // bunch
    part = bunch * CAP
    shared_count = bunch * pair_rows
    packed_count = bunch * PACKED
    score_scale = 1.0 / math.sqrt(head_size)
    step = pl.program_id(0)
    steps = pl.num_programs(0)

    @pl.when(step == 0)
    def _():
        at = iota((slot_count, slot_count), 0)
        causal_ref[...] = jnp.where(iota((slot_count, slot_count), 1) <= at, 0.0, MASKED)

    header_of = jnp.where(
        iota((bunch, packed_count), 1) == iota((bunch, packed_count), 0) * PACKED + PACKED - 1,
        1.0,
        0.0,
    ).astype(BF16)

    def turns(header, first_lane, rows_each, used):
        count = bunch * rows_each
        lane = iota((head_size, count), 1) % rows_each
        match = (iota((head_size, count), 0) == lane + first_lane) & (lane < used)
        tags = dot(header, jnp.where(match, 1.0, 0.0).astype(BF16))
        source = iota((1, count), 1) // rows_each
        own = iota((bunch, count), 0) == source
        tag = jnp.sum(jnp.where(own, tags, 0.0), axis=0, keepdims=True).astype(jnp.int32) - 1
        mine = (tag >= 0) & (tag // (problems * CAP) == step)
        problem = (tag // CAP) % problems
        slot = jnp.where(mine, problem * part + source * CAP + tag % CAP, -1)
        hit = iota((problems * part, count), 0) == slot
        return jnp.where(hit, 1.0, 0.0).astype(BF16)

    ones = jnp.ones((shared_count + packed_count, head_size), BF16)
    peak_ref[...] = jnp.zeros(peak_ref.shape, F32)

    @pl.loop(0, groups)
    def _(group):
        from_sources = pl.ds(group * bunch, bunch)
        at_row = pl.multiple_of(group * part, part)
        packed = over_ref[from_sources].reshape(packed_count, width)
        shared = shared_ref[from_sources].reshape(shared_count, width)
        header = dot(header_of, packed[:, :head_size])
        peak_ref[...] = jnp.maximum(peak_ref[...], jnp.max(header, axis=0, keepdims=True))
        header = header.astype(BF16)
        turn = jnp.concatenate(
            [
                turns(header, step * pair_rows, pair_rows, pair_rows),
                turns(header, steps * pair_rows, PACKED, PACKED - SPARE),
            ],
            axis=1,
        )
        turn_ref[group] = turn
        turned = dot(turn, jnp.concatenate([shared, packed], axis=0))
        marked = turned[:, head_size : 2 * head_size] + (1.0 - dot(turn, ones)) * ABSENT
        turned = jnp.concatenate(
            [turned[:, :head_size], marked, turned[:, 2 * head_size :]], axis=1
        )
        rows_ref[:, pl.ds(at_row, part), :] = turned.astype(BF16).reshape(problems, part, width)

    first_lane = jnp.where(iota((8, head_size), 1) == 0, 1.0, 0.0).astype(BF16)

    def attend(problem):
        q = rows_ref[problem, :, 0:head_size]
        k = rows_ref[problem, :, head_size : 2 * head_size]
        v = rows_ref[problem, :, 2 * head_size : 3 * head_size]
        g = rows_ref[problem, :, 3 * head_size : 4 * head_size]
        marks = lax.dot_general(first_lane, k, CONTRACT_LAST, preferred_element_type=F32)
        present = marks < ABSENT / 2
        bias = jnp.where(present, 0.0, MASKED)[0:1]
        scores = lax.dot_general(q, k, CONTRACT_LAST, preferred_element_type=F32) * score_scale
        scores = scores + (causal_ref[...] + bias)
        weights = jnp.exp(scores - jnp.max(scores, axis=-1, keepdims=True))
        probs = weights / jnp.sum(weights, axis=-1, keepdims=True)
        probs_low = probs.astype(BF16)
        out = dot(probs_low, v).astype(BF16)
        grad_prob = lax.dot_general(g, v, CONTRACT_LAST, preferred_element_type=F32)
        delta = jnp.sum(g.astype(F32) * out.astype(F32), axis=-1, keepdims=True)
        grad_score = (probs * (grad_prob - delta) * score_scale).astype(BF16)
        grad_q = dot(grad_score, k)
        grad_k = lax.dot_general(grad_score, q, CONTRACT_FIRST, preferred_element_type=F32)
        grad_v = lax.dot_general(probs_low, g, CONTRACT_FIRST, preferred_element_type=F32)
        grads_ref[problem, :, 0:head_size] = out
        grads_ref[problem, :, head_size : 2 * head_size] = grad_q.astype(BF16)
        grads_ref[problem, :, 2 * head_size : 3 * head_size] = grad_k.astype(BF16)
        grads_ref[problem, :, 3 * head_size : 4 * head_size] = grad_v.astype(BF16)
        sums = dot(jnp.where(present, 1.0, 0.0).astype(BF16), k)[0:1]
        sums_ref[pl.ds(problem, 1), :] = sums

    @pl.loop(0, problems // 2)
    def _(pair):
        attend(pair * 2)
        attend(pair * 2 + 1)

    rest = slice(back_ref.shape[1] - PACKED, back_ref.shape[1])
    at_pair = pl.multiple_of(step * pair_rows, pair_rows)

    @pl.loop(0, groups)
    def _(group):
        from_sources = pl.ds(group * bunch, bunch)
        at_row = pl.multiple_of(group * part, part)
        leaving = grads_ref[:, pl.ds(at_row, part), :].reshape(problems * part, width)
        sent = lax.dot_general(
            turn_ref[group], leaving, CONTRACT_FIRST, preferred_element_type=F32
        ).astype(BF16)
        back_ref[from_sources, pl.ds(at_pair, pair_rows), :] = sent[:shared_count].reshape(
            bunch, pair_rows, width
        )
        packed = sent[shared_count:].reshape(bunch, PACKED, width)

        @pl.when(step == 0)
        def _():
            back_ref[from_sources, rest, :] = packed

        @pl.when(step > 0)
        def _():
            back_ref[from_sources, rest, :] += packed

    for at in range(2):
        sums = jnp.concatenate(
            [sums_ref[at * owned + slot : at * owned + slot + 1, :] for slot in range(owned)],
            axis=1,
        )
        high = sums.astype(BF16).astype(F32)
        low = sums - high
        turned_by = TURN_BY * (first_head + step * 2 + at)
        home = lax.rem(me_ref[0] + sources * TURN_BY - turned_by, sources)
        row = iota((PACKED, width), 0)
        tile = back_ref[home, rest, :].astype(F32)
        tile = jnp.where(row == PACKED - 2, high, jnp.where(row == PACKED - 1, low, tile))
        back_ref[home, rest, :] = tile.astype(BF16)


def unpack_rows_kernel(
    first_head, me_ref, base_ref, over_ref, cent_ref, shared_ref, packed_ref, *refs
):
    new_ref = refs[-1]
    out_refs = refs[-5:-1]
    owners, _, width = shared_ref.shape
    head_size = width // 4
    owned = cent_ref.shape[1]
    tok_rows, heads = base_ref.shape
    step = pl.program_id(0)
    packed = packed_ref[...].reshape(owners * PACKED, width)
    arrived = shared_ref[...].astype(F32)
    for at in range(2):
        here = iota((tok_rows, heads), 1) == step * 2 + at
        base = jnp.sum(jnp.where(here, base_ref[...], 0), axis=1, keepdims=True)
        over = jnp.sum(jnp.where(here, over_ref[...], 0), axis=1, keepdims=True)
        take = iota((tok_rows, owners * SHARED), 1) == base
        take_over = iota((tok_rows, owners * PACKED), 1) == over
        mine = arrived[:, at * SHARED : (at + 1) * SHARED, :].reshape(owners * SHARED, width)
        rows = dot(jnp.where(take, 1.0, 0.0).astype(BF16), mine.astype(BF16))
        rows = rows + dot(jnp.where(take_over, 1.0, 0.0).astype(BF16), packed)
        rows = rows.astype(BF16)
        for which, out_ref in enumerate(out_refs):
            out_ref[:, at * head_size : (at + 1) * head_size] = rows[
                :, which * head_size : (which + 1) * head_size
            ]
        turned_by = TURN_BY * (first_head + step * 2 + at)
        tile = packed_ref[lax.rem(me_ref[0] + turned_by, owners)].astype(F32)
        spare = iota((PACKED, width), 0) >= PACKED - 2
        key_sums = jnp.sum(jnp.where(spare, tile, 0.0), axis=0, keepdims=True)
        for slot in range(owned):
            blend = DECAY_RATE * cent_ref[at, slot : slot + 1, :]
            blend += (1.0 - DECAY_RATE) * key_sums[:, slot * head_size : (slot + 1) * head_size]
            new_ref[at, slot : slot + 1, :] = blend / jnp.sqrt(
                jnp.mean(blend * blend, axis=-1, keepdims=True) + 1e-06
            )


def params(limit=VMEM_BYTES):
    return pltpu.CompilerParams(vmem_limit_bytes=limit)


def dense(queries, keys, values, out_grad, cluster_ids, cluster_slot, centroids):
    seq_count = lax.axis_size("seq")
    local_heads, tok_rows = cluster_ids.shape[:2]
    cluster_count = cluster_slot.shape[0]
    owned = cluster_count // seq_count
    head_size = centroids.shape[2]
    heads = local_heads
    block_rows = owned * CAP
    width = 4 * head_size
    slot_count = seq_count * CAP
    sent = jax.ShapeDtypeStruct((seq_count, heads * block_rows, width), BF16)
    sent_bytes = seq_count * heads * block_rows * width * 2
    ids_rows = cluster_ids.reshape(local_heads, 1, tok_rows)
    slot_row = cluster_slot.reshape(1, cluster_count)
    block = pl.BlockSpec((seq_count, block_rows, width), lambda h: (0, h, 0))

    def exchange(rows):
        return lax.all_to_all(rows, "seq", split_axis=0, concat_axis=0, tiled=True)

    def pack(chunk):
        column = pl.BlockSpec((tok_rows, head_size), lambda h: (0, chunk * heads + h))
        return pl.pallas_call(
            pack_kernel,
            grid=(heads,),
            in_specs=[
                pl.BlockSpec((1, 1, tok_rows), lambda h: (chunk * heads + h, 0, 0)),
                pl.BlockSpec((1, cluster_count), lambda h: (0, 0)),
                column,
                column,
                column,
                column,
            ],
            out_specs=[block, pl.BlockSpec((1, 1, tok_rows), lambda h: (h, 0, 0))],
            out_shape=[sent, jax.ShapeDtypeStruct((heads, 1, tok_rows), jnp.int32)],
            scratch_shapes=[pltpu.VMEM((tok_rows, tok_rows), BF16)],
            compiler_params=params(),
            cost_estimate=pl.CostEstimate(
                flops=heads * 2 * 1024 * 512 * 640, bytes_accessed=2 * sent_bytes, transcendentals=0
            ),
            name="pack",
        )(ids_rows, slot_row, queries, keys, values, out_grad)

    def own(chunk, received):
        return pl.pallas_call(
            owner_kernel,
            grid=(heads,),
            in_specs=[
                block,
                pl.BlockSpec((1, owned, head_size), lambda h: (chunk * heads + h, 0, 0)),
            ],
            out_specs=[block, pl.BlockSpec((1, owned, head_size), lambda h: (h, 0, 0))],
            out_shape=[sent, jax.ShapeDtypeStruct((heads, owned, head_size), F32)],
            scratch_shapes=[
                pltpu.VMEM((16 * block_rows, 16 * block_rows), BF16),
                pltpu.VMEM((slot_count, slot_count), F32),
                pltpu.VMEM((owned, slot_count, width), BF16),
                pltpu.VMEM((owned, slot_count, width), BF16),
            ],
            compiler_params=params(),
            cost_estimate=pl.CostEstimate(
                flops=heads * owned * 7 * 2 * slot_count * slot_count * head_size,
                bytes_accessed=2 * sent_bytes,
                transcendentals=heads * owned * slot_count * slot_count,
            ),
            name="own",
        )(received, centroids)

    def unpack(chunk, flat_cols, returned, previous):
        column = pl.BlockSpec((tok_rows, head_size), lambda h: (0, chunk * heads + h))
        whole = jax.ShapeDtypeStruct((tok_rows, local_heads * head_size), BF16)

        def kernel(*refs):
            unpack_kernel(chunk, *refs)

        return pl.pallas_call(
            kernel,
            grid=(heads,),
            in_specs=[pl.BlockSpec((tok_rows, heads), lambda h: (0, 0)), block]
            + [pl.BlockSpec(memory_space=pl.ANY)] * len(previous),
            out_specs=[column] * 4,
            out_shape=[whole] * 4,
            input_output_aliases={2 + i: i for i in range(len(previous))},
            compiler_params=params(),
            cost_estimate=pl.CostEstimate(
                flops=heads * 2 * 1024 * 512 * 512, bytes_accessed=2 * sent_bytes, transcendentals=0
            ),
            name="unpack",
        )(flat_cols, returned, *previous)

    packed = [pack(chunk) for chunk in range(1)]
    received = [exchange(rows) for rows, _ in packed]
    owned_now = [own(chunk, rows) for chunk, rows in enumerate(received)]
    returned = [exchange(rows) for rows, _ in owned_now]
    outs = ()
    for chunk in range(1):
        flat_cols = packed[chunk][1].reshape(heads, tok_rows).T
        outs = unpack(chunk, flat_cols, returned[chunk], tuple(outs))
    new_centroids = jnp.concatenate([new for _, new in owned_now], axis=0)
    return (*outs, new_centroids)


def body(queries, keys, values, out_grad, cluster_ids, cluster_slot, centroids):
    seq_count = lax.axis_size("seq")
    local_heads, tok_rows = cluster_ids.shape[:2]
    cluster_count = cluster_slot.shape[0]
    owned, head_size = centroids.shape[1:]
    heads = local_heads // CHUNKS
    width = 4 * head_size
    pair_rows = 2 * SHARED
    steps = heads // 2
    send_rows = steps * pair_rows + PACKED
    slot_count = seq_count * CAP
    problems = 2 * owned
    block_bytes = seq_count * pair_rows * width * 2
    sent_shape = jax.ShapeDtypeStruct((seq_count, send_rows, width), BF16)
    ids_rows = cluster_ids.reshape(local_heads, 1, tok_rows)
    slot_row = cluster_slot.reshape(1, cluster_count)
    me = lax.axis_index("seq").reshape(1)

    def cost(flops, exps=0):
        return pl.CostEstimate(
            flops=flops, bytes_accessed=2 * (steps + 1) * block_bytes, transcendentals=exps
        )

    shared_block = pl.BlockSpec((seq_count, pair_rows, width), lambda s: (0, s, 0))
    packed_block = pl.BlockSpec((seq_count, PACKED, width), lambda s: (0, steps, 0))
    whole_block = pl.BlockSpec((seq_count, send_rows, width), lambda s: (0, 0, 0))
    me_spec = pl.BlockSpec(memory_space=pltpu.SMEM)

    def pack(chunk):
        row_shape = jax.ShapeDtypeStruct((heads, 1, tok_rows), jnp.int32)
        rows_block = pl.BlockSpec((heads, 1, tok_rows), lambda s: (0, 0, 0))
        return pl.pallas_call(
            functools.partial(pack_rows_kernel, chunk * heads),
            grid=(steps,),
            in_specs=[
                pl.BlockSpec((heads, 1, tok_rows), lambda s: (chunk, 0, 0)),
                pl.BlockSpec((1, cluster_count), lambda s: (0, 0)),
            ]
            + [pl.BlockSpec(memory_space=pl.ANY)] * 4,
            out_specs=[whole_block, rows_block, rows_block],
            out_shape=[sent_shape, row_shape, row_shape],
            scratch_shapes=[
                pltpu.VMEM((seq_count, head_size), BF16),
                pltpu.VMEM((seq_count * PACKED, width), F32),
                pltpu.VMEM((steps, 4, tok_rows, 2 * head_size), BF16),
                pltpu.SemaphoreType.DMA((steps, 4)),
            ],
            compiler_params=params(),
            cost_estimate=cost(2 * heads * 1536 * tok_rows * width),
            name="pack_rows",
        )(ids_rows, slot_row, queries, keys, values, out_grad)

    def own(chunk, received):
        return pl.pallas_call(
            functools.partial(own_rows_kernel, chunk * heads),
            grid=(steps,),
            in_specs=[me_spec, shared_block, packed_block],
            out_specs=[whole_block, pl.BlockSpec((8, head_size), lambda s: (0, 0))],
            out_shape=[sent_shape, jax.ShapeDtypeStruct((8, head_size), F32)],
            scratch_shapes=[
                pltpu.VMEM(
                    (seq_count // 16, problems * 16 * CAP, 16 * (pair_rows + PACKED)), BF16
                ),
                pltpu.VMEM((slot_count, slot_count), F32),
                pltpu.VMEM((problems, slot_count, width), BF16),
                pltpu.VMEM((problems, slot_count, width), BF16),
                pltpu.VMEM((problems, head_size), F32),
            ],
            compiler_params=params(),
            cost_estimate=cost(
                steps * problems * 16 * 2 * slot_count * slot_count * head_size,
                steps * problems * slot_count * slot_count,
            ),
            name="own_rows",
        )(me, received, received)

    def unpack(chunk, base_rows, over_rows, returned, previous):
        column = pl.BlockSpec((tok_rows, 2 * head_size), lambda s: (0, chunk * steps + s))
        routes_block = pl.BlockSpec((tok_rows, heads), lambda s: (0, 0))
        centroid_block = pl.BlockSpec(
            (2, owned, head_size), lambda s: (chunk * steps + s, 0, 0)
        )
        return pl.pallas_call(
            functools.partial(unpack_rows_kernel, chunk * heads),
            grid=(steps,),
            in_specs=[
                me_spec,
                routes_block,
                routes_block,
                centroid_block,
                shared_block,
                packed_block,
            ]
            + [pl.BlockSpec(memory_space=pl.ANY)] * len(previous),
            out_specs=[column] * 4 + [centroid_block],
            out_shape=[pltpu.HBM((tok_rows, local_heads * head_size), BF16)] * 4
            + [pltpu.HBM(centroids.shape, F32)],
            input_output_aliases={6 + at: at for at in range(len(previous))},
            compiler_params=params(LESS_VMEM_BYTES),
            cost_estimate=cost(2 * heads * 1536 * tok_rows * width),
            name="unpack_rows",
        )(
            me,
            pltpu.with_memory_space_constraint(base_rows.reshape(heads, tok_rows).T, pltpu.HBM),
            pltpu.with_memory_space_constraint(over_rows.reshape(heads, tok_rows).T, pltpu.HBM),
            centroids,
            returned,
            returned,
            *previous,
        )

    def exchange(rows):
        return lax.all_to_all(rows, "seq", split_axis=0, concat_axis=0, tiled=True)

    packed = [pack(chunk) for chunk in range(CHUNKS)]
    received = [exchange(rows) for rows, _, _ in packed]
    owned_now = [own(chunk, received[chunk]) for chunk in range(CHUNKS)]
    returned = [exchange(back) for back, _ in owned_now]
    outs = ()
    for chunk in range(CHUNKS):
        outs = unpack(chunk, *packed[chunk][1:], returned[chunk], tuple(outs))

    peak = functools.reduce(jnp.maximum, [seen[0:1] for _, seen in owned_now])
    swap = [(at, 1 - at) for at in range(2)]
    peak = jnp.maximum(peak, lax.ppermute(peak, "head", swap))[0, PEAK_LANE]

    def lacking(state):
        return state[0]

    def again(state):
        full = dense(queries, keys, values, out_grad, cluster_ids, cluster_slot, centroids)
        return (jnp.zeros((), jnp.bool_), *full)

    state = lax.while_loop(lacking, again, (peak > PACKED - SPARE, *outs))
    return state[1:]


def solution(mesh):
    return jax.shard_map(
        body,
        mesh=mesh,
        in_specs=(
            P("seq", "head"),
            P("seq", "head"),
            P("seq", "head"),
            P("seq", "head"),
            P("head", "seq", None),
            P(),
            P("head", "seq", None),
        ),
        out_specs=(
            P("seq", "head"),
            P("seq", "head"),
            P("seq", "head"),
            P("seq", "head"),
            P("head", "seq", None),
        ),
        check_vma=False,
    )
```

```python
import functools
import math

import jax
import jax.numpy as jnp
from jax import lax
from jax.experimental import pallas as pl
from jax.experimental.pallas import tpu as pltpu
from jax.sharding import PartitionSpec as P

CAP = 4
DECAY_RATE = 0.9
MASKED = -1e30
ABSENT = 64.0
CHUNKS = 2
SHARED = 8
PACKED = 16
SPARE = 2
PEAK_LANE = 127
TURN_BY = 8
VMEM_BYTES = 63 * 1024 * 1024
LESS_VMEM_BYTES = 40 * 1024 * 1024

F32 = jnp.float32
BF16 = jnp.bfloat16
CONTRACT_LAST = (((1,), (1,)), ((), ()))
CONTRACT_FIRST = (((0,), (0,)), ((), ()))


def iota(shape, dim):
    return lax.broadcasted_iota(jnp.int32, shape, dim)


def dot(left, right):
    return jnp.dot(left, right, preferred_element_type=F32)


def pack_kernel(ids_ref, slot_ref, q_ref, k_ref, v_ref, g_ref, send_ref, flat_ref, earlier_ref):
    tok_rows = ids_ref.shape[2]
    cluster_count = slot_ref.shape[1]
    slot_rows = cluster_count * CAP

    @pl.when(pl.program_id(0) == 0)
    def _():
        earlier_ref[...] = (iota((tok_rows, tok_rows), 0) < iota((tok_rows, tok_rows), 1)).astype(
            F32
        ).astype(BF16)

    ids_row = ids_ref[0]
    member = iota((cluster_count, tok_rows), 0) == ids_row
    member_f = jnp.where(member, 1.0, 0.0)
    member_low = member_f.astype(BF16)
    slots_low = jnp.broadcast_to(slot_ref[...].astype(F32), (8, cluster_count)).astype(BF16)
    slot_row = dot(slots_low, member_low)[0:1]
    rank_row = jnp.sum(dot(member_low, earlier_ref[...]) * member_f, axis=0, keepdims=True)
    flat_row = (slot_row * CAP + rank_row).astype(jnp.int32)
    flat_ref[0] = flat_row
    place = jnp.where(iota((slot_rows, tok_rows), 0) == flat_row, 1.0, 0.0).astype(BF16)
    ones = jnp.ones((tok_rows, 128), BF16)
    head_size = q_ref.shape[1]
    taken = dot(place, ones)
    out_shape = send_ref.shape[:2] + (head_size,)

    def put(at, rows):
        send_ref[:, :, at * head_size : (at + 1) * head_size] = rows.astype(BF16).reshape(out_shape)

    put(0, dot(place, q_ref[...]))
    put(1, dot(place, k_ref[...]) + (1.0 - taken) * ABSENT)
    put(2, dot(place, v_ref[...]))
    put(3, dot(place, g_ref[...]))


def owner_kernel(recv_ref, cent_ref, back_ref, new_ref, turn_ref, causal_ref, rows_ref, grads_ref):
    source_count, block_rows, width = recv_ref.shape
    head_size = width // 4
    owned = block_rows // CAP
    slot_count = source_count * CAP
    group_rows = 16 * block_rows
    groups = source_count // 16
    part = 16 * CAP
    score_scale = 1.0 / math.sqrt(head_size)

    @pl.when(pl.program_id(0) == 0)
    def _():
        row_at = iota((group_rows, group_rows), 0)
        col_at = iota((group_rows, group_rows), 1)
        cluster_of = row_at // part
        source_of = (row_at % part) // CAP
        from_row = source_of * block_rows + cluster_of * CAP + row_at % CAP
        turn_ref[...] = jnp.where(from_row == col_at, 1.0, 0.0).astype(BF16)
        causal_ref[...] = jnp.where(
            iota((slot_count, slot_count), 1) <= iota((slot_count, slot_count), 0), 0.0, MASKED
        )

    turn = turn_ref[...]
    @pl.loop(0, groups)
    def _(group):
        arrived = recv_ref[pl.ds(group * 16, 16)].reshape(group_rows, width)
        turned = dot(turn, arrived).astype(BF16)
        at_row = pl.multiple_of(group * part, part)
        rows_ref[:, pl.ds(at_row, part), :] = turned.reshape(owned, part, width)

    first_lane = jnp.where(iota((8, head_size), 1) == 0, 1.0, 0.0).astype(BF16)
    @pl.loop(0, owned)
    def _(cluster):
        q = rows_ref[cluster, :, 0:head_size]
        k = rows_ref[cluster, :, head_size : 2 * head_size]
        v = rows_ref[cluster, :, 2 * head_size : 3 * head_size]
        g = rows_ref[cluster, :, 3 * head_size : 4 * head_size]
        marks = lax.dot_general(first_lane, k, CONTRACT_LAST, preferred_element_type=F32)
        present = marks < ABSENT / 2
        bias = jnp.where(present, 0.0, MASKED)[0:1]
        scores = lax.dot_general(q, k, CONTRACT_LAST, preferred_element_type=F32) * score_scale
        scores = scores + (causal_ref[...] + bias)
        weights = jnp.exp(scores - jnp.max(scores, axis=-1, keepdims=True))
        probs = weights / jnp.sum(weights, axis=-1, keepdims=True)
        probs_low = probs.astype(BF16)
        out = dot(probs_low, v).astype(BF16)
        grad_prob = lax.dot_general(g, v, CONTRACT_LAST, preferred_element_type=F32)
        delta = jnp.sum(g.astype(F32) * out.astype(F32), axis=-1, keepdims=True)
        grad_score = (probs * (grad_prob - delta) * score_scale).astype(BF16)
        grad_q = dot(grad_score, k)
        grad_k = lax.dot_general(grad_score, q, CONTRACT_FIRST, preferred_element_type=F32)
        grad_v = lax.dot_general(probs_low, g, CONTRACT_FIRST, preferred_element_type=F32)
        grads_ref[cluster, :, 0:head_size] = out
        grads_ref[cluster, :, head_size : 2 * head_size] = grad_q.astype(BF16)
        grads_ref[cluster, :, 2 * head_size : 3 * head_size] = grad_k.astype(BF16)
        grads_ref[cluster, :, 3 * head_size : 4 * head_size] = grad_v.astype(BF16)
        key_sums = dot(jnp.where(present, 1.0, 0.0).astype(BF16), k)[0:1]
        blend = DECAY_RATE * cent_ref[0, pl.ds(cluster, 1), :] + (1.0 - DECAY_RATE) * key_sums
        new_ref[0, pl.ds(cluster, 1), :] = blend / jnp.sqrt(
            jnp.mean(blend * blend, axis=-1, keepdims=True) + 1e-06
        )

    @pl.loop(0, groups)
    def _(group):
        at_row = pl.multiple_of(group * part, part)
        leaving = grads_ref[:, pl.ds(at_row, part), :].reshape(group_rows, width)
        turned = lax.dot_general(turn, leaving, CONTRACT_FIRST, preferred_element_type=F32)
        back_ref[pl.ds(group * 16, 16)] = turned.astype(BF16).reshape(16, block_rows, width)


def unpack_kernel(chunk, flat_ref, ret_ref, *refs):
    out_refs = refs[-4:]
    sources, block_rows, width = ret_ref.shape
    head_size = width // 4
    tok_rows, heads = flat_ref.shape
    slot_rows = sources * block_rows
    here = iota((tok_rows, heads), 1) == pl.program_id(0)
    flat_col = jnp.sum(jnp.where(here, flat_ref[...], 0), axis=1, keepdims=True)
    take = jnp.where(iota((tok_rows, slot_rows), 1) == flat_col, 1.0, 0.0).astype(BF16)
    rows = dot(take, ret_ref[...].reshape(slot_rows, width)).astype(BF16)
    for at, out_ref in enumerate(out_refs):
        out_ref[...] = rows[:, at * head_size : (at + 1) * head_size]


def find_rows(first_head, ids_ref, slot_ref, base_ref, over_ref, header_ref):
    heads, _, tok_rows = ids_ref.shape
    cluster_count = slot_ref.shape[1]
    owners, lanes = header_ref.shape
    earlier = jnp.where(
        iota((tok_rows, tok_rows), 0) < iota((tok_rows, tok_rows), 1), 1.0, 0.0
    ).astype(BF16)
    slots_low = jnp.broadcast_to(slot_ref[...].astype(F32), (8, cluster_count)).astype(BF16)
    members = [
        jnp.where(iota((cluster_count, tok_rows), 0) == ids_ref[head], 1.0, 0.0)
        for head in range(heads)
    ]
    member_low = jnp.concatenate(members, axis=0).astype(BF16)
    earlier_members = dot(member_low, earlier)
    owner_of, tag_of, here_of = [], [], []
    for head in range(heads):
        own = slice(head * cluster_count, (head + 1) * cluster_count)
        slot = dot(slots_low, member_low[own])[0:1].astype(jnp.int32)
        rank = jnp.sum(earlier_members[own] * members[head], axis=0, keepdims=True)
        owner = (slot // CAP + TURN_BY * (first_head + head)) % owners
        owner_of.append(owner)
        tag_of.append((head * CAP + slot % CAP) * CAP + rank.astype(jnp.int32))
        here_of.append(jnp.where(iota((owners, tok_rows), 0) == owner, 1.0, 0.0))
    before_all = dot(jnp.concatenate(here_of, axis=0).astype(BF16), earlier)
    filled = jnp.zeros((owners, 1), F32)
    header = jnp.zeros((owners, lanes), F32)
    for head in range(heads):
        here_f = here_of[head]
        before = before_all[head * owners : (head + 1) * owners]
        place = jnp.sum(before * here_f, axis=0, keepdims=True).astype(jnp.int32)
        late = jnp.sum((before + filled) * here_f, axis=0, keepdims=True)
        late = late.astype(jnp.int32) - SHARED
        filled = filled + jnp.maximum(jnp.sum(here_f, axis=1, keepdims=True) - SHARED, 0.0)
        fits = place < SHARED
        packs = (late < PACKED - SPARE) & (place >= SHARED)
        base_ref[head] = jnp.where(fits, owner_of[head] * SHARED + place, -1)
        over_ref[head] = jnp.where(packs, owner_of[head] * PACKED + late, -1)
        lane = jnp.where(fits, head * SHARED + place, jnp.where(packs, heads * SHARED + late, -1))
        named = (here_f * (tag_of[head] + 1).astype(F32)).astype(BF16)
        lane_at = jnp.where(iota((lanes, tok_rows), 0) == lane, 1.0, 0.0).astype(BF16)
        header = header + lax.dot_general(
            named, lane_at, CONTRACT_LAST, preferred_element_type=F32
        )
    peak = jnp.max(filled, axis=0, keepdims=True)
    header_ref[...] = jnp.where(iota((owners, lanes), 1) == PEAK_LANE, peak, header).astype(BF16)


def token_rows(columns_ref, step, at, head_size):
    lanes = slice(at * head_size, (at + 1) * head_size)
    parts = [columns_ref[step, which, :, lanes] for which in range(columns_ref.shape[1])]
    return jnp.concatenate(parts, axis=1)


def pack_rows_kernel(
    first_head,
    ids_ref,
    slot_ref,
    q_ref,
    k_ref,
    v_ref,
    g_ref,
    send_ref,
    places_ref,
    header_ref,
    total_ref,
    columns_ref,
    arrived_ref,
):
    owners, send_rows, width = send_ref.shape
    tok_rows = q_ref.shape[0]
    head_size = width // 4
    step = pl.program_id(0)

    steps = columns_ref.shape[0]
    heads = places_ref.shape[0] // 2
    base_ref = places_ref.at[pl.ds(0, heads)]
    over_ref = places_ref.at[pl.ds(heads, heads)]

    def column_copy(at_step, which):
        lanes = pl.ds((first_head + 2 * at_step) * head_size, 2 * head_size)
        return pltpu.make_async_copy(
            (q_ref, k_ref, v_ref, g_ref)[which].at[:, lanes],
            columns_ref.at[at_step, which],
            arrived_ref.at[at_step, which],
        )

    @pl.when(step == 0)
    def _():
        for at_step in range(steps):
            for which in range(4):
                column_copy(at_step, which).start()
        find_rows(first_head, ids_ref, slot_ref, base_ref, over_ref, header_ref)

    for at_step in range(steps):

        @pl.when(step == at_step)
        def _():
            for which in range(4):
                column_copy(at_step, which).wait()

    rows = [token_rows(columns_ref, step, at, head_size) for at in range(2)]
    halves = []
    for at in range(2):
        place = iota((owners * SHARED, tok_rows), 0) == base_ref[step * 2 + at]
        placed = dot(jnp.where(place, 1.0, 0.0).astype(BF16), rows[at])
        halves.append(placed.reshape(owners, SHARED, width))
    at_row = pl.multiple_of(step * 2 * SHARED, 2 * SHARED)
    shared = jnp.concatenate(halves, axis=1).astype(BF16)
    send_ref[:, pl.ds(at_row, 2 * SHARED), :] = shared

    places = [
        jnp.where(iota((owners * PACKED, tok_rows), 0) == over_ref[step * 2 + at], 1.0, 0.0).astype(BF16)
        for at in range(2)
    ]
    added = dot(jnp.concatenate(places, axis=1), jnp.concatenate(rows, axis=0))

    @pl.when(step == 0)
    def _():
        total_ref[...] = added

    @pl.when(step == pl.num_programs(0) - 1)
    def _():
        total = total_ref[...] + added
        last_row = iota((owners * PACKED, owners), 1) * PACKED + PACKED - 1
        to_last = jnp.where(iota((owners * PACKED, owners), 0) == last_row, 1.0, 0.0)
        tags = dot(to_last.astype(BF16), header_ref[...])
        total = jnp.concatenate([total[:, :head_size] + tags, total[:, head_size:]], axis=1)
        packed = total.astype(BF16).reshape(owners, PACKED, width)
        send_ref[:, send_rows - PACKED :, :] = packed


def own_rows_kernel(
    first_head,
    me_ref,
    shared_ref,
    over_ref,
    back_ref,
    peak_ref,
    turn_ref,
    causal_ref,
    rows_ref,
    grads_ref,
    sums_ref,
):
    sources, pair_rows, width = shared_ref.shape
    head_size = width // 4
    problems = rows_ref.shape[0]
    owned = problems // 2
    slot_count = sources * CAP
    bunch = 16
    groups = sources // bunch
    part = bunch * CAP
    shared_count = bunch * pair_rows
    packed_count = bunch * PACKED
    score_scale = 1.0 / math.sqrt(head_size)
    step = pl.program_id(0)
    steps = pl.num_programs(0)

    @pl.when(step == 0)
    def _():
        at = iota((slot_count, slot_count), 0)
        causal_ref[...] = jnp.where(iota((slot_count, slot_count), 1) <= at, 0.0, MASKED)

    header_of = jnp.where(
        iota((bunch, packed_count), 1) == iota((bunch, packed_count), 0) * PACKED + PACKED - 1,
        1.0,
        0.0,
    ).astype(BF16)

    def turns(header, first_lane, rows_each, used):
        count = bunch * rows_each
        lane = iota((head_size, count), 1) % rows_each
        match = (iota((head_size, count), 0) == lane + first_lane) & (lane < used)
        tags = dot(header, jnp.where(match, 1.0, 0.0).astype(BF16))
        source = iota((1, count), 1) // rows_each
        own = iota((bunch, count), 0) == source
        tag = jnp.sum(jnp.where(own, tags, 0.0), axis=0, keepdims=True).astype(jnp.int32) - 1
        mine = (tag >= 0) & (tag // (problems * CAP) == step)
        problem = (tag // CAP) % problems
        slot = jnp.where(mine, problem * part + source * CAP + tag % CAP, -1)
        hit = iota((problems * part, count), 0) == slot
        return jnp.where(hit, 1.0, 0.0).astype(BF16)

    ones = jnp.ones((shared_count + packed_count, head_size), BF16)
    peak_ref[...] = jnp.zeros(peak_ref.shape, F32)

    @pl.loop(0, groups)
    def _(group):
        from_sources = pl.ds(group * bunch, bunch)
        at_row = pl.multiple_of(group * part, part)
        packed = over_ref[from_sources].reshape(packed_count, width)
        shared = shared_ref[from_sources].reshape(shared_count, width)
        header = dot(header_of, packed[:, :head_size])
        peak_ref[...] = jnp.maximum(peak_ref[...], jnp.max(header, axis=0, keepdims=True))
        header = header.astype(BF16)
        turn = jnp.concatenate(
            [
                turns(header, step * pair_rows, pair_rows, pair_rows),
                turns(header, steps * pair_rows, PACKED, PACKED - SPARE),
            ],
            axis=1,
        )
        turn_ref[group] = turn
        turned = dot(turn, jnp.concatenate([shared, packed], axis=0))
        marked = turned[:, head_size : 2 * head_size] + (1.0 - dot(turn, ones)) * ABSENT
        turned = jnp.concatenate(
            [turned[:, :head_size], marked, turned[:, 2 * head_size :]], axis=1
        )
        rows_ref[:, pl.ds(at_row, part), :] = turned.astype(BF16).reshape(problems, part, width)

    first_lane = jnp.where(iota((8, head_size), 1) == 0, 1.0, 0.0).astype(BF16)

    def attend(problem):
        q = rows_ref[problem, :, 0:head_size]
        k = rows_ref[problem, :, head_size : 2 * head_size]
        v = rows_ref[problem, :, 2 * head_size : 3 * head_size]
        g = rows_ref[problem, :, 3 * head_size : 4 * head_size]
        marks = lax.dot_general(first_lane, k, CONTRACT_LAST, preferred_element_type=F32)
        present = marks < ABSENT / 2
        bias = jnp.where(present, 0.0, MASKED)[0:1]
        scores = lax.dot_general(q, k, CONTRACT_LAST, preferred_element_type=F32) * score_scale
        scores = scores + (causal_ref[...] + bias)
        weights = jnp.exp(scores - jnp.max(scores, axis=-1, keepdims=True))
        probs = weights / jnp.sum(weights, axis=-1, keepdims=True)
        probs_low = probs.astype(BF16)
        out = dot(probs_low, v).astype(BF16)
        grad_prob = lax.dot_general(g, v, CONTRACT_LAST, preferred_element_type=F32)
        delta = jnp.sum(g.astype(F32) * out.astype(F32), axis=-1, keepdims=True)
        grad_score = (probs * (grad_prob - delta) * score_scale).astype(BF16)
        grad_q = dot(grad_score, k)
        grad_k = lax.dot_general(grad_score, q, CONTRACT_FIRST, preferred_element_type=F32)
        grad_v = lax.dot_general(probs_low, g, CONTRACT_FIRST, preferred_element_type=F32)
        grads_ref[problem, :, 0:head_size] = out
        grads_ref[problem, :, head_size : 2 * head_size] = grad_q.astype(BF16)
        grads_ref[problem, :, 2 * head_size : 3 * head_size] = grad_k.astype(BF16)
        grads_ref[problem, :, 3 * head_size : 4 * head_size] = grad_v.astype(BF16)
        sums = dot(jnp.where(present, 1.0, 0.0).astype(BF16), k)[0:1]
        sums_ref[pl.ds(problem, 1), :] = sums

    @pl.loop(0, problems // 2)
    def _(pair):
        attend(pair * 2)
        attend(pair * 2 + 1)

    rest = slice(back_ref.shape[1] - PACKED, back_ref.shape[1])
    at_pair = pl.multiple_of(step * pair_rows, pair_rows)

    @pl.loop(0, groups)
    def _(group):
        from_sources = pl.ds(group * bunch, bunch)
        at_row = pl.multiple_of(group * part, part)
        leaving = grads_ref[:, pl.ds(at_row, part), :].reshape(problems * part, width)
        sent = lax.dot_general(
            turn_ref[group], leaving, CONTRACT_FIRST, preferred_element_type=F32
        ).astype(BF16)
        back_ref[from_sources, pl.ds(at_pair, pair_rows), :] = sent[:shared_count].reshape(
            bunch, pair_rows, width
        )
        packed = sent[shared_count:].reshape(bunch, PACKED, width)

        @pl.when(step == 0)
        def _():
            back_ref[from_sources, rest, :] = packed

        @pl.when(step > 0)
        def _():
            back_ref[from_sources, rest, :] += packed

    for at in range(2):
        sums = jnp.concatenate(
            [sums_ref[at * owned + slot : at * owned + slot + 1, :] for slot in range(owned)],
            axis=1,
        )
        high = sums.astype(BF16).astype(F32)
        low = sums - high
        turned_by = TURN_BY * (first_head + step * 2 + at)
        home = lax.rem(me_ref[0] + sources * TURN_BY - turned_by, sources)
        row = iota((PACKED, width), 0)
        tile = back_ref[home, rest, :].astype(F32)
        tile = jnp.where(row == PACKED - 2, high, jnp.where(row == PACKED - 1, low, tile))
        back_ref[home, rest, :] = tile.astype(BF16)


def unpack_rows_kernel(
    first_head, me_ref, places_ref, cent_ref, shared_ref, packed_ref, *refs
):
    new_ref = refs[-1]
    out_refs = refs[-5:-1]
    owners, _, width = shared_ref.shape
    head_size = width // 4
    owned = cent_ref.shape[1]
    tok_rows, both = places_ref.shape
    heads = both // 2
    step = pl.program_id(0)
    packed = packed_ref[...].reshape(owners * PACKED, width)
    arrived = shared_ref[...].astype(F32)
    for at in range(2):
        lane = iota((tok_rows, both), 1) - step * 2 - at
        base = jnp.sum(jnp.where(lane == 0, places_ref[...], 0), axis=1, keepdims=True)
        over = jnp.sum(jnp.where(lane == heads, places_ref[...], 0), axis=1, keepdims=True)
        take = iota((tok_rows, owners * SHARED), 1) == base
        take_over = iota((tok_rows, owners * PACKED), 1) == over
        mine = arrived[:, at * SHARED : (at + 1) * SHARED, :].reshape(owners * SHARED, width)
        rows = dot(jnp.where(take, 1.0, 0.0).astype(BF16), mine.astype(BF16))
        rows = rows + dot(jnp.where(take_over, 1.0, 0.0).astype(BF16), packed)
        rows = rows.astype(BF16)
        for which, out_ref in enumerate(out_refs):
            out_ref[:, at * head_size : (at + 1) * head_size] = rows[
                :, which * head_size : (which + 1) * head_size
            ]
        turned_by = TURN_BY * (first_head + step * 2 + at)
        tile = packed_ref[lax.rem(me_ref[0] + turned_by, owners)].astype(F32)
        spare = iota((PACKED, width), 0) >= PACKED - 2
        key_sums = jnp.sum(jnp.where(spare, tile, 0.0), axis=0, keepdims=True)
        for slot in range(owned):
            blend = DECAY_RATE * cent_ref[at, slot : slot + 1, :]
            blend += (1.0 - DECAY_RATE) * key_sums[:, slot * head_size : (slot + 1) * head_size]
            new_ref[at, slot : slot + 1, :] = blend / jnp.sqrt(
                jnp.mean(blend * blend, axis=-1, keepdims=True) + 1e-06
            )


def params(limit=VMEM_BYTES):
    return pltpu.CompilerParams(vmem_limit_bytes=limit)


def dense(queries, keys, values, out_grad, cluster_ids, cluster_slot, centroids):
    seq_count = lax.axis_size("seq")
    local_heads, tok_rows = cluster_ids.shape[:2]
    cluster_count = cluster_slot.shape[0]
    owned = cluster_count // seq_count
    head_size = centroids.shape[2]
    heads = local_heads
    block_rows = owned * CAP
    width = 4 * head_size
    slot_count = seq_count * CAP
    sent = jax.ShapeDtypeStruct((seq_count, heads * block_rows, width), BF16)
    sent_bytes = seq_count * heads * block_rows * width * 2
    ids_rows = cluster_ids.reshape(local_heads, 1, tok_rows)
    slot_row = cluster_slot.reshape(1, cluster_count)
    block = pl.BlockSpec((seq_count, block_rows, width), lambda h: (0, h, 0))

    def exchange(rows):
        return lax.all_to_all(rows, "seq", split_axis=0, concat_axis=0, tiled=True)

    def pack(chunk):
        column = pl.BlockSpec((tok_rows, head_size), lambda h: (0, chunk * heads + h))
        return pl.pallas_call(
            pack_kernel,
            grid=(heads,),
            in_specs=[
                pl.BlockSpec((1, 1, tok_rows), lambda h: (chunk * heads + h, 0, 0)),
                pl.BlockSpec((1, cluster_count), lambda h: (0, 0)),
                column,
                column,
                column,
                column,
            ],
            out_specs=[block, pl.BlockSpec((1, 1, tok_rows), lambda h: (h, 0, 0))],
            out_shape=[sent, jax.ShapeDtypeStruct((heads, 1, tok_rows), jnp.int32)],
            scratch_shapes=[pltpu.VMEM((tok_rows, tok_rows), BF16)],
            compiler_params=params(),
            cost_estimate=pl.CostEstimate(
                flops=heads * 2 * 1024 * 512 * 640, bytes_accessed=2 * sent_bytes, transcendentals=0
            ),
            name="pack",
        )(ids_rows, slot_row, queries, keys, values, out_grad)

    def own(chunk, received):
        return pl.pallas_call(
            owner_kernel,
            grid=(heads,),
            in_specs=[
                block,
                pl.BlockSpec((1, owned, head_size), lambda h: (chunk * heads + h, 0, 0)),
            ],
            out_specs=[block, pl.BlockSpec((1, owned, head_size), lambda h: (h, 0, 0))],
            out_shape=[sent, jax.ShapeDtypeStruct((heads, owned, head_size), F32)],
            scratch_shapes=[
                pltpu.VMEM((16 * block_rows, 16 * block_rows), BF16),
                pltpu.VMEM((slot_count, slot_count), F32),
                pltpu.VMEM((owned, slot_count, width), BF16),
                pltpu.VMEM((owned, slot_count, width), BF16),
            ],
            compiler_params=params(),
            cost_estimate=pl.CostEstimate(
                flops=heads * owned * 7 * 2 * slot_count * slot_count * head_size,
                bytes_accessed=2 * sent_bytes,
                transcendentals=heads * owned * slot_count * slot_count,
            ),
            name="own",
        )(received, centroids)

    def unpack(chunk, flat_cols, returned, previous):
        column = pl.BlockSpec((tok_rows, head_size), lambda h: (0, chunk * heads + h))
        whole = jax.ShapeDtypeStruct((tok_rows, local_heads * head_size), BF16)

        def kernel(*refs):
            unpack_kernel(chunk, *refs)

        return pl.pallas_call(
            kernel,
            grid=(heads,),
            in_specs=[pl.BlockSpec((tok_rows, heads), lambda h: (0, 0)), block]
            + [pl.BlockSpec(memory_space=pl.ANY)] * len(previous),
            out_specs=[column] * 4,
            out_shape=[whole] * 4,
            input_output_aliases={2 + i: i for i in range(len(previous))},
            compiler_params=params(),
            cost_estimate=pl.CostEstimate(
                flops=heads * 2 * 1024 * 512 * 512, bytes_accessed=2 * sent_bytes, transcendentals=0
            ),
            name="unpack",
        )(flat_cols, returned, *previous)

    packed = [pack(chunk) for chunk in range(1)]
    received = [exchange(rows) for rows, _ in packed]
    owned_now = [own(chunk, rows) for chunk, rows in enumerate(received)]
    returned = [exchange(rows) for rows, _ in owned_now]
    outs = ()
    for chunk in range(1):
        flat_cols = packed[chunk][1].reshape(heads, tok_rows).T
        outs = unpack(chunk, flat_cols, returned[chunk], tuple(outs))
    new_centroids = jnp.concatenate([new for _, new in owned_now], axis=0)
    return (*outs, new_centroids)


def body(queries, keys, values, out_grad, cluster_ids, cluster_slot, centroids):
    seq_count = lax.axis_size("seq")
    local_heads, tok_rows = cluster_ids.shape[:2]
    cluster_count = cluster_slot.shape[0]
    owned, head_size = centroids.shape[1:]
    heads = local_heads // CHUNKS
    width = 4 * head_size
    pair_rows = 2 * SHARED
    steps = heads // 2
    send_rows = steps * pair_rows + PACKED
    slot_count = seq_count * CAP
    problems = 2 * owned
    block_bytes = seq_count * pair_rows * width * 2
    sent_shape = jax.ShapeDtypeStruct((seq_count, send_rows, width), BF16)
    ids_rows = cluster_ids.reshape(local_heads, 1, tok_rows)
    slot_row = cluster_slot.reshape(1, cluster_count)
    me = lax.axis_index("seq").reshape(1)

    def cost(flops, exps=0):
        return pl.CostEstimate(
            flops=flops, bytes_accessed=2 * (steps + 1) * block_bytes, transcendentals=exps
        )

    shared_block = pl.BlockSpec((seq_count, pair_rows, width), lambda s: (0, s, 0))
    packed_block = pl.BlockSpec((seq_count, PACKED, width), lambda s: (0, steps, 0))
    whole_block = pl.BlockSpec((seq_count, send_rows, width), lambda s: (0, 0, 0))
    me_spec = pl.BlockSpec(memory_space=pltpu.SMEM)

    def pack(chunk):
        places_shape = jax.ShapeDtypeStruct((2 * heads, 1, tok_rows), jnp.int32)
        places_block = pl.BlockSpec((2 * heads, 1, tok_rows), lambda s: (0, 0, 0))
        return pl.pallas_call(
            functools.partial(pack_rows_kernel, chunk * heads),
            grid=(steps,),
            in_specs=[
                pl.BlockSpec((heads, 1, tok_rows), lambda s: (chunk, 0, 0)),
                pl.BlockSpec((1, cluster_count), lambda s: (0, 0)),
            ]
            + [pl.BlockSpec(memory_space=pl.ANY)] * 4,
            out_specs=[whole_block, places_block],
            out_shape=[sent_shape, places_shape],
            scratch_shapes=[
                pltpu.VMEM((seq_count, head_size), BF16),
                pltpu.VMEM((seq_count * PACKED, width), F32),
                pltpu.VMEM((steps, 4, tok_rows, 2 * head_size), BF16),
                pltpu.SemaphoreType.DMA((steps, 4)),
            ],
            compiler_params=params(),
            cost_estimate=cost(2 * heads * 1536 * tok_rows * width),
            name="pack_rows",
        )(ids_rows, slot_row, queries, keys, values, out_grad)

    def own(chunk, received):
        return pl.pallas_call(
            functools.partial(own_rows_kernel, chunk * heads),
            grid=(steps,),
            in_specs=[me_spec, shared_block, packed_block],
            out_specs=[whole_block, pl.BlockSpec((8, head_size), lambda s: (0, 0))],
            out_shape=[sent_shape, jax.ShapeDtypeStruct((8, head_size), F32)],
            scratch_shapes=[
                pltpu.VMEM(
                    (seq_count // 16, problems * 16 * CAP, 16 * (pair_rows + PACKED)), BF16
                ),
                pltpu.VMEM((slot_count, slot_count), F32),
                pltpu.VMEM((problems, slot_count, width), BF16),
                pltpu.VMEM((problems, slot_count, width), BF16),
                pltpu.VMEM((problems, head_size), F32),
            ],
            compiler_params=params(),
            cost_estimate=cost(
                steps * problems * 16 * 2 * slot_count * slot_count * head_size,
                steps * problems * slot_count * slot_count,
            ),
            name="own_rows",
        )(me, received, received)

    def unpack(chunk, places, returned, previous):
        column = pl.BlockSpec((tok_rows, 2 * head_size), lambda s: (0, chunk * steps + s))
        places_block = pl.BlockSpec((tok_rows, 2 * heads), lambda s: (0, 0))
        centroid_block = pl.BlockSpec(
            (2, owned, head_size), lambda s: (chunk * steps + s, 0, 0)
        )
        return pl.pallas_call(
            functools.partial(unpack_rows_kernel, chunk * heads),
            grid=(steps,),
            in_specs=[
                me_spec,
                places_block,
                centroid_block,
                shared_block,
                packed_block,
            ]
            + [pl.BlockSpec(memory_space=pl.ANY)] * len(previous),
            out_specs=[column] * 4 + [centroid_block],
            out_shape=[pltpu.HBM((tok_rows, local_heads * head_size), BF16)] * 4
            + [pltpu.HBM(centroids.shape, F32)],
            input_output_aliases={5 + at: at for at in range(len(previous))},
            compiler_params=params(LESS_VMEM_BYTES),
            cost_estimate=cost(2 * heads * 1536 * tok_rows * width),
            name="unpack_rows",
        )(
            me,
            places.reshape(2 * heads, tok_rows).T,
            centroids,
            returned,
            returned,
            *previous,
        )

    def exchange(rows):
        return lax.all_to_all(rows, "seq", split_axis=0, concat_axis=0, tiled=True)

    packed = [pack(chunk) for chunk in range(CHUNKS)]
    received = [exchange(rows) for rows, _ in packed]
    owned_now = [own(chunk, received[chunk]) for chunk in range(CHUNKS)]
    returned = [exchange(back) for back, _ in owned_now]
    outs = ()
    for chunk in range(CHUNKS):
        outs = unpack(chunk, packed[chunk][1], returned[chunk], tuple(outs))

    peak = functools.reduce(jnp.maximum, [seen[0:1] for _, seen in owned_now])
    swap = [(at, 1 - at) for at in range(2)]
    peak = jnp.maximum(peak, lax.ppermute(peak, "head", swap))[0, PEAK_LANE]

    def lacking(state):
        return state[0]

    def again(state):
        full = dense(queries, keys, values, out_grad, cluster_ids, cluster_slot, centroids)
        return (jnp.zeros((), jnp.bool_), *full)

    state = lax.while_loop(lacking, again, (peak > PACKED - SPARE, *outs))
    return state[1:]


def solution(mesh):
    return jax.shard_map(
        body,
        mesh=mesh,
        in_specs=(
            P("seq", "head"),
            P("seq", "head"),
            P("seq", "head"),
            P("seq", "head"),
            P("head", "seq", None),
            P(),
            P("head", "seq", None),
        ),
        out_specs=(
            P("seq", "head"),
            P("seq", "head"),
            P("seq", "head"),
            P("seq", "head"),
            P("head", "seq", None),
        ),
        check_vma=False,
    )
```

```python
import functools
import math

import jax
import jax.numpy as jnp
from jax import lax
from jax.experimental import pallas as pl
from jax.experimental.pallas import tpu as pltpu
from jax.sharding import PartitionSpec as P

CAP = 4
DECAY_RATE = 0.9
MASKED = -1e30
ABSENT = 64.0
CHUNKS = 2
SHARED = 8
PACKED = 16
SPARE = 2
PEAK_LANE = 127
TURN_BY = 8
VMEM_BYTES = 63 * 1024 * 1024
LESS_VMEM_BYTES = 40 * 1024 * 1024

F32 = jnp.float32
BF16 = jnp.bfloat16
CONTRACT_LAST = (((1,), (1,)), ((), ()))
CONTRACT_FIRST = (((0,), (0,)), ((), ()))


def iota(shape, dim):
    return lax.broadcasted_iota(jnp.int32, shape, dim)


def dot(left, right):
    return jnp.dot(left, right, preferred_element_type=F32)


def pack_kernel(ids_ref, slot_ref, q_ref, k_ref, v_ref, g_ref, send_ref, flat_ref, earlier_ref):
    tok_rows = ids_ref.shape[2]
    cluster_count = slot_ref.shape[1]
    slot_rows = cluster_count * CAP

    @pl.when(pl.program_id(0) == 0)
    def _():
        earlier_ref[...] = (iota((tok_rows, tok_rows), 0) < iota((tok_rows, tok_rows), 1)).astype(
            F32
        ).astype(BF16)

    ids_row = ids_ref[0]
    member = iota((cluster_count, tok_rows), 0) == ids_row
    member_f = jnp.where(member, 1.0, 0.0)
    member_low = member_f.astype(BF16)
    slots_low = jnp.broadcast_to(slot_ref[...].astype(F32), (8, cluster_count)).astype(BF16)
    slot_row = dot(slots_low, member_low)[0:1]
    rank_row = jnp.sum(dot(member_low, earlier_ref[...]) * member_f, axis=0, keepdims=True)
    flat_row = (slot_row * CAP + rank_row).astype(jnp.int32)
    flat_ref[0] = flat_row
    place = jnp.where(iota((slot_rows, tok_rows), 0) == flat_row, 1.0, 0.0).astype(BF16)
    ones = jnp.ones((tok_rows, 128), BF16)
    head_size = q_ref.shape[1]
    taken = dot(place, ones)
    out_shape = send_ref.shape[:2] + (head_size,)

    def put(at, rows):
        send_ref[:, :, at * head_size : (at + 1) * head_size] = rows.astype(BF16).reshape(out_shape)

    put(0, dot(place, q_ref[...]))
    put(1, dot(place, k_ref[...]) + (1.0 - taken) * ABSENT)
    put(2, dot(place, v_ref[...]))
    put(3, dot(place, g_ref[...]))


def owner_kernel(recv_ref, cent_ref, back_ref, new_ref, turn_ref, causal_ref, rows_ref, grads_ref):
    source_count, block_rows, width = recv_ref.shape
    head_size = width // 4
    owned = block_rows // CAP
    slot_count = source_count * CAP
    group_rows = 16 * block_rows
    groups = source_count // 16
    part = 16 * CAP
    score_scale = 1.0 / math.sqrt(head_size)

    @pl.when(pl.program_id(0) == 0)
    def _():
        row_at = iota((group_rows, group_rows), 0)
        col_at = iota((group_rows, group_rows), 1)
        cluster_of = row_at // part
        source_of = (row_at % part) // CAP
        from_row = source_of * block_rows + cluster_of * CAP + row_at % CAP
        turn_ref[...] = jnp.where(from_row == col_at, 1.0, 0.0).astype(BF16)
        causal_ref[...] = jnp.where(
            iota((slot_count, slot_count), 1) <= iota((slot_count, slot_count), 0), 0.0, MASKED
        )

    turn = turn_ref[...]
    @pl.loop(0, groups)
    def _(group):
        arrived = recv_ref[pl.ds(group * 16, 16)].reshape(group_rows, width)
        turned = dot(turn, arrived).astype(BF16)
        at_row = pl.multiple_of(group * part, part)
        rows_ref[:, pl.ds(at_row, part), :] = turned.reshape(owned, part, width)

    first_lane = jnp.where(iota((8, head_size), 1) == 0, 1.0, 0.0).astype(BF16)
    @pl.loop(0, owned)
    def _(cluster):
        q = rows_ref[cluster, :, 0:head_size]
        k = rows_ref[cluster, :, head_size : 2 * head_size]
        v = rows_ref[cluster, :, 2 * head_size : 3 * head_size]
        g = rows_ref[cluster, :, 3 * head_size : 4 * head_size]
        marks = lax.dot_general(first_lane, k, CONTRACT_LAST, preferred_element_type=F32)
        present = marks < ABSENT / 2
        bias = jnp.where(present, 0.0, MASKED)[0:1]
        scores = lax.dot_general(q, k, CONTRACT_LAST, preferred_element_type=F32) * score_scale
        scores = scores + (causal_ref[...] + bias)
        weights = jnp.exp(scores - jnp.max(scores, axis=-1, keepdims=True))
        probs = weights / jnp.sum(weights, axis=-1, keepdims=True)
        probs_low = probs.astype(BF16)
        out = dot(probs_low, v).astype(BF16)
        grad_prob = lax.dot_general(g, v, CONTRACT_LAST, preferred_element_type=F32)
        delta = jnp.sum(g.astype(F32) * out.astype(F32), axis=-1, keepdims=True)
        grad_score = (probs * (grad_prob - delta) * score_scale).astype(BF16)
        grad_q = dot(grad_score, k)
        grad_k = lax.dot_general(grad_score, q, CONTRACT_FIRST, preferred_element_type=F32)
        grad_v = lax.dot_general(probs_low, g, CONTRACT_FIRST, preferred_element_type=F32)
        grads_ref[cluster, :, 0:head_size] = out
        grads_ref[cluster, :, head_size : 2 * head_size] = grad_q.astype(BF16)
        grads_ref[cluster, :, 2 * head_size : 3 * head_size] = grad_k.astype(BF16)
        grads_ref[cluster, :, 3 * head_size : 4 * head_size] = grad_v.astype(BF16)
        key_sums = dot(jnp.where(present, 1.0, 0.0).astype(BF16), k)[0:1]
        blend = DECAY_RATE * cent_ref[0, pl.ds(cluster, 1), :] + (1.0 - DECAY_RATE) * key_sums
        new_ref[0, pl.ds(cluster, 1), :] = blend / jnp.sqrt(
            jnp.mean(blend * blend, axis=-1, keepdims=True) + 1e-06
        )

    @pl.loop(0, groups)
    def _(group):
        at_row = pl.multiple_of(group * part, part)
        leaving = grads_ref[:, pl.ds(at_row, part), :].reshape(group_rows, width)
        turned = lax.dot_general(turn, leaving, CONTRACT_FIRST, preferred_element_type=F32)
        back_ref[pl.ds(group * 16, 16)] = turned.astype(BF16).reshape(16, block_rows, width)


def unpack_kernel(chunk, flat_ref, ret_ref, *refs):
    out_refs = refs[-4:]
    sources, block_rows, width = ret_ref.shape
    head_size = width // 4
    tok_rows, heads = flat_ref.shape
    slot_rows = sources * block_rows
    here = iota((tok_rows, heads), 1) == pl.program_id(0)
    flat_col = jnp.sum(jnp.where(here, flat_ref[...], 0), axis=1, keepdims=True)
    take = jnp.where(iota((tok_rows, slot_rows), 1) == flat_col, 1.0, 0.0).astype(BF16)
    rows = dot(take, ret_ref[...].reshape(slot_rows, width)).astype(BF16)
    for at, out_ref in enumerate(out_refs):
        out_ref[...] = rows[:, at * head_size : (at + 1) * head_size]


def find_rows(first_head, ids_ref, slot_ref, base_ref, over_ref, header_ref):
    heads, _, tok_rows = ids_ref.shape
    cluster_count = slot_ref.shape[1]
    owners, lanes = header_ref.shape
    earlier = jnp.where(
        iota((tok_rows, tok_rows), 0) < iota((tok_rows, tok_rows), 1), 1.0, 0.0
    ).astype(BF16)
    slots_low = jnp.broadcast_to(slot_ref[...].astype(F32), (8, cluster_count)).astype(BF16)
    members = [
        jnp.where(iota((cluster_count, tok_rows), 0) == ids_ref[head], 1.0, 0.0)
        for head in range(heads)
    ]
    member_low = jnp.concatenate(members, axis=0).astype(BF16)
    earlier_members = dot(member_low, earlier)
    owner_of, tag_of, here_of = [], [], []
    for head in range(heads):
        own = slice(head * cluster_count, (head + 1) * cluster_count)
        slot = dot(slots_low, member_low[own])[0:1].astype(jnp.int32)
        rank = jnp.sum(earlier_members[own] * members[head], axis=0, keepdims=True)
        owner = (slot // CAP + TURN_BY * (first_head + head)) % owners
        owner_of.append(owner)
        tag_of.append((head * CAP + slot % CAP) * CAP + rank.astype(jnp.int32))
        here_of.append(jnp.where(iota((owners, tok_rows), 0) == owner, 1.0, 0.0))
    before_all = dot(jnp.concatenate(here_of, axis=0).astype(BF16), earlier)
    filled = jnp.zeros((owners, 1), F32)
    header = jnp.zeros((owners, lanes), F32)
    for head in range(heads):
        here_f = here_of[head]
        before = before_all[head * owners : (head + 1) * owners]
        place = jnp.sum(before * here_f, axis=0, keepdims=True).astype(jnp.int32)
        late = jnp.sum((before + filled) * here_f, axis=0, keepdims=True)
        late = late.astype(jnp.int32) - SHARED
        filled = filled + jnp.maximum(jnp.sum(here_f, axis=1, keepdims=True) - SHARED, 0.0)
        fits = place < SHARED
        packs = (late < PACKED - SPARE) & (place >= SHARED)
        base_ref[head] = jnp.where(fits, owner_of[head] * SHARED + place, -1)
        over_ref[head] = jnp.where(packs, owner_of[head] * PACKED + late, -1)
        lane = jnp.where(fits, head * SHARED + place, jnp.where(packs, heads * SHARED + late, -1))
        named = (here_f * (tag_of[head] + 1).astype(F32)).astype(BF16)
        lane_at = jnp.where(iota((lanes, tok_rows), 0) == lane, 1.0, 0.0).astype(BF16)
        header = header + lax.dot_general(
            named, lane_at, CONTRACT_LAST, preferred_element_type=F32
        )
    peak = jnp.max(filled, axis=0, keepdims=True)
    header_ref[...] = jnp.where(iota((owners, lanes), 1) == PEAK_LANE, peak, header).astype(BF16)


def token_rows(columns_ref, step, at, head_size):
    lanes = slice(at * head_size, (at + 1) * head_size)
    parts = [columns_ref[step, which, :, lanes] for which in range(columns_ref.shape[1])]
    return jnp.concatenate(parts, axis=1)


def pack_rows_kernel(
    first_head,
    ids_ref,
    slot_ref,
    q_ref,
    k_ref,
    v_ref,
    g_ref,
    send_ref,
    places_ref,
    header_ref,
    columns_ref,
    arrived_ref,
):
    owners, send_rows, width = send_ref.shape
    tok_rows = q_ref.shape[0]
    head_size = width // 4

    steps = columns_ref.shape[0]
    heads = places_ref.shape[0] // 2
    base_ref = places_ref.at[pl.ds(0, heads)]
    over_ref = places_ref.at[pl.ds(heads, heads)]

    def column_copy(at_step, which):
        lanes = pl.ds((first_head + 2 * at_step) * head_size, 2 * head_size)
        return pltpu.make_async_copy(
            (q_ref, k_ref, v_ref, g_ref)[which].at[:, lanes],
            columns_ref.at[at_step, which],
            arrived_ref.at[at_step, which],
        )

    for at_step in range(steps):
        for which in range(4):
            column_copy(at_step, which).start()
    find_rows(first_head, ids_ref, slot_ref, base_ref, over_ref, header_ref)

    all_rows, all_places = [], []
    for step in range(steps):
        for which in range(4):
            column_copy(step, which).wait()
        rows = [token_rows(columns_ref, step, at, head_size) for at in range(2)]
        halves = []
        for at in range(2):
            place = iota((owners * SHARED, tok_rows), 0) == base_ref[step * 2 + at]
            placed = dot(jnp.where(place, 1.0, 0.0).astype(BF16), rows[at])
            halves.append(placed.reshape(owners, SHARED, width))
            over = iota((owners * PACKED, tok_rows), 0) == over_ref[step * 2 + at]
            all_places.append(jnp.where(over, 1.0, 0.0).astype(BF16))
        all_rows += rows
        shared = jnp.concatenate(halves, axis=1).astype(BF16)
        send_ref[:, step * 2 * SHARED : (step + 1) * 2 * SHARED, :] = shared

    total = dot(jnp.concatenate(all_places, axis=1), jnp.concatenate(all_rows, axis=0))
    last_row = iota((owners * PACKED, owners), 1) * PACKED + PACKED - 1
    to_last = jnp.where(iota((owners * PACKED, owners), 0) == last_row, 1.0, 0.0)
    tags = dot(to_last.astype(BF16), header_ref[...])
    total = jnp.concatenate([total[:, :head_size] + tags, total[:, head_size:]], axis=1)
    packed = total.astype(BF16).reshape(owners, PACKED, width)
    send_ref[:, send_rows - PACKED :, :] = packed


def own_rows_kernel(
    first_head,
    me_ref,
    shared_ref,
    over_ref,
    back_ref,
    peak_ref,
    turn_ref,
    causal_ref,
    rows_ref,
    grads_ref,
    sums_ref,
):
    sources, pair_rows, width = shared_ref.shape
    head_size = width // 4
    problems = rows_ref.shape[0]
    owned = problems // 2
    slot_count = sources * CAP
    bunch = 16
    groups = sources // bunch
    part = bunch * CAP
    shared_count = bunch * pair_rows
    packed_count = bunch * PACKED
    score_scale = 1.0 / math.sqrt(head_size)
    step = pl.program_id(0)
    steps = pl.num_programs(0)

    @pl.when(step == 0)
    def _():
        at = iota((slot_count, slot_count), 0)
        causal_ref[...] = jnp.where(iota((slot_count, slot_count), 1) <= at, 0.0, MASKED)

    header_of = jnp.where(
        iota((bunch, packed_count), 1) == iota((bunch, packed_count), 0) * PACKED + PACKED - 1,
        1.0,
        0.0,
    ).astype(BF16)

    def turns(header, first_lane, rows_each, used):
        count = bunch * rows_each
        lane = iota((head_size, count), 1) % rows_each
        match = (iota((head_size, count), 0) == lane + first_lane) & (lane < used)
        tags = dot(header, jnp.where(match, 1.0, 0.0).astype(BF16))
        source = iota((1, count), 1) // rows_each
        own = iota((bunch, count), 0) == source
        tag = jnp.sum(jnp.where(own, tags, 0.0), axis=0, keepdims=True).astype(jnp.int32) - 1
        mine = (tag >= 0) & (tag // (problems * CAP) == step)
        problem = (tag // CAP) % problems
        slot = jnp.where(mine, problem * part + source * CAP + tag % CAP, -1)
        hit = iota((problems * part, count), 0) == slot
        return jnp.where(hit, 1.0, 0.0).astype(BF16)

    ones = jnp.ones((shared_count + packed_count, head_size), BF16)
    peak_ref[...] = jnp.zeros(peak_ref.shape, F32)

    @pl.loop(0, groups)
    def _(group):
        from_sources = pl.ds(group * bunch, bunch)
        at_row = pl.multiple_of(group * part, part)
        packed = over_ref[from_sources].reshape(packed_count, width)
        shared = shared_ref[from_sources].reshape(shared_count, width)
        header = dot(header_of, packed[:, :head_size])
        peak_ref[...] = jnp.maximum(peak_ref[...], jnp.max(header, axis=0, keepdims=True))
        header = header.astype(BF16)
        turn = jnp.concatenate(
            [
                turns(header, step * pair_rows, pair_rows, pair_rows),
                turns(header, steps * pair_rows, PACKED, PACKED - SPARE),
            ],
            axis=1,
        )
        turn_ref[group] = turn
        turned = dot(turn, jnp.concatenate([shared, packed], axis=0))
        marked = turned[:, head_size : 2 * head_size] + (1.0 - dot(turn, ones)) * ABSENT
        turned = jnp.concatenate(
            [turned[:, :head_size], marked, turned[:, 2 * head_size :]], axis=1
        )
        rows_ref[:, pl.ds(at_row, part), :] = turned.astype(BF16).reshape(problems, part, width)

    first_lane = jnp.where(iota((8, head_size), 1) == 0, 1.0, 0.0).astype(BF16)

    def attend(problem):
        q = rows_ref[problem, :, 0:head_size]
        k = rows_ref[problem, :, head_size : 2 * head_size]
        v = rows_ref[problem, :, 2 * head_size : 3 * head_size]
        g = rows_ref[problem, :, 3 * head_size : 4 * head_size]
        marks = lax.dot_general(first_lane, k, CONTRACT_LAST, preferred_element_type=F32)
        present = marks < ABSENT / 2
        bias = jnp.where(present, 0.0, MASKED)[0:1]
        scores = lax.dot_general(q, k, CONTRACT_LAST, preferred_element_type=F32) * score_scale
        scores = scores + (causal_ref[...] + bias)
        weights = jnp.exp(scores - jnp.max(scores, axis=-1, keepdims=True))
        probs = weights / jnp.sum(weights, axis=-1, keepdims=True)
        probs_low = probs.astype(BF16)
        out = dot(probs_low, v).astype(BF16)
        grad_prob = lax.dot_general(g, v, CONTRACT_LAST, preferred_element_type=F32)
        delta = jnp.sum(g.astype(F32) * out.astype(F32), axis=-1, keepdims=True)
        grad_score = (probs * (grad_prob - delta) * score_scale).astype(BF16)
        grad_q = dot(grad_score, k)
        grad_k = lax.dot_general(grad_score, q, CONTRACT_FIRST, preferred_element_type=F32)
        grad_v = lax.dot_general(probs_low, g, CONTRACT_FIRST, preferred_element_type=F32)
        grads_ref[problem, :, 0:head_size] = out
        grads_ref[problem, :, head_size : 2 * head_size] = grad_q.astype(BF16)
        grads_ref[problem, :, 2 * head_size : 3 * head_size] = grad_k.astype(BF16)
        grads_ref[problem, :, 3 * head_size : 4 * head_size] = grad_v.astype(BF16)
        sums = dot(jnp.where(present, 1.0, 0.0).astype(BF16), k)[0:1]
        sums_ref[pl.ds(problem, 1), :] = sums

    @pl.loop(0, problems // 2)
    def _(pair):
        attend(pair * 2)
        attend(pair * 2 + 1)

    rest = slice(back_ref.shape[1] - PACKED, back_ref.shape[1])
    at_pair = pl.multiple_of(step * pair_rows, pair_rows)

    @pl.loop(0, groups)
    def _(group):
        from_sources = pl.ds(group * bunch, bunch)
        at_row = pl.multiple_of(group * part, part)
        leaving = grads_ref[:, pl.ds(at_row, part), :].reshape(problems * part, width)
        sent = lax.dot_general(
            turn_ref[group], leaving, CONTRACT_FIRST, preferred_element_type=F32
        ).astype(BF16)
        back_ref[from_sources, pl.ds(at_pair, pair_rows), :] = sent[:shared_count].reshape(
            bunch, pair_rows, width
        )
        packed = sent[shared_count:].reshape(bunch, PACKED, width)

        @pl.when(step == 0)
        def _():
            back_ref[from_sources, rest, :] = packed

        @pl.when(step > 0)
        def _():
            back_ref[from_sources, rest, :] += packed

    for at in range(2):
        sums = jnp.concatenate(
            [sums_ref[at * owned + slot : at * owned + slot + 1, :] for slot in range(owned)],
            axis=1,
        )
        high = sums.astype(BF16).astype(F32)
        low = sums - high
        turned_by = TURN_BY * (first_head + step * 2 + at)
        home = lax.rem(me_ref[0] + sources * TURN_BY - turned_by, sources)
        row = iota((PACKED, width), 0)
        tile = back_ref[home, rest, :].astype(F32)
        tile = jnp.where(row == PACKED - 2, high, jnp.where(row == PACKED - 1, low, tile))
        back_ref[home, rest, :] = tile.astype(BF16)


def unpack_rows_kernel(
    first_head, me_ref, places_ref, cent_ref, shared_ref, packed_ref, *refs
):
    new_ref = refs[-1]
    out_refs = refs[-5:-1]
    owners, _, width = shared_ref.shape
    head_size = width // 4
    owned = cent_ref.shape[1]
    tok_rows, both = places_ref.shape
    heads = both // 2
    step = pl.program_id(0)
    packed = packed_ref[...].reshape(owners * PACKED, width)
    arrived = shared_ref[...].astype(F32)
    for at in range(2):
        lane = iota((tok_rows, both), 1) - step * 2 - at
        base = jnp.sum(jnp.where(lane == 0, places_ref[...], 0), axis=1, keepdims=True)
        over = jnp.sum(jnp.where(lane == heads, places_ref[...], 0), axis=1, keepdims=True)
        take = iota((tok_rows, owners * SHARED), 1) == base
        take_over = iota((tok_rows, owners * PACKED), 1) == over
        mine = arrived[:, at * SHARED : (at + 1) * SHARED, :].reshape(owners * SHARED, width)
        rows = dot(jnp.where(take, 1.0, 0.0).astype(BF16), mine.astype(BF16))
        rows = rows + dot(jnp.where(take_over, 1.0, 0.0).astype(BF16), packed)
        rows = rows.astype(BF16)
        for which, out_ref in enumerate(out_refs):
            out_ref[:, at * head_size : (at + 1) * head_size] = rows[
                :, which * head_size : (which + 1) * head_size
            ]
        turned_by = TURN_BY * (first_head + step * 2 + at)
        tile = packed_ref[lax.rem(me_ref[0] + turned_by, owners)].astype(F32)
        spare = iota((PACKED, width), 0) >= PACKED - 2
        key_sums = jnp.sum(jnp.where(spare, tile, 0.0), axis=0, keepdims=True)
        for slot in range(owned):
            blend = DECAY_RATE * cent_ref[at, slot : slot + 1, :]
            blend += (1.0 - DECAY_RATE) * key_sums[:, slot * head_size : (slot + 1) * head_size]
            new_ref[at, slot : slot + 1, :] = blend / jnp.sqrt(
                jnp.mean(blend * blend, axis=-1, keepdims=True) + 1e-06
            )


def params(limit=VMEM_BYTES):
    return pltpu.CompilerParams(vmem_limit_bytes=limit)


def dense(queries, keys, values, out_grad, cluster_ids, cluster_slot, centroids):
    seq_count = lax.axis_size("seq")
    local_heads, tok_rows = cluster_ids.shape[:2]
    cluster_count = cluster_slot.shape[0]
    owned = cluster_count // seq_count
    head_size = centroids.shape[2]
    heads = local_heads
    block_rows = owned * CAP
    width = 4 * head_size
    slot_count = seq_count * CAP
    sent = jax.ShapeDtypeStruct((seq_count, heads * block_rows, width), BF16)
    sent_bytes = seq_count * heads * block_rows * width * 2
    ids_rows = cluster_ids.reshape(local_heads, 1, tok_rows)
    slot_row = cluster_slot.reshape(1, cluster_count)
    block = pl.BlockSpec((seq_count, block_rows, width), lambda h: (0, h, 0))

    def exchange(rows):
        return lax.all_to_all(rows, "seq", split_axis=0, concat_axis=0, tiled=True)

    def pack(chunk):
        column = pl.BlockSpec((tok_rows, head_size), lambda h: (0, chunk * heads + h))
        return pl.pallas_call(
            pack_kernel,
            grid=(heads,),
            in_specs=[
                pl.BlockSpec((1, 1, tok_rows), lambda h: (chunk * heads + h, 0, 0)),
                pl.BlockSpec((1, cluster_count), lambda h: (0, 0)),
                column,
                column,
                column,
                column,
            ],
            out_specs=[block, pl.BlockSpec((1, 1, tok_rows), lambda h: (h, 0, 0))],
            out_shape=[sent, jax.ShapeDtypeStruct((heads, 1, tok_rows), jnp.int32)],
            scratch_shapes=[pltpu.VMEM((tok_rows, tok_rows), BF16)],
            compiler_params=params(),
            cost_estimate=pl.CostEstimate(
                flops=heads * 2 * 1024 * 512 * 640, bytes_accessed=2 * sent_bytes, transcendentals=0
            ),
            name="pack",
        )(ids_rows, slot_row, queries, keys, values, out_grad)

    def own(chunk, received):
        return pl.pallas_call(
            owner_kernel,
            grid=(heads,),
            in_specs=[
                block,
                pl.BlockSpec((1, owned, head_size), lambda h: (chunk * heads + h, 0, 0)),
            ],
            out_specs=[block, pl.BlockSpec((1, owned, head_size), lambda h: (h, 0, 0))],
            out_shape=[sent, jax.ShapeDtypeStruct((heads, owned, head_size), F32)],
            scratch_shapes=[
                pltpu.VMEM((16 * block_rows, 16 * block_rows), BF16),
                pltpu.VMEM((slot_count, slot_count), F32),
                pltpu.VMEM((owned, slot_count, width), BF16),
                pltpu.VMEM((owned, slot_count, width), BF16),
            ],
            compiler_params=params(),
            cost_estimate=pl.CostEstimate(
                flops=heads * owned * 7 * 2 * slot_count * slot_count * head_size,
                bytes_accessed=2 * sent_bytes,
                transcendentals=heads * owned * slot_count * slot_count,
            ),
            name="own",
        )(received, centroids)

    def unpack(chunk, flat_cols, returned, previous):
        column = pl.BlockSpec((tok_rows, head_size), lambda h: (0, chunk * heads + h))
        whole = jax.ShapeDtypeStruct((tok_rows, local_heads * head_size), BF16)

        def kernel(*refs):
            unpack_kernel(chunk, *refs)

        return pl.pallas_call(
            kernel,
            grid=(heads,),
            in_specs=[pl.BlockSpec((tok_rows, heads), lambda h: (0, 0)), block]
            + [pl.BlockSpec(memory_space=pl.ANY)] * len(previous),
            out_specs=[column] * 4,
            out_shape=[whole] * 4,
            input_output_aliases={2 + i: i for i in range(len(previous))},
            compiler_params=params(),
            cost_estimate=pl.CostEstimate(
                flops=heads * 2 * 1024 * 512 * 512, bytes_accessed=2 * sent_bytes, transcendentals=0
            ),
            name="unpack",
        )(flat_cols, returned, *previous)

    packed = [pack(chunk) for chunk in range(1)]
    received = [exchange(rows) for rows, _ in packed]
    owned_now = [own(chunk, rows) for chunk, rows in enumerate(received)]
    returned = [exchange(rows) for rows, _ in owned_now]
    outs = ()
    for chunk in range(1):
        flat_cols = packed[chunk][1].reshape(heads, tok_rows).T
        outs = unpack(chunk, flat_cols, returned[chunk], tuple(outs))
    new_centroids = jnp.concatenate([new for _, new in owned_now], axis=0)
    return (*outs, new_centroids)


def body(queries, keys, values, out_grad, cluster_ids, cluster_slot, centroids):
    seq_count = lax.axis_size("seq")
    local_heads, tok_rows = cluster_ids.shape[:2]
    cluster_count = cluster_slot.shape[0]
    owned, head_size = centroids.shape[1:]
    heads = local_heads // CHUNKS
    width = 4 * head_size
    pair_rows = 2 * SHARED
    steps = heads // 2
    send_rows = steps * pair_rows + PACKED
    slot_count = seq_count * CAP
    problems = 2 * owned
    block_bytes = seq_count * pair_rows * width * 2
    sent_shape = jax.ShapeDtypeStruct((seq_count, send_rows, width), BF16)
    ids_rows = cluster_ids.reshape(local_heads, 1, tok_rows)
    slot_row = cluster_slot.reshape(1, cluster_count)
    me = lax.axis_index("seq").reshape(1)

    def cost(flops, exps=0):
        return pl.CostEstimate(
            flops=flops, bytes_accessed=2 * (steps + 1) * block_bytes, transcendentals=exps
        )

    shared_block = pl.BlockSpec((seq_count, pair_rows, width), lambda s: (0, s, 0))
    packed_block = pl.BlockSpec((seq_count, PACKED, width), lambda s: (0, steps, 0))
    whole_block = pl.BlockSpec((seq_count, send_rows, width), lambda s: (0, 0, 0))
    me_spec = pl.BlockSpec(memory_space=pltpu.SMEM)

    def pack(chunk):
        places_shape = jax.ShapeDtypeStruct((2 * heads, 1, tok_rows), jnp.int32)
        places_block = pl.BlockSpec((2 * heads, 1, tok_rows), lambda s: (0, 0, 0))
        return pl.pallas_call(
            functools.partial(pack_rows_kernel, chunk * heads),
            grid=(1,),
            in_specs=[
                pl.BlockSpec((heads, 1, tok_rows), lambda s: (chunk, 0, 0)),
                pl.BlockSpec((1, cluster_count), lambda s: (0, 0)),
            ]
            + [pl.BlockSpec(memory_space=pl.ANY)] * 4,
            out_specs=[whole_block, places_block],
            out_shape=[sent_shape, places_shape],
            scratch_shapes=[
                pltpu.VMEM((seq_count, head_size), BF16),
                pltpu.VMEM((steps, 4, tok_rows, 2 * head_size), BF16),
                pltpu.SemaphoreType.DMA((steps, 4)),
            ],
            compiler_params=params(),
            cost_estimate=cost(2 * heads * 1536 * tok_rows * width),
            name="pack_rows",
        )(ids_rows, slot_row, queries, keys, values, out_grad)

    def own(chunk, received):
        return pl.pallas_call(
            functools.partial(own_rows_kernel, chunk * heads),
            grid=(steps,),
            in_specs=[me_spec, shared_block, packed_block],
            out_specs=[whole_block, pl.BlockSpec((8, head_size), lambda s: (0, 0))],
            out_shape=[sent_shape, jax.ShapeDtypeStruct((8, head_size), F32)],
            scratch_shapes=[
                pltpu.VMEM(
                    (seq_count // 16, problems * 16 * CAP, 16 * (pair_rows + PACKED)), BF16
                ),
                pltpu.VMEM((slot_count, slot_count), F32),
                pltpu.VMEM((problems, slot_count, width), BF16),
                pltpu.VMEM((problems, slot_count, width), BF16),
                pltpu.VMEM((problems, head_size), F32),
            ],
            compiler_params=params(),
            cost_estimate=cost(
                steps * problems * 16 * 2 * slot_count * slot_count * head_size,
                steps * problems * slot_count * slot_count,
            ),
            name="own_rows",
        )(me, received, received)

    def unpack(chunk, places, returned, previous):
        column = pl.BlockSpec((tok_rows, 2 * head_size), lambda s: (0, chunk * steps + s))
        places_block = pl.BlockSpec((tok_rows, 2 * heads), lambda s: (0, 0))
        centroid_block = pl.BlockSpec(
            (2, owned, head_size), lambda s: (chunk * steps + s, 0, 0)
        )
        return pl.pallas_call(
            functools.partial(unpack_rows_kernel, chunk * heads),
            grid=(steps,),
            in_specs=[
                me_spec,
                places_block,
                centroid_block,
                shared_block,
                packed_block,
            ]
            + [pl.BlockSpec(memory_space=pl.ANY)] * len(previous),
            out_specs=[column] * 4 + [centroid_block],
            out_shape=[pltpu.HBM((tok_rows, local_heads * head_size), BF16)] * 4
            + [pltpu.HBM(centroids.shape, F32)],
            input_output_aliases={5 + at: at for at in range(len(previous))},
            compiler_params=params(LESS_VMEM_BYTES),
            cost_estimate=cost(2 * heads * 1536 * tok_rows * width),
            name="unpack_rows",
        )(
            me,
            places.reshape(2 * heads, tok_rows).T,
            centroids,
            returned,
            returned,
            *previous,
        )

    def exchange(rows):
        return lax.all_to_all(rows, "seq", split_axis=0, concat_axis=0, tiled=True)

    packed = [pack(chunk) for chunk in range(CHUNKS)]
    received = [exchange(rows) for rows, _ in packed]
    owned_now = [own(chunk, received[chunk]) for chunk in range(CHUNKS)]
    returned = [exchange(back) for back, _ in owned_now]
    outs = ()
    for chunk in range(CHUNKS):
        outs = unpack(chunk, packed[chunk][1], returned[chunk], tuple(outs))

    peak = functools.reduce(jnp.maximum, [seen[0:1] for _, seen in owned_now])
    swap = [(at, 1 - at) for at in range(2)]
    peak = jnp.maximum(peak, lax.ppermute(peak, "head", swap))[0, PEAK_LANE]

    def lacking(state):
        return state[0]

    def again(state):
        full = dense(queries, keys, values, out_grad, cluster_ids, cluster_slot, centroids)
        return (jnp.zeros((), jnp.bool_), *full)

    state = lax.while_loop(lacking, again, (peak > PACKED - SPARE, *outs))
    return state[1:]


def solution(mesh):
    return jax.shard_map(
        body,
        mesh=mesh,
        in_specs=(
            P("seq", "head"),
            P("seq", "head"),
            P("seq", "head"),
            P("seq", "head"),
            P("head", "seq", None),
            P(),
            P("head", "seq", None),
        ),
        out_specs=(
            P("seq", "head"),
            P("seq", "head"),
            P("seq", "head"),
            P("seq", "head"),
            P("head", "seq", None),
        ),
        check_vma=False,
    )
```
